128 devices in a mesh: dp: 8 (over x, core), expert: 16 (over z, y).
Axes of the slice: x: 4, y: 4, z: 4, core: 2. Of those that a mesh axis runs over, the one named last changes fastest.
Arguments:
- tokens: bfloat16 [32768, 1024], P(('dp', 'expert')), may hold values from -6 to 6
- routes: int32 [32768, 2], P(('dp', 'expert')), may hold values from 0 to 15, all different within a row
- cotangent: bfloat16 [32768, 1024], P(('dp', 'expert')), may hold values from -6 to 6
- attention_gain: float32 [1024], replicated, may hold values from 0.5 to 1.5
- query_weight: bfloat16 [1024, 1024], replicated, may hold values from -0.1875 to 0.1875
- key_weight: bfloat16 [1024, 1024], replicated, may hold values from -0.1875 to 0.1875
- value_weight: bfloat16 [1024, 1024], replicated, may hold values from -0.1875 to 0.1875
- output_weight: bfloat16 [1024, 1024], replicated, may hold values from -1.5 to 1.5
- bias_table: float32 [32, 16], replicated, may hold values from -3 to 3
- feedforward_gain: float32 [1024], replicated, may hold values from 0.5 to 1.5
- router_weight: float32 [1024, 16], replicated, may hold values from -0.125 to 0.125
- gate_weight: bfloat16 [16, 1024, 2816], P('expert'), may hold values from -0.1875 to 0.1875
- up_weight: bfloat16 [16, 1024, 2816], P('expert'), may hold values from -0.1875 to 0.1875
- down_weight: bfloat16 [16, 2816, 1024], P('expert'), may hold values from -0.109375 to 0.109375
Outputs:
- block_out: bfloat16 [32768, 1024], P(('dp', 'expert'))
- input_grad: float32 [32768, 1024], P(('dp', 'expert'))
- attention_gain_grad: float32 [1024], replicated
- query_grad: float32 [1024, 1024], replicated
- key_grad: float32 [1024, 1024], replicated
- value_grad: float32 [1024, 1024], replicated
- output_grad: float32 [1024, 1024], replicated
- bias_grad: float32 [32, 16], replicated
- feedforward_gain_grad: float32 [1024], replicated
- router_grad: float32 [1024, 16], replicated
- gate_grad: float32 [16, 1024, 2816], P('expert', None, 'dp')
- up_grad: float32 [16, 1024, 2816], P('expert', None, 'dp')
- down_grad: float32 [16, 2816, 1024], P('expert', 'dp')
The draws below stay inside these ranges and needn't reach their ends.
Inputs may be any that keep to these rules, and one draw needn't show every extreme that they name: `routes`: each row names two different experts.
All inputs are finite; a program needn't handle non-finite values.
Results may differ from the reference program's by a relative error of at most 0.019.
Values may be sent and summed in bfloat16 or wider, within the bound.
No kernel may reach another device: no remote copies, remote signals or barrier semaphores. Data moves between devices by JAX's collectives and lax.ppermute only.
A program may use at most 256 MiB of HBM per device.

```python
import math
import jax
import jax.numpy as jnp
import numpy as np
from jax import lax

D = 1024
FF = 2816
H = 16
HD = 64
BUCKETS = 32
TOK_DEV = 256
EXPERTS = 16
CAP = 40
TOKENS = 32768


def block_levels(key, dims, split, least, high):
    level, own = 1.0, jax.random.fold_in(key, 6)
    for dim, shards_of in split:
        draws = jnp.exp(jax.random.uniform(jax.random.fold_in(own, dim), (shards_of,), jnp.float32, least / len(split), high / len(split)))
        level = level * jnp.repeat(draws, dims[dim] // shards_of).reshape([-1 if axis == dim else 1 for axis in range(len(dims))])
    return level


def picks_of(rng, rows, number_of, top, lift):
    sequence = jax.random.permutation(jax.random.fold_in(rng, 1), number_of)
    boost = sequence
    for power in range(3):
        boost = boost * boost // number_of
    boost = boost * lift // number_of
    lots = jax.random.randint(jax.random.fold_in(rng, 2), (rows, number_of), 0, 4096) + boost
    sure = jax.random.permutation(jax.random.fold_in(rng, 3), rows)[jnp.arange(number_of) % rows]
    lots = jnp.where(jnp.arange(rows)[:, None] == sure[None, :], 1 << 14, lots)
    priority = lots * number_of + jnp.arange(number_of)
    return lax.top_k(priority.astype(jnp.int32), top)[1].astype(jnp.int32)


def normal_values(stream_key, shape, scale, most, split=(), held_as=jnp.bfloat16):
    values = scale * jax.random.normal(stream_key, shape, jnp.float32)
    if split:
        values = values * block_levels(stream_key, shape, split, -0.22, 0.18)
    return jnp.clip(values, -most, most).astype(held_as)


def setup_inputs(seed: int = 0) -> dict:
    arg_keys = jax.random.split(jax.random.key(seed), 15)
    return {
        "tokens": normal_values(arg_keys[0], (TOKENS, D), 1.0, 6.0, ((0, 128),)),
        "routes": picks_of(arg_keys[1], TOKENS, EXPERTS, 2, 1024),
        "cotangent": normal_values(arg_keys[2], (TOKENS, D), 1.0, 6.0, ((0, 128),)),
        "attention_gain": jnp.clip(1.0 + 0.1 * jax.random.normal(arg_keys[3], (D,), jnp.float32), 0.5, 1.5),
        "query_weight": normal_values(arg_keys[4], (D, H * HD), D ** -0.5, 0.1875),
        "key_weight": normal_values(arg_keys[5], (D, H * HD), D ** -0.5, 0.1875),
        "value_weight": normal_values(arg_keys[6], (D, H * HD), D ** -0.5, 0.1875),
        "output_weight": normal_values(arg_keys[7], (H * HD, D), (max(1, H * HD // 64)) ** -0.5, 1.5),
        "bias_table": normal_values(arg_keys[8], (BUCKETS, H), 1.0, 3.0, (), jnp.float32),
        "feedforward_gain": jnp.clip(1.0 + 0.1 * jax.random.normal(arg_keys[9], (D,), jnp.float32), 0.5, 1.5),
        "router_weight": normal_values(arg_keys[10], (D, EXPERTS), (2 * D) ** -0.5, 0.125, (), jnp.float32),
        "gate_weight": normal_values(arg_keys[11], (EXPERTS, D, FF), D ** -0.5, 0.1875, ((0, 16),)),
        "up_weight": normal_values(arg_keys[12], (EXPERTS, D, FF), D ** -0.5, 0.1875, ((0, 16),)),
        "down_weight": normal_values(arg_keys[13], (EXPERTS, FF, D), FF ** -0.5, 0.109375, ((0, 16),)),
    }


EPSILON = 1e-06
Z_COEF = 0.001
BALANCE_COEF = 0.01
PRECISE = lax.Precision.HIGHEST

@jax.custom_vjp
def low(v):
    return lax.optimization_barrier(v.astype(jnp.bfloat16)).astype(jnp.float32)

@jax.custom_vjp
def low_back(v):
    return v

def low_keep(v):
    return (low(v), None)

def low_pass(kept, grad):
    return (grad,)

def back_keep(v):
    return (v, None)

def back_low(kept, grad):
    return (low(grad),)
low.defvjp(low_keep, low_pass)
low_back.defvjp(back_keep, back_low)

def rounded_both(value):
    return low_back(low(value))

def bucket_table(length, bucket_count):
    half_count = bucket_count // 2
    exact_count = half_count // 2
    position = np.arange(length)
    relative = position[None, :] - position[:, None]
    distance = np.abs(relative)
    spread = np.log(np.maximum(distance, 1) / exact_count) / np.log(128.0 / exact_count) * (half_count - exact_count)
    far_bucket = np.minimum(exact_count + np.floor(np.maximum(spread, 0.0)).astype(np.int32), half_count - 1)
    bucket_index = np.where(distance < exact_count, distance, far_bucket)
    return (bucket_index + (relative > 0) * half_count).astype(np.int32)

def routing(routes, expert_count, capacity):
    length = routes.shape[0]
    columns = lax.broadcasted_iota(jnp.int32, (length, expert_count), 1)
    hot_first = (routes[:, 0:1] == columns).astype(jnp.int32)
    hot_second = (routes[:, 1:2] == columns).astype(jnp.int32)
    filled = lax.optimization_barrier(jnp.sum(hot_first, axis=0)).astype(jnp.int32)
    before_first = (jnp.cumsum(hot_first, axis=0) - hot_first).astype(jnp.int32)
    before_second = (jnp.cumsum(hot_second, axis=0) - hot_second + filled[None, :]).astype(jnp.int32)
    place_first = lax.optimization_barrier(jnp.sum(before_first * hot_first, axis=1)).astype(jnp.int32)
    place_second = lax.optimization_barrier(jnp.sum(before_second * hot_second, axis=1)).astype(jnp.int32)
    slot_first = jnp.where(place_first < capacity, routes[:, 0] * capacity + place_first, -1).astype(jnp.int32)
    slot_second = jnp.where(place_second < capacity, routes[:, 1] * capacity + place_second, -1).astype(jnp.int32)
    first_share = filled.astype(jnp.float32) / length
    return (slot_first, slot_second, first_share)

def gating(logits, routes):
    router_probs = jax.nn.softmax(logits, axis=-1)
    columns = lax.broadcasted_iota(jnp.int32, logits.shape, 1)
    first_pick = lax.optimization_barrier(jnp.sum(jnp.where(routes[:, 0:1] == columns, router_probs, 0.0), axis=1))
    second_pick = lax.optimization_barrier(jnp.sum(jnp.where(routes[:, 1:2] == columns, router_probs, 0.0), axis=1))
    pair_total = first_pick + second_pick
    return (router_probs, jnp.stack([first_pick / pair_total, second_pick / pair_total], axis=1))

def rms_norm(hidden, gain):
    return hidden * lax.rsqrt(lax.optimization_barrier(jnp.mean(hidden * hidden, axis=-1, keepdims=True)) + EPSILON) * gain

def group_layer(parameters, source, routes):
    attention_gain, query_weight, key_weight, value_weight, output_weight, bias_table, feedforward_gain, router_weight, gate_weight, up_weight, down_weight = parameters
    length, model_width = source.shape
    normed = low(rms_norm(source, attention_gain))
    query_act = rounded_both(jnp.dot(normed, query_weight, precision=PRECISE)).reshape(length, H, HD)
    key_act = rounded_both(jnp.dot(normed, key_weight, precision=PRECISE)).reshape(length, H, HD)
    value_act = rounded_both(jnp.dot(normed, value_weight, precision=PRECISE)).reshape(length, H, HD)
    buckets = jnp.asarray(bucket_table(length, BUCKETS))
    bias_full = jnp.transpose(bias_table[buckets], (2, 0, 1))
    scores = jnp.einsum('ihd,jhd->hij', query_act, key_act, precision=PRECISE) * (1.0 / math.sqrt(HD)) + bias_full
    scores = low_back(scores)
    attn_probs = jax.nn.softmax(scores, axis=-1)
    heads_out = rounded_both(jnp.einsum('hij,jhd->ihd', low(attn_probs), value_act, precision=PRECISE)).reshape(length, H * HD)
    middle = source + low_back(jnp.dot(heads_out, output_weight, precision=PRECISE))
    normed2 = rms_norm(middle, feedforward_gain)
    logits = jnp.dot(normed2, router_weight, precision=PRECISE)
    router_probs, gate_values = gating(logits, routes)
    slot_first, slot_second, first_share = routing(routes, EXPERTS, CAP)
    columns = lax.broadcasted_iota(jnp.int32, (length, EXPERTS * CAP), 1)
    hot_first = (slot_first[:, None] == columns).astype(jnp.float32)
    hot_second = (slot_second[:, None] == columns).astype(jnp.float32)
    dispatch = hot_first + hot_second
    sent_rows = low_back(jnp.dot(dispatch.T, low(normed2), precision=PRECISE)).reshape(EXPERTS, CAP, model_width)
    gate_act = low_back(jnp.einsum('ecd,edf->ecf', sent_rows, gate_weight, precision=PRECISE))
    up_act = low_back(jnp.einsum('ecd,edf->ecf', sent_rows, up_weight, precision=PRECISE))
    hidden = low(jax.nn.gelu(gate_act) * up_act)
    returned = rounded_both(jnp.einsum('ecf,efd->ecd', hidden, down_weight, precision=PRECISE)).reshape(EXPERTS * CAP, model_width)
    combine = gate_values[:, 0:1] * hot_first + gate_values[:, 1:2] * hot_second
    result = middle + jnp.dot(combine, returned, precision=PRECISE)
    router_lse = jax.nn.logsumexp(logits, axis=-1)
    auxiliary = Z_COEF * jnp.sum(router_lse * router_lse) + BALANCE_COEF * EXPERTS * jnp.sum(first_share * lax.optimization_barrier(jnp.sum(router_probs, axis=0)))
    return (result, auxiliary)

def reference(tokens, routes, cotangent, attention_gain, query_weight, key_weight, value_weight, output_weight, bias_table, feedforward_gain, router_weight, gate_weight, up_weight, down_weight):
    parameters = tuple((array.astype(jnp.float32) for array in (attention_gain, query_weight, key_weight, value_weight, output_weight, bias_table, feedforward_gain, router_weight, gate_weight, up_weight, down_weight)))
    source = tokens.astype(jnp.float32)
    groups = tokens.shape[0] // TOK_DEV
    grouped_routes = routes.reshape(groups, TOK_DEV, 2)
    checked = jax.checkpoint(group_layer)

    def forward(weights, inputs):
        results, auxes = lax.map(lambda paired: checked(weights, paired[0], paired[1]), (inputs.reshape(groups, TOK_DEV, -1), grouped_routes))
        return (results.reshape(inputs.shape), jnp.sum(auxes))
    (result, auxiliary), pull = jax.vjp(forward, parameters, source)
    weight_grads, input_grad = pull((cotangent.astype(jnp.float32), jnp.ones((), jnp.float32)))
    return (result.astype(jnp.bfloat16), input_grad, weight_grads[0], weight_grads[1], weight_grads[2], weight_grads[3], weight_grads[4], weight_grads[5], weight_grads[6], weight_grads[7], weight_grads[8], weight_grads[9], weight_grads[10])
```

```python
import math

import jax
import jax.numpy as jnp
import numpy as np
from jax import lax
from jax.experimental import pallas as pl
from jax.experimental.pallas import tpu as pltpu
from jax.sharding import PartitionSpec as P

EPSILON = 1e-06
Z_COEF = 0.001
BALANCE_COEF = 0.01
PRECISE = lax.Precision.HIGHEST
LANES = 128
MIB = 1024 * 1024
VMEM = pl.BlockSpec(memory_space=pltpu.VMEM)
HBM = pl.BlockSpec(memory_space=pl.ANY)
SMEM = pl.BlockSpec(memory_space=pltpu.SMEM)


def bucket_table(length, bucket_count):
    half_count = bucket_count // 2
    exact_count = half_count // 2
    position = np.arange(length)
    relative = position[None, :] - position[:, None]
    distance = np.abs(relative)
    spread = (
        np.log(np.maximum(distance, 1) / exact_count)
        / np.log(128.0 / exact_count)
        * (half_count - exact_count)
    )
    far_bucket = np.minimum(
        exact_count + np.floor(np.maximum(spread, 0.0)).astype(np.int32), half_count - 1
    )
    bucket_index = np.where(distance < exact_count, distance, far_bucket)
    return (bucket_index + (relative > 0) * half_count).astype(np.int32)


def bucket_lines(length, bucket_count):
    table = bucket_table(length, bucket_count)
    line = np.concatenate([table[::-1, 0], table[0, 1:]])
    hot = np.zeros((2, bucket_count, 2 * length), np.float32)
    for place, bucket in enumerate(line):
        hot[0, bucket, place] = 1.0
        hot[1, bucket, 2 * length - 2 - place] = 1.0
    return hot


def dot(left, right, dims=((1,), (0,)), precision=None):
    return lax.dot_general(
        left, right, (dims, ((), ())), precision=precision, preferred_element_type=jnp.float32
    )


ROWS = ((0,), (0,))
COLS = ((1,), (1,))


def iota(shape, axis):
    return lax.broadcasted_iota(jnp.int32, shape, axis)


def ones_where(condition, dtype=jnp.bfloat16):
    return jnp.where(condition, 1.0, 0.0).astype(dtype)


def call(body, outs, scratch=(), vmem=60, **options):
    return pl.pallas_call(
        body,
        out_shape=outs,
        scratch_shapes=list(scratch),
        compiler_params=pltpu.CompilerParams(vmem_limit_bytes=vmem * MIB),
        cost_estimate=pl.CostEstimate(flops=1024, bytes_accessed=1024, transcendentals=0),
        **options,
    )


def shape(dims, dtype=jnp.bfloat16):
    return jax.ShapeDtypeStruct(dims, dtype)


def route_body(capacity, experts, routes_t, cotangent, slots_t, columns, cot_slots):
    length = cotangent.shape[0]
    before = ones_where(iota((length, length), 0) < iota((length, length), 1))
    picked = routes_t[...]
    expert = iota((experts, length), 0)
    hot1 = ones_where(expert == picked[0:1], jnp.float32)
    hot2 = ones_where(expert == picked[1:2], jnp.float32)
    filled = jnp.sum(hot1, axis=1, keepdims=True)
    number1 = dot(hot1.astype(jnp.bfloat16), before)
    number2 = dot(hot2.astype(jnp.bfloat16), before) + filled
    place1 = jnp.sum(number1 * hot1, axis=0, keepdims=True).astype(jnp.int32)
    place2 = jnp.sum(number2 * hot2, axis=0, keepdims=True).astype(jnp.int32)
    slot1 = jnp.where(place1 < capacity, picked[0:1] * capacity + place1, -1)
    slot2 = jnp.where(place2 < capacity, picked[1:2] * capacity + place2, -1)
    slots_t[0:1] = slot1
    slots_t[1:2] = slot2
    lines = jnp.concatenate([slot1, slot2, picked, jnp.zeros((4, length), jnp.int32)], axis=0)
    columns[...] = lines.T
    slot = iota((experts * capacity, length), 0)
    dispatch = ones_where((slot == slot1) | (slot == slot2))
    cot_slots[...] = dot(dispatch, cotangent[...]).astype(jnp.bfloat16)


def route(routes, cotangent, experts, capacity):
    length, width = cotangent.shape
    return call(
        lambda *refs: route_body(capacity, experts, *refs),
        [
            shape((2, length), jnp.int32),
            shape((length, 8), jnp.int32),
            shape((experts * capacity, width)),
        ],
        in_specs=[VMEM] * 2,
        out_specs=[VMEM] * 3,
        name="route",
    )(routes.T, cotangent)


def rms(x):
    return lax.rsqrt(jnp.mean(x * x, axis=1, keepdims=True) + EPSILON)


def split3(x):
    high = x.astype(jnp.bfloat16)
    rest = x - high.astype(jnp.float32)
    mid = rest.astype(jnp.bfloat16)
    return high, mid, (rest - mid.astype(jnp.float32)).astype(jnp.bfloat16)


def lane_parts(column):
    lane = iota((column.shape[0], LANES), 1)
    spread = jnp.zeros(lane.shape, jnp.float32)
    for place, part in enumerate(split3(column)):
        spread = jnp.where(lane == place, part.astype(jnp.float32), spread)
    return spread.astype(jnp.bfloat16)


def sum_parts(lanes):
    parts = lanes.astype(jnp.float32)
    return parts[:, 0:1] + parts[:, 1:2] + parts[:, 2:3]


def attend_body(
    heads, tokens, attention_gain, feedforward_gain, table_t, line_hot, router_t, columns, slots_t,
    wq, wk, wv, wo,
    normed, query, key, value, heads_out, middle, logits, gates, sent,
    weights, lines, arrived,
):
    length, width = tokens.shape
    size = width // heads
    copies = [
        pltpu.make_async_copy(source, weights.at[place], arrived.at[place])
        for place, source in enumerate((wq, wk, wv, wo))
    ]
    for copy in copies:
        copy.start()
    lines[...] = dot(table_t[...], line_hot[0], precision=PRECISE)
    x = tokens[...].astype(jnp.float32)
    low = (x * rms(x) * attention_gain[...]).astype(jnp.bfloat16)
    normed[...] = low
    for place, out in enumerate((query, key, value)):
        copies[place].wait()
        out[...] = dot(low, weights[place]).astype(jnp.bfloat16)
    first = iota((length, 2 * size), 1) < size
    zero = jnp.zeros((length, 2 * size), jnp.bfloat16)
    scale = 1.0 / math.sqrt(size)
    for pair in range(heads // 2):
        span = slice(pair * 2 * size, (pair + 1) * 2 * size)
        q, k, v = query[:, span] * jnp.bfloat16(scale), key[:, span], value[:, span]
        outs = []
        for side in range(2):
            q_side = jnp.where(first, q, zero) if side == 0 else jnp.where(first, zero, q)
            head = 2 * pair + side
            line = jnp.broadcast_to(lines[head : head + 1, :], (length, 2 * length))
            bias = pltpu.roll(line, length + 1, 1, stride=1, stride_axis=0)[:, :length]
            scores = dot(q_side, k, COLS) + bias
            top = jnp.max(scores, axis=1, keepdims=True)
            grown = jnp.exp(scores - top)
            total = jnp.sum(grown, axis=1, keepdims=True)
            outs.append(dot((grown * (1.0 / total)).astype(jnp.bfloat16), v))
        heads_out[:, span] = jnp.where(first, outs[0], outs[1]).astype(jnp.bfloat16)
    copies[3].wait()
    mid = x + dot(heads_out[...], weights[3])
    middle[...] = mid
    normed2 = mid * rms(mid) * feedforward_gain[...]
    logit = dot(normed2, router_t[...], COLS, PRECISE)
    logits[...] = logit
    picked = columns[:, 2:4]
    expert = iota(logit.shape, 1)
    logit1 = jnp.sum(jnp.where(expert == picked[:, 0:1], logit, 0.0), axis=1, keepdims=True)
    logit2 = jnp.sum(jnp.where(expert == picked[:, 1:2], logit, 0.0), axis=1, keepdims=True)
    gate1 = 1.0 / (1.0 + jnp.exp(logit2 - logit1))
    gate2 = 1.0 / (1.0 + jnp.exp(logit1 - logit2))
    gates[:, 0:1] = gate1
    gates[:, 1:2] = gate2
    slot = iota((sent.shape[0], length), 0)
    hot1 = ones_where(slot == slots_t[0:1])
    hot2 = ones_where(slot == slots_t[1:2])
    sent[:, :width] = dot(hot1 + hot2, normed2.astype(jnp.bfloat16)).astype(jnp.bfloat16)
    sent[:, width:] = (dot(hot1, lane_parts(gate1)) + dot(hot2, lane_parts(gate2))).astype(jnp.bfloat16)


def attend(heads, slot_count, line_hot, tokens, attention_gain, feedforward_gain, table_t, router_t, columns, slots_t, weights):
    length, width = tokens.shape
    experts = router_t.shape[0]
    act = shape((length, width))
    return call(
        lambda *refs: attend_body(heads, *refs),
        [
            act, act, act, act, act,
            shape((length, width), jnp.float32),
            shape((length, experts), jnp.float32),
            shape((length, 2), jnp.float32),
            shape((slot_count, width + LANES)),
        ],
        scratch=[
            pltpu.VMEM((4, width, width), jnp.bfloat16),
            pltpu.VMEM((heads, 2 * length), jnp.float32),
            pltpu.SemaphoreType.DMA((4,)),
        ],
        in_specs=[VMEM] * 8 + [HBM] * 4,
        out_specs=[VMEM] * 9,
        name="attend",
    )(tokens, attention_gain, feedforward_gain, table_t, line_hot, router_t, columns, slots_t, *weights)

def gelu_parts(x):
    slope = math.sqrt(2.0 / math.pi)
    square = x * x
    t = jnp.tanh(slope * x * (1.0 + 0.044715 * square))
    half = 0.5 * (1.0 + t)
    return x * half, half + 0.5 * x * (1.0 - t * t) * slope * (1.0 + 3.0 * 0.044715 * square)


def chunks_of(total, most):
    return [(start, min(most, total - start)) for start in range(0, total, most)]


FF_CHUNK = 768


def hidden_grad_body(rows, down, out, weight, arrived):
    spans = chunks_of(weight.shape[0], FF_CHUNK)
    copies = [
        pltpu.make_async_copy(
            down.at[0, pl.ds(start, size), :], weight.at[pl.ds(start, size), :], arrived.at[place]
        )
        for place, (start, size) in enumerate(spans)
    ]
    for copy in copies:
        copy.start()
    x = rows[...]
    for copy, (start, size) in zip(copies, spans):
        copy.wait()
        out[:, start : start + size] = dot(x, weight[start : start + size, :], COLS).astype(jnp.bfloat16)


def hidden_grad(rows, down_weight):
    count, width = rows.shape
    hidden = down_weight.shape[1]
    return call(
        hidden_grad_body,
        shape((count, hidden)),
        scratch=[
            pltpu.VMEM((hidden, width), jnp.bfloat16),
            pltpu.SemaphoreType.DMA((len(chunks_of(hidden, FF_CHUNK)),)),
        ],
        in_specs=[VMEM, HBM],
        out_specs=VMEM,
        name="hidden_grad",
    )(rows, down_weight)


def expert_body(width, rows, back, gate_weight, up_weight, hidden, gate_low, up_low, out, gate, up, total, arrived):
    spans = chunks_of(gate.shape[1], FF_CHUNK)
    copies = []
    for place, (start, size) in enumerate(spans):
        span = pl.ds(start, size)
        for side, (source, target) in enumerate(((gate_weight, gate), (up_weight, up))):
            copies.append(
                pltpu.make_async_copy(source.at[0, :, span], target.at[:, span], arrived.at[2 * place + side])
            )
    for copy in copies:
        copy.start()
    x = rows[:, :width]
    choice = jnp.zeros((x.shape[0], 1), jnp.float32)
    for place, (start, size) in enumerate(spans):
        span = slice(start, start + size)
        copies[2 * place].wait()
        gate_act = dot(x, gate[:, span])
        copies[2 * place + 1].wait()
        up_act = dot(x, up[:, span])
        act, slope = gelu_parts(gate_act)
        low = (act * up_act).astype(jnp.bfloat16)
        hidden[:, span] = low
        grad = back[:, span].astype(jnp.float32)
        choice = choice + jnp.sum(low.astype(jnp.float32) * grad, axis=1, keepdims=True)
        gate_grad = (grad * up_act * slope).astype(jnp.bfloat16)
        up_grad = (grad * act).astype(jnp.bfloat16)
        gate_low[:, span] = gate_grad
        up_low[:, span] = up_grad
        part = dot(gate_grad, gate[:, span], COLS) + dot(up_grad, up[:, span], COLS)
        if place == 0:
            total[...] = part
        else:
            total[...] += part
    out[:, :width] = total[...].astype(jnp.bfloat16)
    out[:, width:] = lane_parts(choice)


def expert(rows, back, gate_weight, up_weight):
    count = rows.shape[0]
    width, hidden = gate_weight.shape[1:]
    act = shape((count, hidden))
    return call(
        lambda *refs: expert_body(width, *refs),
        [act, act, act, shape(rows.shape)],
        scratch=[
            pltpu.VMEM((width, hidden), jnp.bfloat16),
            pltpu.VMEM((width, hidden), jnp.bfloat16),
            pltpu.VMEM((count, width), jnp.float32),
            pltpu.SemaphoreType.DMA((2 * len(chunks_of(hidden, FF_CHUNK)),)),
        ],
        in_specs=[VMEM, VMEM, HBM, HBM],
        out_specs=[VMEM] * 4,
        name="expert",
    )(rows, back, gate_weight, up_weight)


def returned_body(hidden, down, out, weight, arrived):
    spans = chunks_of(weight.shape[1], 512)
    copies = [
        pltpu.make_async_copy(
            down.at[0, :, pl.ds(start, size)], weight.at[:, pl.ds(start, size)], arrived.at[place]
        )
        for place, (start, size) in enumerate(spans)
    ]
    for copy in copies:
        copy.start()
    x = hidden[...]
    for copy, (start, size) in zip(copies, spans):
        copy.wait()
        out[:, start : start + size] = dot(x, weight[:, start : start + size]).astype(jnp.bfloat16)


def expert_out(hidden, down_weight):
    count = hidden.shape[0]
    inner, width = down_weight.shape[1:]
    return call(
        returned_body,
        shape((count, width)),
        scratch=[
            pltpu.VMEM((inner, width), jnp.bfloat16),
            pltpu.SemaphoreType.DMA((len(chunks_of(width, 512)),)),
        ],
        in_specs=[VMEM, HBM],
        out_specs=VMEM,
        name="expert_out",
    )(hidden, down_weight)


def weight_grad_body(width, acts, rows, sent, out, held, turned, scaled, staged, arrived, left):
    hidden = acts.shape[1]
    spans = chunks_of(hidden, FF_CHUNK)
    copies = [
        pltpu.make_async_copy(acts.at[:, pl.ds(start, size)], held.at[:, pl.ds(start, size)], arrived.at[place])
        for place, (start, size) in enumerate(spans)
    ]
    for copy in copies:
        copy.start()
    scaled[...] = (rows[:, :width].astype(jnp.float32) * sum_parts(sent[:, width:])).astype(jnp.bfloat16)
    backs = []
    for place, (copy, (start, size)) in enumerate(zip(copies, spans)):
        span = slice(start, start + size)
        copy.wait()
        turned[span, :] = held[:, span].T
        staged[span, :] = dot(turned[span, :], scaled[...]).astype(jnp.bfloat16)
        target = pl.ds(start, size)
        backs.append(pltpu.make_async_copy(staged.at[target, :], out.at[target, :], left.at[place]))
        backs[-1].start()
    for back in backs:
        back.wait()


def weight_grad(acts, rows, sent, width):
    count, hidden = acts.shape
    chunks = len(chunks_of(hidden, FF_CHUNK))
    return call(
        lambda *refs: weight_grad_body(width, *refs),
        shape((hidden, width)),
        scratch=[
            pltpu.VMEM((count, hidden), jnp.bfloat16),
            pltpu.VMEM((hidden, count), jnp.bfloat16),
            pltpu.VMEM((count, width), jnp.bfloat16),
            pltpu.VMEM((hidden, width), jnp.bfloat16),
            pltpu.SemaphoreType.DMA((chunks,)),
            pltpu.SemaphoreType.DMA((chunks,)),
        ],
        in_specs=[HBM, VMEM, VMEM],
        out_specs=HBM,
        name="weight_grad",
    )(acts, rows, sent)


def combine_body(returned, columns, gates, middle, block_out):
    length = middle.shape[0]
    slot = iota((length, returned.shape[0]), 1)
    rows = returned[...]
    rows1 = dot(ones_where(slot == columns[:, 0:1]), rows)
    rows2 = dot(ones_where(slot == columns[:, 1:2]), rows)
    block_out[...] = (middle[...] + gates[:, 0:1] * rows1 + gates[:, 1:2] * rows2).astype(jnp.bfloat16)


def combine(returned, columns, gates, middle):
    length, width = middle.shape
    return call(
        combine_body,
        shape((length, width)),
        in_specs=[VMEM] * 4,
        out_specs=VMEM,
        name="combine",
    )(returned, columns, gates, middle)


def router_back(logit, choice, gate1, gate2, picked):
    experts = logit.shape[1]
    top = jnp.max(logit, axis=1, keepdims=True)
    grown = jnp.exp(logit - top)
    total = jnp.sum(grown, axis=1, keepdims=True)
    probs = grown / total
    lse = top + jnp.log(total)
    expert = iota(logit.shape, 1)
    hot1 = ones_where(expert == picked[:, 0:1], jnp.float32)
    hot = hot1 - ones_where(expert == picked[:, 1:2], jnp.float32)
    balance = (BALANCE_COEF * experts) * jnp.mean(hot1, axis=0, keepdims=True)
    even = jnp.sum(probs * balance, axis=1, keepdims=True)
    return hot * (choice * gate1 * gate2) + probs * (balance - even + 2.0 * Z_COEF * lse)


def diagonals(x):
    length = x.shape[0]
    x = jnp.concatenate([x, jnp.zeros_like(x)], axis=1)
    while x.shape[0] > 1:
        half = x.shape[0] // 2
        x = pltpu.roll(x[:half], half, 1) + x[half:]
    return x


def attend_back_body(
    heads, core, sent_grad, columns, gates, middle, feedforward_gain, cotangent, table_t, line_hot,
    logits, router_t, query, key, value, wo,
    middle_grad, send, mine, gain_grad, bias_lines, router_grad,
    weight, lines, heads_grad, arrived,
):
    length, width = middle.shape
    size = width // heads
    half = width // 2
    copy = pltpu.make_async_copy(wo, weight, arrived)
    copy.start()
    lines[...] = dot(table_t[...], line_hot[1], precision=PRECISE)
    slot = iota((length, sent_grad.shape[0]), 1)
    rows = sent_grad[...]
    rows1 = dot(ones_where(slot == columns[:, 0:1]), rows)
    rows2 = dot(ones_where(slot == columns[:, 1:2]), rows)
    gate1, gate2 = gates[:, 0:1], gates[:, 1:2]
    choice = sum_parts(rows1[:, width:] - rows2[:, width:])
    logit_grad = router_back(logits[...], choice, gate1, gate2, columns[:, 2:4])
    mid = middle[...]
    r = rms(mid)
    scaled = mid * r
    router_grad[...] = dot(logit_grad, scaled * feedforward_gain[...], ROWS, PRECISE)
    normed2_grad = (
        gate1 * rows1[:, :width] + gate2 * rows2[:, :width] + dot(logit_grad, router_t[...], precision=PRECISE)
    )
    u = normed2_grad * feedforward_gain[...]
    gain_grad[...] = jnp.sum(normed2_grad * scaled, axis=0, keepdims=True)
    grad = (
        cotangent[...].astype(jnp.float32)
        + r * u
        - mid * (r * r * r * jnp.mean(u * mid, axis=1, keepdims=True))
    )
    middle_grad[...] = grad
    low = grad.astype(jnp.bfloat16)
    copy.wait()
    heads_grad[...] = dot(low, weight[...], COLS).astype(jnp.bfloat16)
    away = 1 - core[0]

    @pl.when(away == 0)
    def _():
        send[:, 3 * half :] = low[:, :half]
        mine[:, 3 * half :] = low[:, half:]

    @pl.when(away == 1)
    def _():
        send[:, 3 * half :] = low[:, half:]
        mine[:, 3 * half :] = low[:, :half]

    pair_width = 2 * size
    first = iota((length, pair_width), 1) < size
    zero = jnp.zeros((length, pair_width), jnp.bfloat16)
    scale = jnp.bfloat16(1.0 / math.sqrt(size))
    pairs = heads // 4
    for turn, out in enumerate((send, mine)):
        side_of = away if turn == 0 else core[0]
        for step in range(pairs):
            pair = side_of * pairs + step
            span = pl.ds(pl.multiple_of(pair * pair_width, pair_width), pair_width)
            q, k, v, g = query[:, span] * scale, key[:, span], value[:, span], heads_grad[:, span]
            kept = []
            for side in range(2):
                q_side = jnp.where(first, q, zero) if side == 0 else jnp.where(first, zero, q)
                g_side = jnp.where(first, g, zero) if side == 0 else jnp.where(first, zero, g)
                head = 2 * pair + side
                line = jnp.broadcast_to(lines[pl.ds(head, 1), :], (length, 2 * length))
                bias = pltpu.roll(line, length + 1, 1, stride=1, stride_axis=0)[:, :length]
                scores = dot(k, q_side, COLS) + bias
                top = jnp.max(scores, axis=0, keepdims=True)
                grown = jnp.exp(scores - top)
                probs = grown * (1.0 / jnp.sum(grown, axis=0, keepdims=True))
                probs_grad = dot(v, g_side, COLS)
                score_grad = probs * (probs_grad - jnp.sum(probs * probs_grad, axis=0, keepdims=True))
                score_low = score_grad.astype(jnp.bfloat16)
                bias_lines[pl.ds(head, 1), :] = diagonals(score_low.astype(jnp.float32))
                kept.append(
                    (
                        dot(score_low, k * scale, ROWS),
                        dot(score_low, q),
                        dot(probs.astype(jnp.bfloat16), g),
                    )
                )
            for place in range(3):
                start = place * half + step * pair_width
                out[:, start : start + pair_width] = jnp.where(first, kept[0][place], kept[1][place]).astype(
                    jnp.bfloat16
                )


def attend_back(heads, core, line_hot, sent_grad, columns, gates, middle, feedforward_gain, cotangent, table_t, logits, router_t, query, key, value, wo):
    length, width = middle.shape
    return call(
        lambda *refs: attend_back_body(heads, *refs),
        [
            shape((length, width), jnp.float32),
            shape((length, 2 * width)),
            shape((length, 2 * width)),
            shape((1, width), jnp.float32),
            shape((heads, 2 * length), jnp.float32),
            shape(router_t.shape, jnp.float32),
        ],
        scratch=[
            pltpu.VMEM((width, width), jnp.bfloat16),
            pltpu.VMEM((heads, 2 * length), jnp.float32),
            pltpu.VMEM((length, width), jnp.bfloat16),
            pltpu.SemaphoreType.DMA,
        ],
        in_specs=[SMEM] + [VMEM] * 13 + [HBM],
        out_specs=[VMEM] * 6,
        name="attend_back",
    )(core, sent_grad, columns, gates, middle, feedforward_gain, cotangent, table_t, line_hot, logits, router_t, query, key, value, wo)


def input_back_body(core, send, mine, middle_grad, tokens, attention_gain, bias_lines, line_hot, wq, wk, wv, input_grad, gain_grad, bias_grad, weights, arrived):
    length, width = tokens.shape
    half = width // 2
    copies = [
        pltpu.make_async_copy(source, weights.at[place], arrived.at[place])
        for place, source in enumerate((wq, wk, wv))
    ]
    for copy in copies:
        copy.start()
    bias_grad[...] = dot(bias_lines[...], line_hot[1], COLS, PRECISE)
    x = tokens[...].astype(jnp.float32)
    s = rms(x)
    total = jnp.zeros((length, width), jnp.float32)
    near = pl.ds(pl.multiple_of(core[0] * half, half), half)
    far = pl.ds(pl.multiple_of((1 - core[0]) * half, half), half)
    for place in range(3):
        copies[place].wait()
        columns = slice(place * half, (place + 1) * half)
        total = total + dot(mine[:, columns], weights[place, :, near], COLS)
        total = total + dot(send[:, columns], weights[place, :, far], COLS)
    w = total * attention_gain[...]
    gain_grad[...] = jnp.sum(total * x * s, axis=0, keepdims=True)
    input_grad[...] = middle_grad[...] + s * w - x * (s * s * s * jnp.mean(w * x, axis=1, keepdims=True))


def input_back(core, line_hot, send, mine, middle_grad, tokens, attention_gain, bias_lines, wq, wk, wv):
    length, width = tokens.shape
    buckets = line_hot.shape[1]
    heads = bias_lines.shape[0]
    return call(
        input_back_body,
        [
            shape((length, width), jnp.float32),
            shape((1, width), jnp.float32),
            shape((heads, buckets), jnp.float32),
        ],
        scratch=[pltpu.VMEM((3, width, width), jnp.bfloat16), pltpu.SemaphoreType.DMA((3,))],
        in_specs=[SMEM] + [VMEM] * 7 + [HBM] * 3,
        out_specs=[VMEM] * 3,
        name="input_back",
    )(core, send, mine, middle_grad, tokens, attention_gain, bias_lines, line_hot, wq, wk, wv)


def resplit(lanes):
    half = LANES // 2
    total = lanes + pltpu.roll(lanes, half, 1)
    high = total.astype(jnp.bfloat16).astype(jnp.float32)
    return jnp.where(iota(lanes.shape, 1) < half, high, total - high)


def rotated(place, side, block, step):
    return pl.ds(pl.multiple_of(((place + step) % side) * block, block), block)


def products_body(side, where, normed, normed_far, heads_out, heads_far, mine, came, gain, feedforward_gain, router, bias_t, *rest):
    pieces, (payload, vectors, left) = rest[: 2 * side], rest[2 * side :]
    length, width = normed.shape
    half = width // 2
    for place in range(4):
        near, far = (normed, normed_far) if place < 3 else (heads_out, heads_far)
        span = slice(place * half, (place + 1) * half)
        payload[:, span] = (
            dot(near[...], mine[:, span], ROWS) + dot(far[...], came[:, span], ROWS)
        ).astype(jnp.bfloat16)
    experts = router.shape[0]
    heads, buckets = bias_t.shape
    vectors[...] = jnp.zeros_like(vectors)
    vectors[0:1, :] = gain[...]
    vectors[1:2, :] = feedforward_gain[...]
    vectors[8 : 8 + experts, :] = router[...]
    vectors[32 : 32 + heads, :buckets] = bias_t[...]
    payload[:, 4 * half :] = resplit(vectors[...].T).astype(jnp.bfloat16)
    block = half // side
    copies = []
    for axis in range(2):
        for step in range(side):
            start = axis * half + ((where[2 + axis] + step) % side) * block
            copies.append(
                pltpu.make_async_copy(
                    payload.at[pl.ds(pl.multiple_of(start, block), block), :],
                    pieces[axis * side + step],
                    left.at[axis * side + step],
                )
            )
    for copy in copies:
        copy.start()
    for copy in copies:
        copy.wait()


def products(where, side, normed, normed_far, heads_out, heads_far, mine, came, gain, feedforward_gain, router, bias_t):
    length, width = normed.shape
    wide = 2 * width + LANES
    return call(
        lambda *refs: products_body(side, *refs),
        [shape((width // 2 // side, wide))] * (2 * side),
        scratch=[
            pltpu.VMEM((width, wide), jnp.bfloat16),
            pltpu.VMEM((LANES, width), jnp.float32),
            pltpu.SemaphoreType.DMA((2 * side,)),
        ],
        in_specs=[SMEM] + [VMEM] * 10,
        out_specs=[HBM] * (2 * side),
        name="products",
    )(where, normed, normed_far, heads_out, heads_far, mine, came, gain, feedforward_gain, router, bias_t)


def total_of(refs):
    total = refs[0][...].astype(jnp.float32)
    for ref in refs[1:]:
        total = total + ref[...].astype(jnp.float32)
    wide = total.shape[1] - LANES
    return total[:, :wide].astype(jnp.bfloat16), resplit(total[:, wide:]).astype(jnp.bfloat16)


def fold_body(side, where, *refs):
    sums = refs[-1]
    for axis in range(2):
        main, lanes = total_of(refs[axis * side : (axis + 1) * side])
        wide = main.shape[1]
        sums[axis, :, :wide] = main
        sums[axis, :, wide:] = lanes
        block = main.shape[0] // side
        for step in range(side):
            refs[(2 + axis) * side + step][...] = sums[axis, rotated(where[3 - axis], side, block, step), :]


def fold(where, side, pieces):
    rows, wide = pieces[0].shape
    return call(
        lambda *refs: fold_body(side, *refs),
        [shape((rows // side, wide))] * (2 * side),
        scratch=[pltpu.VMEM((2, rows, wide), jnp.bfloat16)],
        in_specs=[SMEM] + [VMEM] * (2 * side),
        out_specs=[VMEM] * (2 * side),
        vmem=12,
        name="fold",
    )(where, *pieces)


def join_body(side, *refs):
    out = refs[-1]
    for axis in range(2):
        main, lanes = total_of(refs[axis * side : (axis + 1) * side])
        rows, wide = main.shape
        out[axis * rows : (axis + 1) * rows, :wide] = main
        out[axis * rows : (axis + 1) * rows, wide:] = lanes


def join(side, pieces):
    rows, wide = pieces[0].shape
    return call(
        lambda *refs: join_body(side, *refs),
        shape((2 * rows, wide)),
        in_specs=[VMEM] * (2 * side),
        out_specs=VMEM,
        vmem=12,
        name="join",
    )(*pieces)


def part_body(*refs):
    main, lanes = total_of(refs[:-2])
    rows, wide = refs[-1].shape
    for axis, out in enumerate(refs[-2:]):
        out[:, : wide - LANES] = main[axis * rows : (axis + 1) * rows]
        out[:, wide - LANES :] = lanes[axis * rows : (axis + 1) * rows]


def part(pieces):
    rows, wide = pieces[0].shape
    return call(
        part_body,
        [shape((rows // 2, wide))] * 2,
        in_specs=[VMEM] * len(pieces),
        out_specs=[VMEM] * 2,
        vmem=12,
        name="part",
    )(*pieces)


def put_body(side, where, *refs):
    outs = refs[2 * side :]
    block = refs[0].shape[0]
    for axis, out in enumerate(outs):
        for step in range(side):
            out[rotated(where[3 - axis], side, block, step), :] = refs[axis * side + step][...]


def put(where, side, pieces):
    rows, wide = pieces[0].shape
    return call(
        lambda *refs: put_body(side, *refs),
        [shape((side * rows, wide))] * 2,
        in_specs=[SMEM] + [VMEM] * (2 * side),
        out_specs=[VMEM] * 2,
        vmem=12,
        name="put",
    )(where, *pieces)


def finish_body(side, where, *refs):
    count = 2 * side
    near, far = refs[:count], refs[count : 2 * count]
    *outs, gain, feedforward_gain, router_t, bias_t = refs[2 * count : 2 * count + 8]
    held, staged, arrived, left = refs[2 * count + 8 :]
    rows = near[0].shape[0]
    half = staged.shape[3] // 2
    copies = []
    for place in range(count):
        for which, source in enumerate((near[place], far[place])):
            slot = 2 * place + which
            copies.append(pltpu.make_async_copy(source, held.at[slot], arrived.at[slot]))
            copies[-1].start()
    backs = []
    for place in range(count):
        axis, step = place // side, place % side
        start = axis * half + ((where[2 + axis] + step) % side) * rows
        start = pl.multiple_of(start, rows)
        for which in range(2):
            slot = 2 * place + which
            copies[slot].wait()
            core = where[0] if which == 0 else 1 - where[0]
            target = pl.ds(pl.multiple_of(core * half, half), half)
            for matrix in range(4):
                staged[place, matrix, :, target] = held[slot, :, matrix * half : (matrix + 1) * half].astype(
                    jnp.float32
                )
        lanes = held[2 * place, :, 4 * half :].astype(jnp.float32) + held[2 * place + 1, :, 4 * half :].astype(jnp.float32)
        turned = (lanes + pltpu.roll(lanes, LANES // 2, 1)).T
        line = pl.ds(start, rows)
        gain[:, line] = turned[0:1]
        feedforward_gain[:, line] = turned[1:2]
        router_t[:, line] = turned[8 : 8 + router_t.shape[0]]

        @pl.when(start == 0)
        def _():
            bias_t[...] = turned[32 : 32 + bias_t.shape[0], : bias_t.shape[1]]

        for matrix in range(4):
            backs.append(
                pltpu.make_async_copy(
                    staged.at[place, matrix], outs[matrix].at[line, :], left.at[4 * place + matrix]
                )
            )
            backs[-1].start()
    for back in backs:
        back.wait()


def finish(where, side, near, far, experts, buckets, heads):
    rows, wide = near[0].shape
    width = 2 * side * rows
    whole = shape((width, width), jnp.float32)
    count = 2 * side
    return call(
        lambda *refs: finish_body(side, *refs),
        [whole] * 4
        + [shape((1, width), jnp.float32)] * 2
        + [shape((experts, width), jnp.float32), shape((heads, buckets), jnp.float32)],
        scratch=[
            pltpu.VMEM((2 * count, rows, wide), jnp.bfloat16),
            pltpu.VMEM((count, 4, rows, width), jnp.float32),
            pltpu.SemaphoreType.DMA((2 * count,)),
            pltpu.SemaphoreType.DMA((4 * count,)),
        ],
        in_specs=[SMEM] + [HBM] * (2 * count),
        out_specs=[HBM] * 4 + [VMEM] * 4,
        name="finish",
    )(where, *near, *far)


def rotate_x(count, step):
    return [(x * 2 + c, ((x + step) % count) * 2 + c) for x in range(count) for c in range(2)]


def rotate_plane(side, axis, step):
    return [
        (z * side + y, ((z + step * axis) % side) * side + (y + step * (1 - axis)) % side)
        for z in range(side)
        for y in range(side)
    ]


def swap_cores(count):
    return [(x * 2 + c, x * 2 + 1 - c) for x in range(count) for c in range(2)]


def shards(
    tokens,
    routes,
    cotangent,
    attention_gain,
    query_weight,
    key_weight,
    value_weight,
    output_weight,
    bias_table,
    feedforward_gain,
    router_weight,
    gate_weight,
    up_weight,
    down_weight,
):
    length, width = tokens.shape
    buckets, heads = bias_table.shape
    experts = lax.axis_size("expert")
    chips = lax.axis_size("dp") // 2
    side = math.isqrt(experts)
    replica, expert_place = lax.axis_index("dp"), lax.axis_index("expert")
    where = jnp.stack([replica % 2, replica // 2, expert_place % side, expert_place // side])
    capacity = max(2, (10 * length + 4 * experts - 1) // (4 * experts))
    swap = swap_cores(chips)
    line_hot = jnp.asarray(bucket_lines(length, buckets))
    gain1, gain2 = attention_gain[None], feedforward_gain[None]

    def exchange(rows):
        return lax.all_to_all(
            rows.reshape(experts, capacity, -1), "expert", split_axis=0, concat_axis=0, tiled=True
        ).reshape(experts * capacity, -1)

    table_t, router_t = bias_table.T, router_weight.T
    slots_t, columns, cot_slots = route(routes, cotangent, experts, capacity)
    cot_rows = exchange(cot_slots)
    normed, query, key, value, heads_out, middle, logits, gates, sent = attend(
        heads, experts * capacity, line_hot, tokens, gain1, gain2, table_t, router_t, columns, slots_t,
        (query_weight, key_weight, value_weight, output_weight),
    )

    def swapped(array):
        return lax.ppermute(array, "dp", swap)

    rows = exchange(sent)
    normed_far, heads_far = swapped(normed), swapped(heads_out)
    back = hidden_grad(cot_rows, down_weight)
    rows, normed_far, heads_far = lax.optimization_barrier((rows, normed_far, heads_far))
    hidden, gate_low, up_low, rows_grad = expert(rows, back, gate_weight, up_weight)
    sent_grad = exchange(rows_grad)

    def scatter_dp(part):
        return lax.psum_scatter(part, "dp", scatter_dimension=0, tiled=True)

    down_part = weight_grad(hidden, cot_rows, rows, width)
    gate_part = weight_grad(gate_low, rows, rows, width)
    returned = expert_out(hidden, down_weight)
    sent_grad, returned, down_part, gate_part = lax.optimization_barrier((sent_grad, returned, down_part, gate_part))
    down_grad, gate_grad = scatter_dp(down_part), scatter_dp(gate_part)
    returned = exchange(returned)

    middle_grad, send, mine, gain2_part, bias_lines, router_part = attend_back(
        heads, where, line_hot, sent_grad, columns, gates, middle, gain2, cotangent, table_t, logits,
        router_t, query, key, value, output_weight,
    )
    came = swapped(send)
    input_grad, gain1_part, bias_part = input_back(
        where, line_hot, send, mine, middle_grad, tokens, gain1, bias_lines, query_weight, key_weight, value_weight
    )
    came, returned = lax.optimization_barrier((came, returned))
    pieces = products(
        where, side, normed, normed_far, heads_out, heads_far, mine, came, gain1_part, gain2_part, router_part, bias_part
    )

    def turn(axis, piece, step):
        return lax.ppermute(piece, "expert", rotate_plane(side, axis, step))

    def scatter_plane(pieces, flip):
        return [
            turn(axis ^ flip, pieces[axis * side + step], step) if step else pieces[axis * side]
            for axis in range(2)
            for step in range(side)
        ]

    def gather_plane(parts, flip):
        return [turn(axis ^ flip, parts[axis], -step) if step else parts[axis] for axis in range(2) for step in range(side)]

    pieces, up_low, returned = lax.optimization_barrier((pieces, up_low, returned))
    folded_in = scatter_plane(pieces, 0)
    up_part = weight_grad(up_low, rows, rows, width)
    block_out = combine(returned, columns, gates, middle)
    folded_in, up_part, block_out = lax.optimization_barrier((folded_in, up_part, block_out))
    up_grad = scatter_dp(up_part)
    joined_in = scatter_plane(fold(where, side, folded_in), 1)
    down_grad, gate_grad = down_grad.astype(jnp.float32), gate_grad.astype(jnp.float32)
    joined_in, down_grad, gate_grad = lax.optimization_barrier((joined_in, down_grad, gate_grad))
    shard = join(side, joined_in)
    parts = part([shard] + [lax.ppermute(shard, "dp", rotate_x(chips, step)) for step in range(1, chips)])
    parts = put(where, side, gather_plane(parts, 1))
    near = gather_plane(parts, 0)
    up_grad = up_grad.astype(jnp.float32)
    near, up_grad = lax.optimization_barrier((near, up_grad))
    far = [swapped(piece) for piece in near]
    query_grad, key_grad, value_grad, output_grad, gain1_grad, gain2_grad, router_grad_t, bias_grad_t = finish(
        where, side, near, far, experts, buckets, heads
    )
    return (
        block_out,
        input_grad,
        gain1_grad[0],
        query_grad,
        key_grad,
        value_grad,
        output_grad,
        bias_grad_t.T,
        gain2_grad[0],
        router_grad_t.T,
        gate_grad.T[None],
        up_grad.T[None],
        down_grad[None],
    )


def solution(mesh):
    return jax.shard_map(
        shards,
        mesh=mesh,
        in_specs=(
            P(("dp", "expert"), None),
            P(("dp", "expert"), None),
            P(("dp", "expert"), None),
            P(),
            P(),
            P(),
            P(),
            P(),
            P(),
            P(),
            P(),
            P("expert", None, None),
            P("expert", None, None),
            P("expert", None, None),
        ),
        out_specs=(
            P(("dp", "expert"), None),
            P(("dp", "expert"), None),
            P(),
            P(),
            P(),
            P(),
            P(),
            P(),
            P(),
            P(),
            P("expert", None, "dp"),
            P("expert", None, "dp"),
            P("expert", "dp", None),
        ),
        check_vma=False,
    )
```

```python
import math

import jax
import jax.numpy as jnp
import numpy as np
from jax import lax
from jax.experimental import pallas as pl
from jax.experimental.pallas import tpu as pltpu
from jax.sharding import PartitionSpec as P

EPSILON = 1e-06
Z_COEF = 0.001
BALANCE_COEF = 0.01
PRECISE = lax.Precision.HIGHEST
LANES = 128
BLOCK = 16
MIB = 1024 * 1024
VMEM = pl.BlockSpec(memory_space=pltpu.VMEM)
HBM = pl.BlockSpec(memory_space=pl.ANY)
SMEM = pl.BlockSpec(memory_space=pltpu.SMEM)


def bucket_table(length, bucket_count):
    half_count = bucket_count // 2
    exact_count = half_count // 2
    position = np.arange(length)
    relative = position[None, :] - position[:, None]
    distance = np.abs(relative)
    spread = (
        np.log(np.maximum(distance, 1) / exact_count)
        / np.log(128.0 / exact_count)
        * (half_count - exact_count)
    )
    far_bucket = np.minimum(
        exact_count + np.floor(np.maximum(spread, 0.0)).astype(np.int32), half_count - 1
    )
    bucket_index = np.where(distance < exact_count, distance, far_bucket)
    return (bucket_index + (relative > 0) * half_count).astype(np.int32)


def bucket_lines(length, bucket_count):
    table = bucket_table(length, bucket_count)
    line = np.concatenate([table[::-1, 0], table[0, 1:]])
    hot = np.zeros((2, bucket_count, 2 * length), np.float32)
    for place, bucket in enumerate(line):
        hot[0, bucket, place] = 1.0
        hot[1, bucket, 2 * length - 2 - place] = 1.0
    return hot


def dot(left, right, dims=((1,), (0,)), precision=None):
    return lax.dot_general(
        left, right, (dims, ((), ())), precision=precision, preferred_element_type=jnp.float32
    )


ROWS = ((0,), (0,))
COLS = ((1,), (1,))


def iota(shape, axis):
    return lax.broadcasted_iota(jnp.int32, shape, axis)


def ones_where(condition, dtype=jnp.bfloat16):
    return jnp.where(condition, 1.0, 0.0).astype(dtype)


def call(body, outs, scratch=(), vmem=63, **options):
    return pl.pallas_call(
        body,
        out_shape=outs,
        scratch_shapes=list(scratch),
        compiler_params=pltpu.CompilerParams(vmem_limit_bytes=vmem * MIB),
        cost_estimate=pl.CostEstimate(flops=1024, bytes_accessed=1024, transcendentals=0),
        **options,
    )


def shape(dims, dtype=jnp.bfloat16):
    return jax.ShapeDtypeStruct(dims, dtype)


def route_body(capacity, experts, routes_t, cotangent, slots_t, columns, cot_slots):
    length = cotangent.shape[0]
    before = ones_where(iota((length, length), 0) < iota((length, length), 1))
    picked = routes_t[...]
    expert = iota((experts, length), 0)
    hot1 = ones_where(expert == picked[0:1], jnp.float32)
    hot2 = ones_where(expert == picked[1:2], jnp.float32)
    filled = jnp.sum(hot1, axis=1, keepdims=True)
    number1 = dot(hot1.astype(jnp.bfloat16), before)
    number2 = dot(hot2.astype(jnp.bfloat16), before) + filled
    place1 = jnp.sum(number1 * hot1, axis=0, keepdims=True).astype(jnp.int32)
    place2 = jnp.sum(number2 * hot2, axis=0, keepdims=True).astype(jnp.int32)
    slot1 = jnp.where(place1 < capacity, picked[0:1] * capacity + place1, -1)
    slot2 = jnp.where(place2 < capacity, picked[1:2] * capacity + place2, -1)
    slots_t[0:1] = slot1
    slots_t[1:2] = slot2
    lines = jnp.concatenate([slot1, slot2, picked, jnp.zeros((4, length), jnp.int32)], axis=0)
    columns[...] = lines.T
    slot = iota((experts * capacity, length), 0)
    dispatch = ones_where((slot == slot1) | (slot == slot2))
    cot_slots[...] = dot(dispatch, cotangent[...]).astype(jnp.bfloat16)


def route(routes, cotangent, experts, capacity):
    length, width = cotangent.shape
    return call(
        lambda *refs: route_body(capacity, experts, *refs),
        [
            shape((2, length), jnp.int32),
            shape((length, 8), jnp.int32),
            shape((experts * capacity, width)),
        ],
        in_specs=[VMEM] * 2,
        out_specs=[VMEM] * 3,
        name="route",
    )(routes.T, cotangent)


def start_all(copies):
    for copy in copies:
        copy.start()
    return copies


def wait_all(copies):
    for copy in copies:
        copy.wait()


def split2(x):
    high = x.astype(jnp.bfloat16)
    return high, (x - high.astype(jnp.float32)).astype(jnp.bfloat16)


def rms(x):
    return lax.rsqrt(jnp.mean(x * x, axis=1, keepdims=True) + EPSILON)


def split3(x):
    high = x.astype(jnp.bfloat16)
    rest = x - high.astype(jnp.float32)
    mid = rest.astype(jnp.bfloat16)
    return high, mid, (rest - mid.astype(jnp.float32)).astype(jnp.bfloat16)


def lane_parts(column):
    lane = iota((column.shape[0], LANES), 1)
    spread = jnp.zeros(lane.shape, jnp.float32)
    for place, part in enumerate(split3(column)):
        spread = jnp.where(lane == place, part.astype(jnp.float32), spread)
    return spread.astype(jnp.bfloat16)


def sum_parts(lanes):
    parts = lanes.astype(jnp.float32)
    return parts[:, 0:1] + parts[:, 1:2] + parts[:, 2:3]


def attend_body(
    heads, where, tokens, attention_gain, feedforward_gain, table_t, line_hot, router_t, columns, slots_t,
    wq, wk, wv, wo,
    normed_out, query_out, key_out, value_out, heads_done, left_send, middle, logits, gates, sent,
    weights, lines, acts, arrived, left,
):
    length, width = tokens.shape
    size = width // heads
    copies = start_all(
        [
            pltpu.make_async_copy(source, weights.at[place], arrived.at[place])
            for place, source in enumerate((wq, wk, wv, wo))
        ]
    )
    backs = [
        pltpu.make_async_copy(acts.at[place], target, left.at[place])
        for place, target in enumerate((normed_out, query_out, key_out, value_out, heads_done))
    ]
    lines[...] = dot(table_t[...], line_hot[0], precision=PRECISE)
    x = tokens[...].astype(jnp.float32)
    low = (x * rms(x) * attention_gain[...]).astype(jnp.bfloat16)
    acts[0] = low
    backs[0].start()
    for place in range(3):
        copies[place].wait()
        acts[place + 1] = dot(acts[0], weights[place]).astype(jnp.bfloat16)
        backs[place + 1].start()
    first = iota((length, 2 * size), 1) < size
    zero = jnp.zeros((length, 2 * size), jnp.bfloat16)
    scale = 1.0 / math.sqrt(size)
    for pair in range(heads // 2):
        span = slice(pair * 2 * size, (pair + 1) * 2 * size)
        q, k, v = acts[1, :, span] * jnp.bfloat16(scale), acts[2, :, span], acts[3, :, span]
        outs = []
        for side in range(2):
            q_side = jnp.where(first, q, zero) if side == 0 else jnp.where(first, zero, q)
            head = 2 * pair + side
            line = jnp.broadcast_to(lines[head : head + 1, :], (length, 2 * length))
            bias = pltpu.roll(line, length + 1, 1, stride=1, stride_axis=0)[:, :length]
            scores = dot(q_side, k, COLS) + bias
            top = jnp.max(scores, axis=1, keepdims=True)
            grown = jnp.exp(scores - top)
            total = jnp.sum(grown, axis=1, keepdims=True)
            outs.append(dot((grown * (1.0 / total)).astype(jnp.bfloat16), v))
        acts[4, :, span] = jnp.where(first, outs[0], outs[1]).astype(jnp.bfloat16)
    backs[4].start()
    half = width // 2
    other = pl.ds(pl.multiple_of((1 - where[0]) * half, half), half)
    left_send[:, :half] = acts[0, :, other]
    left_send[:, half:] = acts[4, :, other]
    copies[3].wait()
    mid = x + dot(acts[4], weights[3])
    middle[...] = mid
    normed2 = mid * rms(mid) * feedforward_gain[...]
    high, rest = split2(normed2)
    experts = router_t.shape[0]
    router_high, router_rest = split2(router_t[...])
    logit = dot(high, router_high, COLS) + dot(high, router_rest, COLS) + dot(rest, router_high, COLS)
    logits[...] = logit
    picked = columns[:, 2:4]
    expert = iota(logit.shape, 1)
    logit1 = jnp.sum(jnp.where(expert == picked[:, 0:1], logit, 0.0), axis=1, keepdims=True)
    logit2 = jnp.sum(jnp.where(expert == picked[:, 1:2], logit, 0.0), axis=1, keepdims=True)
    gate1 = 1.0 / (1.0 + jnp.exp(logit2 - logit1))
    gate2 = 1.0 / (1.0 + jnp.exp(logit1 - logit2))
    gates[:, 0:1] = gate1
    gates[:, 1:2] = gate2
    slot = iota((sent.shape[0], length), 0)
    hot1 = ones_where(slot == slots_t[0:1])
    hot2 = ones_where(slot == slots_t[1:2])
    sent[:, :width] = dot(hot1 + hot2, high).astype(jnp.bfloat16)
    sent[:, width:] = (dot(hot1, lane_parts(gate1)) + dot(hot2, lane_parts(gate2))).astype(jnp.bfloat16)
    wait_all(backs)


def attend(heads, slot_count, where, line_hot, tokens, attention_gain, feedforward_gain, table_t, router_t, columns, slots_t, weights):
    length, width = tokens.shape
    experts = router_t.shape[0]
    act = shape((length, width))
    return call(
        lambda *refs: attend_body(heads, *refs),
        [
            act, act, act, act, act, act,
            shape((length, width), jnp.float32),
            shape((length, experts), jnp.float32),
            shape((length, 2), jnp.float32),
            shape((slot_count, width + LANES)),
        ],
        scratch=[
            pltpu.VMEM((4, width, width), jnp.bfloat16),
            pltpu.VMEM((heads, 2 * length), jnp.float32),
            pltpu.VMEM((5, length, width), jnp.bfloat16),
            pltpu.SemaphoreType.DMA((4,)),
            pltpu.SemaphoreType.DMA((5,)),
        ],
        in_specs=[SMEM] + [VMEM] * 8 + [HBM] * 4,
        out_specs=[HBM] * 5 + [VMEM] * 5,
        name="attend",
    )(where, tokens, attention_gain, feedforward_gain, table_t, line_hot, router_t, columns, slots_t, *weights)

def gelu_parts(x):
    slope = math.sqrt(2.0 / math.pi)
    cubic = 0.044715 * slope
    square = x * x
    half = 0.5 + 0.5 * jnp.tanh(x * (slope + cubic * square))
    act = x * half
    return act, half + (act - act * half) * (2.0 * slope + 6.0 * cubic * square)


def chunks_of(total, most):
    return [(start, min(most, total - start)) for start in range(0, total, most)]


FF_CHUNK = 768


def hidden_grad_body(rows, down, out, weight, arrived):
    spans = chunks_of(weight.shape[0], FF_CHUNK)
    copies = [
        pltpu.make_async_copy(
            down.at[0, pl.ds(start, size), :], weight.at[pl.ds(start, size), :], arrived.at[place]
        )
        for place, (start, size) in enumerate(spans)
    ]
    for copy in copies:
        copy.start()
    x = rows[...]
    for copy, (start, size) in zip(copies, spans):
        copy.wait()
        out[:, start : start + size] = dot(x, weight[start : start + size, :], COLS).astype(jnp.bfloat16)


def hidden_grad(rows, down_weight):
    count, width = rows.shape
    hidden = down_weight.shape[1]
    return call(
        hidden_grad_body,
        shape((count, hidden)),
        scratch=[
            pltpu.VMEM((hidden, width), jnp.bfloat16),
            pltpu.SemaphoreType.DMA((len(chunks_of(hidden, FF_CHUNK)),)),
        ],
        in_specs=[VMEM, HBM],
        out_specs=VMEM,
        name="hidden_grad",
    )(rows, down_weight)


EXPERT_CHUNK = 512


def expert_body(width, rows, back, gate_weight, up_weight, hidden, gate_low, up_low, out, gate, up, grads, kept, acts, total, arrived, left):
    spans = chunks_of(gate.shape[1], EXPERT_CHUNK)
    copies = []
    for place, (start, size) in enumerate(spans):
        span = pl.ds(start, size)
        for side, (source, target) in enumerate(
            ((gate_weight.at[0], gate), (up_weight.at[0], up), (back, grads))
        ):
            copies.append(
                pltpu.make_async_copy(source.at[:, span], target.at[:, span], arrived.at[3 * place + side])
            )
            copies[-1].start()
    count = len(spans)
    choice = jnp.zeros((rows.shape[0], 1), jnp.float32)
    backs = []
    for turn in range(count + 2):
        if turn < count:
            start, size = spans[turn]
            span = slice(start, start + size)
            for side in range(3):
                copies[3 * turn + side].wait()
            acts[turn % 2, 0, :, :size] = dot(rows[:, :width], gate[:, span])
            acts[turn % 2, 1, :, :size] = dot(rows[:, :width], up[:, span])
        if 0 < turn <= count:
            place = turn - 1
            start, size = spans[place]
            span = slice(start, start + size)
            act, slope = gelu_parts(acts[place % 2, 0, :, :size])
            up_act = acts[place % 2, 1, :, :size]
            grad = grads[:, span].astype(jnp.float32)
            value = act * up_act
            up_grad = grad * act
            kept[0, :, span] = value.astype(jnp.bfloat16)
            kept[1, :, span] = (grad * up_act * slope).astype(jnp.bfloat16)
            kept[2, :, span] = up_grad.astype(jnp.bfloat16)
            choice = choice + jnp.sum(up_grad * up_act, axis=1, keepdims=True)
        if turn > 1:
            place = turn - 2
            start, size = spans[place]
            span = slice(start, start + size)
            part = dot(kept[1, :, span], gate[:, span], COLS) + dot(kept[2, :, span], up[:, span], COLS)
            if place == 0:
                total[...] = part
            else:
                total[...] += part
            for which, target in enumerate((hidden, gate_low, up_low)):
                backs.append(
                    pltpu.make_async_copy(
                        kept.at[which, :, pl.ds(start, size)],
                        target.at[:, pl.ds(start, size)],
                        left.at[3 * place + which],
                    )
                )
                backs[-1].start()
    out[:, :width] = total[...].astype(jnp.bfloat16)
    out[:, width:] = lane_parts(choice)
    for copy in backs:
        copy.wait()


def expert(rows, back, gate_weight, up_weight):
    count = rows.shape[0]
    width, hidden = gate_weight.shape[1:]
    act = shape((count, hidden))
    chunks = len(chunks_of(hidden, EXPERT_CHUNK))
    return call(
        lambda *refs: expert_body(width, *refs),
        [act, act, act, shape(rows.shape)],
        scratch=[
            pltpu.VMEM((width, hidden), jnp.bfloat16),
            pltpu.VMEM((width, hidden), jnp.bfloat16),
            pltpu.VMEM((count, hidden), jnp.bfloat16),
            pltpu.VMEM((3, count, hidden), jnp.bfloat16),
            pltpu.VMEM((2, 2, count, EXPERT_CHUNK), jnp.float32),
            pltpu.VMEM((count, width), jnp.float32),
            pltpu.SemaphoreType.DMA((3 * chunks,)),
            pltpu.SemaphoreType.DMA((3 * chunks,)),
        ],
        in_specs=[VMEM] + [HBM] * 3,
        out_specs=[HBM, HBM, HBM, VMEM],
        name="expert",
    )(rows, back, gate_weight, up_weight)


def expert_out_body(hidden, down, out, acts, weight, total, arrived):
    spans = chunks_of(weight.shape[0], FF_CHUNK)
    copies = []
    for place, (start, size) in enumerate(spans):
        span = pl.ds(start, size)
        copies.append(pltpu.make_async_copy(hidden.at[:, span], acts.at[:, span], arrived.at[2 * place]))
        copies.append(pltpu.make_async_copy(down.at[0, span, :], weight.at[span, :], arrived.at[2 * place + 1]))
    start_all(copies)
    for place, (start, size) in enumerate(spans):
        wait_all(copies[2 * place : 2 * place + 2])
        part = dot(acts[:, start : start + size], weight[start : start + size, :])
        if place == 0:
            total[...] = part
        elif place < len(spans) - 1:
            total[...] += part
        else:
            out[...] = (total[...] + part).astype(jnp.bfloat16)


def expert_out(hidden, down_weight):
    count = hidden.shape[0]
    inner, width = down_weight.shape[1:]
    return call(
        expert_out_body,
        shape((count, width)),
        scratch=[
            pltpu.VMEM((count, inner), jnp.bfloat16),
            pltpu.VMEM((inner, width), jnp.bfloat16),
            pltpu.VMEM((count, width), jnp.float32),
            pltpu.SemaphoreType.DMA((2 * len(chunks_of(inner, FF_CHUNK)),)),
        ],
        in_specs=[HBM] * 2,
        out_specs=VMEM,
        name="expert_out",
    )(hidden, down_weight)


def expert_grads_body(count, width, *refs):
    sources, lefts, sent = refs[:count], refs[count : 2 * count], refs[2 * count]
    targets = refs[2 * count + 1 : 3 * count + 1]
    acts, turned, scaled, staged, arrived, left = refs[3 * count + 1 :]
    spans = chunks_of(sources[0].shape[1], FF_CHUNK)
    steps = [(which, start, size) for which in range(count) for start, size in spans]
    coming = start_all(
        [
            pltpu.make_async_copy(
                sources[which].at[:, pl.ds(start, size)], acts.at[which, :, pl.ds(start, size)], arrived.at[turn]
            )
            for turn, (which, start, size) in enumerate(steps)
        ]
    )
    gate = sum_parts(sent[:, width:])
    for which in range(count):
        scaled[which] = (lefts[which][:, :width].astype(jnp.float32) * gate).astype(jnp.bfloat16)
    backs = []
    for turn in range(len(steps) + 1):
        if turn < len(steps):
            which, start, size = steps[turn]
            coming[turn].wait()
            turned[turn % 2, :size, :] = acts[which, :, start : start + size].T
        if turn > 0:
            which, start, size = steps[turn - 1]
            slot = (turn - 1) % staged.shape[0]
            if turn - 1 >= staged.shape[0]:
                backs[turn - 1 - staged.shape[0]].wait()
            staged[slot, :size, :] = dot(turned[(turn - 1) % 2, :size, :], scaled[which]).astype(jnp.bfloat16)
            backs.append(
                pltpu.make_async_copy(
                    staged.at[slot, pl.ds(0, size), :], targets[which].at[pl.ds(start, size), :], left.at[turn - 1]
                )
            )
            backs[-1].start()
    wait_all(backs[-staged.shape[0] :])


def expert_grads(pairs, sent, width):
    count = len(pairs)
    slots, inner = pairs[0][0].shape
    chunks = len(chunks_of(inner, FF_CHUNK))
    return call(
        lambda *refs: expert_grads_body(count, width, *refs),
        [shape((inner, width))] * count,
        scratch=[
            pltpu.VMEM((count, slots, inner), jnp.bfloat16),
            pltpu.VMEM((2, FF_CHUNK, slots), jnp.bfloat16),
            pltpu.VMEM((count, slots, width), jnp.bfloat16),
            pltpu.VMEM((4, FF_CHUNK, width), jnp.bfloat16),
            pltpu.SemaphoreType.DMA((count * chunks,)),
            pltpu.SemaphoreType.DMA((count * chunks,)),
        ],
        in_specs=[HBM] * count + [VMEM] * (count + 1),
        out_specs=[HBM] * count,
        name="expert_grads",
    )(*[acts for acts, rows in pairs], *[rows for acts, rows in pairs], sent)


def combine_body(returned, columns, gates, middle, block_out):
    length = middle.shape[0]
    slot = iota((length, returned.shape[0]), 1)
    rows = returned[...]
    rows1 = dot(ones_where(slot == columns[:, 0:1]), rows)
    rows2 = dot(ones_where(slot == columns[:, 1:2]), rows)
    block_out[...] = (middle[...] + gates[:, 0:1] * rows1 + gates[:, 1:2] * rows2).astype(jnp.bfloat16)


def combine(returned, columns, gates, middle):
    length, width = middle.shape
    return call(
        combine_body,
        shape((length, width)),
        in_specs=[VMEM] * 4,
        out_specs=VMEM,
        name="combine",
    )(returned, columns, gates, middle)


def router_back(logit, choice, gate1, gate2, picked):
    experts = logit.shape[1]
    top = jnp.max(logit, axis=1, keepdims=True)
    grown = jnp.exp(logit - top)
    total = jnp.sum(grown, axis=1, keepdims=True)
    probs = grown / total
    lse = top + jnp.log(total)
    expert = iota(logit.shape, 1)
    hot1 = ones_where(expert == picked[:, 0:1], jnp.float32)
    hot = hot1 - ones_where(expert == picked[:, 1:2], jnp.float32)
    balance = (BALANCE_COEF * experts) * jnp.mean(hot1, axis=0, keepdims=True)
    even = jnp.sum(probs * balance, axis=1, keepdims=True)
    return hot * (choice * gate1 * gate2) + probs * (balance - even + 2.0 * Z_COEF * lse)


def diagonals(x):
    half = x.shape[0] // 2
    top, low = x[:half], x[half:]
    x = jnp.concatenate([low[:, :half], low[:, half:] + top[:, :half], top[:, half:], jnp.zeros_like(low[:, :half])], axis=1)
    while x.shape[0] > 1:
        half = x.shape[0] // 2
        x = pltpu.roll(x[:half], half, 1) + x[half:]
    return x


def attend_back_body(
    heads, sent_grad, columns, gates, middle, feedforward_gain, cotangent, table_t, line_hot,
    logits, router_t, query, key, value, wo,
    middle_grad, backs, gain_grad, bias_lines, router_grad,
    weight, acts, lines, heads_grad, grad_out, backs_out, arrived, left,
):
    length, width = middle.shape
    size = width // heads
    half = width // 2
    copies = start_all(
        [pltpu.make_async_copy(wo, weight, arrived.at[3])]
        + [
            pltpu.make_async_copy(source, acts.at[place], arrived.at[place])
            for place, source in enumerate((query, key, value))
        ]
    )
    lines[...] = dot(table_t[...], line_hot[1], precision=PRECISE)
    slot = iota((length, sent_grad.shape[0]), 1)
    rows = sent_grad[...]
    rows1 = dot(ones_where(slot == columns[:, 0:1]), rows)
    rows2 = dot(ones_where(slot == columns[:, 1:2]), rows)
    gate1, gate2 = gates[:, 0:1], gates[:, 1:2]
    choice = sum_parts(rows1[:, width:] - rows2[:, width:])
    logit_grad = router_back(logits[...], choice, gate1, gate2, columns[:, 2:4])
    mid = middle[...]
    r = rms(mid)
    scaled = mid * r
    high, rest = split2(scaled * feedforward_gain[...])
    grad_high, grad_rest = split2(logit_grad)
    router_high, router_rest = split2(router_t[...])
    router_grad[...] = dot(grad_high, high, ROWS) + dot(grad_rest, high, ROWS) + dot(grad_high, rest, ROWS)
    normed2_grad = (
        gate1 * rows1[:, :width]
        + gate2 * rows2[:, :width]
        + (dot(grad_high, router_high) + dot(grad_rest, router_high) + dot(grad_high, router_rest))
    )
    u = normed2_grad * feedforward_gain[...]
    gain_grad[...] = jnp.sum(normed2_grad * scaled, axis=0, keepdims=True)
    grad = (
        cotangent[...].astype(jnp.float32)
        + r * u
        - mid * (r * r * r * jnp.mean(u * mid, axis=1, keepdims=True))
    )
    grad_out[...] = grad
    grad_copy = pltpu.make_async_copy(grad_out, middle_grad, left.at[2])
    grad_copy.start()
    low = grad.astype(jnp.bfloat16)
    wait_all(copies)
    heads_grad[...] = dot(low, weight[...], COLS).astype(jnp.bfloat16)
    backs_out[:, 3 * width :] = low
    pair_width = 2 * size
    first = iota((length, pair_width), 1) < size
    first_t = iota((pair_width, length), 0) < size
    zero = jnp.zeros((length, pair_width), jnp.bfloat16)
    scale = jnp.bfloat16(1.0 / math.sqrt(size))
    for pair in range(heads // 2):
        start = pair * pair_width
        span = slice(start, start + pair_width)
        q, k, v, g = acts[0, :, span] * scale, acts[1, :, span], acts[2, :, span], heads_grad[:, span]
        k_turned = (k * scale).T
        kept = []
        for side in range(2):
            q_side = jnp.where(first, q, zero) if side == 0 else jnp.where(first, zero, q)
            g_side = jnp.where(first, g, zero) if side == 0 else jnp.where(first, zero, g)
            head = 2 * pair + side
            line = jnp.broadcast_to(lines[head : head + 1, :], (length, 2 * length))
            bias = pltpu.roll(line, length + 1, 1, stride=1, stride_axis=0)[:, :length]
            scores = dot(k, q_side, COLS) + bias
            top = jnp.max(scores, axis=0, keepdims=True)
            grown = jnp.exp(scores - top)
            probs = grown * (1.0 / jnp.sum(grown, axis=0, keepdims=True))
            probs_grad = dot(v, g_side, COLS)
            score_grad = probs * (probs_grad - jnp.sum(probs * probs_grad, axis=0, keepdims=True))
            score_low = score_grad.astype(jnp.bfloat16)
            bias_lines[head : head + 1, :] = diagonals(score_low.astype(jnp.float32))
            kept.append(
                (
                    dot(k_turned, score_low),
                    dot(score_low, q),
                    dot(probs.astype(jnp.bfloat16), g),
                )
            )
        results = (
            jnp.where(first_t, kept[0][0], kept[1][0]).astype(jnp.bfloat16).T,
            jnp.where(first, kept[0][1], kept[1][1]).astype(jnp.bfloat16),
            jnp.where(first, kept[0][2], kept[1][2]).astype(jnp.bfloat16),
        )
        for place, result in enumerate(results):
            backs_out[:, place * width + start : place * width + start + pair_width] = result
    leaving = pltpu.make_async_copy(backs_out, backs, left.at[0])
    leaving.start()
    leaving.wait()
    grad_copy.wait()


def attend_back(heads, line_hot, sent_grad, columns, gates, middle, feedforward_gain, cotangent, table_t, logits, router_t, query, key, value, wo):
    length, width = middle.shape
    return call(
        lambda *refs: attend_back_body(heads, *refs),
        [
            shape((length, width), jnp.float32),
            shape((length, 4 * width)),
            shape((1, width), jnp.float32),
            shape((heads, 2 * length), jnp.float32),
            shape(router_t.shape, jnp.float32),
        ],
        scratch=[
            pltpu.VMEM((width, width), jnp.bfloat16),
            pltpu.VMEM((3, length, width), jnp.bfloat16),
            pltpu.VMEM((heads, 2 * length), jnp.float32),
            pltpu.VMEM((length, width), jnp.bfloat16),
            pltpu.VMEM((length, width), jnp.float32),
            pltpu.VMEM((length, 4 * width), jnp.bfloat16),
            pltpu.SemaphoreType.DMA((4,)),
            pltpu.SemaphoreType.DMA((3,)),
        ],
        in_specs=[VMEM] * 10 + [HBM] * 4,
        out_specs=[HBM] * 2 + [VMEM] * 3,
        name="attend_back",
    )(sent_grad, columns, gates, middle, feedforward_gain, cotangent, table_t, line_hot, logits, router_t, query, key, value, wo)


def input_back_body(backs_in, grad_in, tokens, attention_gain, bias_lines, line_hot, wq, wk, wv, input_grad, vectors, weights, backs, middle_grad, arrived):
    length, width = tokens.shape
    copies = []
    for place, source in enumerate((wq, wk, wv)):
        span = pl.ds(place * width, width)
        copies.append(pltpu.make_async_copy(backs_in.at[:, span], backs.at[:, span], arrived.at[place]))
        copies.append(pltpu.make_async_copy(source, weights.at[place], arrived.at[3 + place]))
    copies.append(pltpu.make_async_copy(grad_in, middle_grad, arrived.at[6]))
    start_all(copies)
    bias = dot(bias_lines[...], line_hot[1], COLS, PRECISE)
    rows = bias.shape[0] // 4
    bias = jnp.concatenate([bias[rows * part : rows * (part + 1)] for part in range(4)], axis=1)
    x = tokens[...].astype(jnp.float32)
    s = rms(x)
    total = jnp.zeros((length, width), jnp.float32)
    for place in range(3):
        wait_all(copies[2 * place : 2 * place + 2])
        total = total + dot(backs[:, place * width : (place + 1) * width], weights[place], COLS)
    w = total * attention_gain[...]
    gain = jnp.sum(total * x * s, axis=0, keepdims=True)
    vectors[...] = jnp.zeros_like(vectors)
    for part in range(width // LANES):
        vectors[part : part + 1, :] = gain[:, part * LANES : (part + 1) * LANES]
    vectors[width // LANES : width // LANES + rows, :] = bias
    copies[6].wait()
    input_grad[...] = middle_grad[...] + s * w - x * (s * s * s * jnp.mean(w * x, axis=1, keepdims=True))


def input_back(line_hot, backs, middle_grad, tokens, attention_gain, bias_lines, wq, wk, wv):
    length, width = tokens.shape
    return call(
        input_back_body,
        [
            shape((length, width), jnp.float32),
            shape((BLOCK, LANES), jnp.float32),
        ],
        scratch=[
            pltpu.VMEM((3, width, width), jnp.bfloat16),
            pltpu.VMEM((length, 3 * width), jnp.bfloat16),
            pltpu.VMEM((length, width), jnp.float32),
            pltpu.SemaphoreType.DMA((7,)),
        ],
        in_specs=[HBM] * 2 + [VMEM] * 4 + [HBM] * 3,
        out_specs=[VMEM] * 2,
        name="input_back",
    )(backs, middle_grad, tokens, attention_gain, bias_lines, line_hot, wq, wk, wv)


EXTRA = 2 * LANES


def resplit(lanes):
    half = LANES // 2
    total = lanes + pltpu.roll(lanes, half, 1)
    high = total.astype(jnp.bfloat16).astype(jnp.float32)
    return jnp.where(iota(lanes.shape, 1) < half, high, total - high)


def rotated(place, side, block, step):
    return pl.ds(pl.multiple_of(((place + step) % side) * block, block), block)


def products_body(side, where, normed, heads_out, left_far, backs_in, far_in, feedforward_gain, router, *rest):
    pieces, (lefts, backs, payload, vectors, arrived, left) = rest[:side], rest[side:]
    length, width = normed.shape
    half = width // 2
    mine = pl.ds(pl.multiple_of(where[0] * half, half), half)
    copies = start_all(
        [
            pltpu.make_async_copy(normed.at[:, mine], lefts.at[0, :, pl.ds(0, half)], arrived.at[0]),
            pltpu.make_async_copy(heads_out.at[:, mine], lefts.at[0, :, pl.ds(half, half)], arrived.at[1]),
            pltpu.make_async_copy(left_far, lefts.at[1], arrived.at[2]),
        ]
        + [
            pltpu.make_async_copy(
                source.at[:, pl.ds(place * width, width)],
                backs.at[which, :, pl.ds(place * width, width)],
                arrived.at[3 + 2 * place + which],
            )
            for place in range(4)
            for which, source in enumerate((backs_in, far_in))
        ]
    )
    experts = router.shape[0]
    vectors[...] = jnp.zeros_like(vectors)
    vectors[0:1, :] = feedforward_gain[...]
    vectors[8 : 8 + experts, :] = router[...]
    for place in range(2):
        start = 4 * width + place * LANES
        payload[:, start : start + LANES] = resplit(vectors[:, place * half : (place + 1) * half].T).astype(jnp.bfloat16)
    position = where[2 + where[0]]
    leaving = []

    def leave(part, start, size):
        for step, piece in enumerate(pieces):
            leaving.append(
                pltpu.make_async_copy(
                    payload.at[rotated(position, side, half // side, step), pl.ds(start, size)],
                    piece.at[:, pl.ds(start, size)],
                    left.at[part * side + step],
                )
            )
            leaving[-1].start()

    leave(4, 4 * width, EXTRA)
    wait_all(copies[:3])
    for place in range(4):
        wait_all(copies[3 + 2 * place : 5 + 2 * place])
        span = slice(place * width, (place + 1) * width)
        start = 0 if place < 3 else half
        payload[:, span] = (
            dot(lefts[0, :, start : start + half], backs[0, :, span], ROWS)
            + dot(lefts[1, :, start : start + half], backs[1, :, span], ROWS)
        ).astype(jnp.bfloat16)
        leave(place, place * width, width)
    wait_all(leaving)


def products(where, side, normed, heads_out, left_far, backs, backs_far, feedforward_gain, router):
    length, width = normed.shape
    wide = 4 * width + EXTRA
    return call(
        lambda *refs: products_body(side, *refs),
        [shape((width // 2 // side, wide))] * side,
        scratch=[
            pltpu.VMEM((2, length, width), jnp.bfloat16),
            pltpu.VMEM((2, length, 4 * width), jnp.bfloat16),
            pltpu.VMEM((width // 2, wide), jnp.bfloat16),
            pltpu.VMEM((LANES, width), jnp.float32),
            pltpu.SemaphoreType.DMA((11,)),
            pltpu.SemaphoreType.DMA((5 * side,)),
        ],
        in_specs=[SMEM] + [HBM] * 5 + [VMEM] * 2,
        out_specs=[HBM] * side,
        name="products",
    )(where, normed, heads_out, left_far, backs, backs_far, feedforward_gain, router)


def total_into(out, refs, late):
    total = refs[0][...].astype(jnp.float32)
    for ref in refs[1:]:
        total = total + ref[...].astype(jnp.float32)
    wide = total.shape[1] - EXTRA - (LANES if late else 0)
    out[:, :wide] = total[:, :wide].astype(jnp.bfloat16)
    for start in range(wide, wide + EXTRA, LANES):
        out[:, start : start + LANES] = resplit(total[:, start : start + LANES]).astype(jnp.bfloat16)
    if late:
        out[:, wide + EXTRA :] = stack_parts(total[:BLOCK, wide + EXTRA :] + total[BLOCK:, wide + EXTRA :])


def stack_parts(block):
    return jnp.concatenate(split2(block), axis=0)


def fold_body(side, where, vectors, *refs):
    pieces, outs, total = refs[:side], refs[side : 2 * side], refs[-1]
    total_into(total, pieces, False)
    position = where[3 - where[0]]
    wide = total.shape[1]
    late = stack_parts(vectors[...])
    for step, out in enumerate(outs):
        out[:, :wide] = total[rotated(position, side, out.shape[0], step), :]
        out[:, wide:] = late


def fold(where, side, vectors, pieces):
    rows, wide = pieces[0].shape
    return call(
        lambda *refs: fold_body(side, *refs),
        [shape((rows // side, wide + LANES))] * side,
        scratch=[pltpu.VMEM((rows, wide), jnp.bfloat16)],
        in_specs=[SMEM] + [VMEM] * (side + 1),
        out_specs=[VMEM] * side,
        vmem=16,
        name="fold",
    )(where, vectors, *pieces)


def add_pieces(pieces):
    return call(
        lambda *refs: total_into(refs[-1], refs[:-1], True),
        shape(pieces[0].shape),
        in_specs=[VMEM] * len(pieces),
        out_specs=VMEM,
        vmem=12,
        name="add_pieces",
    )(*pieces)


def put_body(side, where, *refs):
    pieces, (whole, upper, lower) = refs[:side], refs[side:]
    position = where[3 - where[0]]
    rows = upper.shape[0]
    for step in range(side):
        whole[rotated(position, side, pieces[0].shape[0], step), :] = pieces[step][...]
    upper[...] = whole[:rows, :]
    lower[...] = whole[rows:, :]


def put(where, side, pieces):
    rows, wide = pieces[0].shape
    half = shape((side * rows // 2, wide))
    return call(
        lambda *refs: put_body(side, *refs),
        [shape((side * rows, wide)), half, half],
        in_specs=[SMEM] + [VMEM] * side,
        out_specs=[VMEM] * 3,
        vmem=24,
        name="put",
    )(where, *pieces)


def finish_body(side, steps, where, *refs):
    parts = sum(cut for step, cut in steps)
    pieces, refs = (refs[:parts], refs[parts : 2 * parts]), refs[2 * parts :]
    up_low, *outs, up_out, gain, feedforward_gain, router_t, bias_t, held, staged, up_held, up_staged, late, arrived, left = refs
    rows = staged.shape[2]
    width = staged.shape[3]
    half = width // 2
    copies = []
    for which in range(2):
        place = 0
        for block, (step, cut) in enumerate(steps):
            size = rows // cut
            copies.append(
                start_all(
                    [
                        pltpu.make_async_copy(
                            pieces[which][place + part],
                            held.at[which, block, pl.ds(part * size, size), :],
                            arrived.at[which * parts + place + part],
                        )
                        for part in range(cut)
                    ]
                )
            )
            place += cut
    up_copy = pltpu.make_async_copy(up_low, up_held, arrived.at[2 * parts])
    up_copy.start()
    for vector in (feedforward_gain, router_t, late):
        vector[...] = jnp.zeros_like(vector)
    backs = []
    for block, (step, cut) in enumerate(steps):
        for which in range(2):
            core = where[0] if which == 0 else 1 - where[0]
            slot = which * len(steps) + block
            wait_all(copies[slot])
            start = pl.multiple_of(((where[2 + core] + step) % side) * rows, rows)
            line = pl.ds(pl.multiple_of(core * half + start, rows), rows)
            for matrix in range(4):
                staged[slot, matrix] = held[which, block, :, matrix * width : (matrix + 1) * width].astype(jnp.float32)
                backs.append(
                    pltpu.make_async_copy(
                        staged.at[slot, matrix], outs[matrix].at[line, :], left.at[4 * slot + matrix]
                    )
                )
                backs[-1].start()
            for place in range(2):
                lanes = held[which, block, :, 4 * width + place * LANES : 4 * width + (place + 1) * LANES]
                lanes = lanes.astype(jnp.float32)
                turned = (lanes + pltpu.roll(lanes, LANES // 2, 1)).T
                line = pl.ds(pl.multiple_of(place * half + start, rows), rows)
                feedforward_gain[:, line] += turned[0:1]
                router_t[:, line] += turned[8 : 8 + router_t.shape[0]]
            block_rows = held[which, block, : 2 * BLOCK, 4 * width + EXTRA :].astype(jnp.float32)
            late[...] += block_rows[:BLOCK] + block_rows[BLOCK:]
    up_copy.wait()
    up_staged[...] = up_held[...].astype(jnp.float32)
    backs.append(pltpu.make_async_copy(up_staged, up_out, left.at[8 * len(steps)]))
    backs[-1].start()
    lines = width // LANES
    for part in range(lines):
        gain[:, part * LANES : (part + 1) * LANES] = late[part : part + 1, :]
    heads, buckets = bias_t.shape
    for part in range(4):
        bias_t[part * heads // 4 : (part + 1) * heads // 4, :] = late[
            lines : lines + heads // 4, part * buckets : (part + 1) * buckets
        ]
    wait_all(backs)


def finish(where, side, steps, near, far, up_low, experts, buckets, heads):
    wide = near[0].shape[1]
    width = (wide - EXTRA - LANES) // 4
    rows = width // 2 // side
    count, parts = len(steps), len(near)
    return call(
        lambda *refs: finish_body(side, steps, *refs),
        [shape((width, width), jnp.float32)] * 4
        + [
            shape(up_low.shape, jnp.float32),
            shape((1, width), jnp.float32),
            shape((1, width), jnp.float32),
            shape((experts, width), jnp.float32),
            shape((heads, buckets), jnp.float32),
        ],
        scratch=[
            pltpu.VMEM((2, count, rows, wide), jnp.bfloat16),
            pltpu.VMEM((2 * count, 4, rows, width), jnp.float32),
            pltpu.VMEM(up_low.shape, jnp.bfloat16),
            pltpu.VMEM(up_low.shape, jnp.float32),
            pltpu.VMEM((BLOCK, LANES), jnp.float32),
            pltpu.SemaphoreType.DMA((2 * parts + 1,)),
            pltpu.SemaphoreType.DMA((8 * count + 1,)),
        ],
        in_specs=[SMEM] + [HBM] * (2 * parts + 1),
        out_specs=[HBM] * 5 + [VMEM] * 4,
        name="finish",
    )(where, *near, *far, up_low)


def rotate_x(count, step):
    return [(x * 2 + c, ((x + step) % count) * 2 + c) for x in range(count) for c in range(2)]


def rotate_plane(chips, side, flip, step):
    pairs = []
    for x in range(chips):
        for core in range(2):
            for z in range(side):
                for y in range(side):
                    along_z = core ^ flip
                    to = ((z + step) % side, y) if along_z else (z, (y + step) % side)
                    base = (x * 2 + core) * side * side
                    pairs.append((base + z * side + y, base + to[0] * side + to[1]))
    return pairs


def swap_cores(count):
    return [(x * 2 + c, x * 2 + 1 - c) for x in range(count) for c in range(2)]


def shards(
    tokens,
    routes,
    cotangent,
    attention_gain,
    query_weight,
    key_weight,
    value_weight,
    output_weight,
    bias_table,
    feedforward_gain,
    router_weight,
    gate_weight,
    up_weight,
    down_weight,
):
    length, width = tokens.shape
    buckets, heads = bias_table.shape
    experts = lax.axis_size("expert")
    chips = lax.axis_size("dp") // 2
    side = math.isqrt(experts)
    replica, expert_place = lax.axis_index("dp"), lax.axis_index("expert")
    where = jnp.stack([replica % 2, replica // 2, expert_place % side, expert_place // side])
    capacity = max(2, (10 * length + 4 * experts - 1) // (4 * experts))
    swap = swap_cores(chips)
    line_hot = jnp.asarray(bucket_lines(length, buckets))
    gain1, gain2 = attention_gain[None], feedforward_gain[None]

    def exchange(rows):
        return lax.all_to_all(
            rows.reshape(experts, capacity, -1), "expert", split_axis=0, concat_axis=0, tiled=True
        ).reshape(experts * capacity, -1)

    table_t, router_t = bias_table.T, router_weight.T
    slots_t, columns, cot_slots = route(routes, cotangent, experts, capacity)
    cot_rows = exchange(cot_slots)
    normed, query, key, value, heads_out, left, middle, logits, gates, sent = attend(
        heads, experts * capacity, where, line_hot, tokens, gain1, gain2, table_t, router_t, columns, slots_t,
        (query_weight, key_weight, value_weight, output_weight),
    )

    def swapped(array):
        return lax.ppermute(array, "dp", swap)

    rows = exchange(sent)
    left_far = swapped(left)
    back = hidden_grad(cot_rows, down_weight)
    rows, left_far = lax.optimization_barrier((rows, left_far))
    hidden, gate_low, up_low, rows_grad = expert(rows, back, gate_weight, up_weight)
    sent_grad = exchange(rows_grad)

    def scatter_dp(part):
        return lax.psum_scatter(part, "dp", scatter_dimension=0, tiled=True)

    grads = expert_grads(((hidden, cot_rows), (gate_low, rows), (up_low, rows)), rows, width)
    sent_grad, grads = lax.optimization_barrier((sent_grad, grads))
    down_grad, gate_grad = scatter_dp(grads[0]), scatter_dp(grads[1])

    middle_grad, backs, gain2_part, bias_lines, router_part = attend_back(
        heads, line_hot, sent_grad, columns, gates, middle, gain2, cotangent, table_t, logits,
        router_t, query, key, value, output_weight,
    )
    backs_far = swapped(backs)
    pieces = products(where, side, normed, heads_out, left_far, backs, backs_far, gain2_part, router_part)

    def turn(piece, flip, step):
        return lax.ppermute(piece, ("dp", "expert"), rotate_plane(chips, side, flip, step))

    def scatter_plane(pieces, flip):
        return [pieces[0]] + [turn(pieces[step], flip, step) for step in range(1, side)]

    pieces, hidden, backs = lax.optimization_barrier((pieces, hidden, backs))
    folded_in = scatter_plane(pieces, 0)
    input_grad, vectors = input_back(
        line_hot, backs, middle_grad, tokens, gain1, bias_lines, query_weight, key_weight, value_weight
    )
    returned = expert_out(hidden, down_weight)
    down_grad = down_grad.astype(jnp.float32)
    folded_in, vectors, returned, down_grad = lax.optimization_barrier((folded_in, vectors, returned, down_grad))
    shard = add_pieces(scatter_plane(fold(where, side, vectors, folded_in), 1))
    shard, returned = lax.optimization_barrier((shard, returned))
    returned = exchange(returned)
    total = add_pieces([shard] + [lax.ppermute(shard, "dp", rotate_x(chips, step)) for step in range(1, chips)])
    total, up_part, returned = lax.optimization_barrier((total, grads[2], returned))
    up_low = scatter_dp(up_part)
    gathered = [total] + [turn(total, 1, -step) for step in range(1, side)]
    gate_grad = gate_grad.astype(jnp.float32)
    block_out = combine(returned, columns, gates, middle)
    gathered, gate_grad, block_out = lax.optimization_barrier((gathered, gate_grad, block_out))
    own, upper, lower = put(where, side, gathered)
    minus_upper, plus_lower = turn(upper, 0, 1), turn(lower, 0, -1)
    minus_lower, plus_upper = turn(lower, 0, 1), turn(upper, 0, -1)
    across = [turn(minus_upper, 0, 1), turn(plus_lower, 0, -1)]
    near = [own, plus_upper, plus_lower, minus_upper, minus_lower, *across]
    far = [swapped(piece) for piece in near]
    query_grad, key_grad, value_grad, output_grad, up_grad, gain1_grad, gain2_grad, router_grad_t, bias_grad_t = finish(
        where, side, ((0, 1), (1, 2), (3, 2), (2, 2)), near, far, up_low, experts, buckets, heads
    )
    return (
        block_out,
        input_grad,
        gain1_grad[0],
        query_grad,
        key_grad,
        value_grad,
        output_grad,
        bias_grad_t.T,
        gain2_grad[0],
        router_grad_t.T,
        gate_grad.T[None],
        up_grad.T[None],
        down_grad[None],
    )


def solution(mesh):
    return jax.shard_map(
        shards,
        mesh=mesh,
        in_specs=(
            P(("dp", "expert"), None),
            P(("dp", "expert"), None),
            P(("dp", "expert"), None),
            P(),
            P(),
            P(),
            P(),
            P(),
            P(),
            P(),
            P(),
            P("expert", None, None),
            P("expert", None, None),
            P("expert", None, None),
        ),
        out_specs=(
            P(("dp", "expert"), None),
            P(("dp", "expert"), None),
            P(),
            P(),
            P(),
            P(),
            P(),
            P(),
            P(),
            P(),
            P("expert", None, "dp"),
            P("expert", None, "dp"),
            P("expert", "dp", None),
        ),
        check_vma=False,
    )
```

```python
import math

import jax
import jax.numpy as jnp
import numpy as np
from jax import lax
from jax.experimental import pallas as pl
from jax.experimental.pallas import tpu as pltpu
from jax.sharding import PartitionSpec as P

EPSILON = 1e-06
Z_COEF = 0.001
BALANCE_COEF = 0.01
PRECISE = lax.Precision.HIGHEST
LANES = 128
BLOCK = 16
MIB = 1024 * 1024
VMEM = pl.BlockSpec(memory_space=pltpu.VMEM)
HBM = pl.BlockSpec(memory_space=pl.ANY)
SMEM = pl.BlockSpec(memory_space=pltpu.SMEM)


def bucket_table(length, bucket_count):
    half_count = bucket_count // 2
    exact_count = half_count // 2
    position = np.arange(length)
    relative = position[None, :] - position[:, None]
    distance = np.abs(relative)
    spread = (
        np.log(np.maximum(distance, 1) / exact_count)
        / np.log(128.0 / exact_count)
        * (half_count - exact_count)
    )
    far_bucket = np.minimum(
        exact_count + np.floor(np.maximum(spread, 0.0)).astype(np.int32), half_count - 1
    )
    bucket_index = np.where(distance < exact_count, distance, far_bucket)
    return (bucket_index + (relative > 0) * half_count).astype(np.int32)


def bucket_lines(length, bucket_count):
    table = bucket_table(length, bucket_count)
    line = np.concatenate([table[::-1, 0], table[0, 1:]])
    hot = np.zeros((2, bucket_count, 2 * length), np.float32)
    for place, bucket in enumerate(line):
        hot[0, bucket, place] = 1.0
        hot[1, bucket, 2 * length - 2 - place] = 1.0
    return hot


def dot(left, right, dims=((1,), (0,)), precision=None):
    return lax.dot_general(
        left, right, (dims, ((), ())), precision=precision, preferred_element_type=jnp.float32
    )


ROWS = ((0,), (0,))
COLS = ((1,), (1,))


def iota(shape, axis):
    return lax.broadcasted_iota(jnp.int32, shape, axis)


def ones_where(condition, dtype=jnp.bfloat16):
    return jnp.where(condition, 1.0, 0.0).astype(dtype)


def call(body, outs, scratch=(), vmem=63, flops=1024, **options):
    return pl.pallas_call(
        body,
        out_shape=outs,
        scratch_shapes=list(scratch),
        compiler_params=pltpu.CompilerParams(vmem_limit_bytes=vmem * MIB),
        cost_estimate=pl.CostEstimate(flops=flops, bytes_accessed=1024, transcendentals=0),
        **options,
    )


def shape(dims, dtype=jnp.bfloat16):
    return jax.ShapeDtypeStruct(dims, dtype)


def route_body(capacity, experts, routes_t, cotangent, slots_t, columns, cot_slots):
    length = cotangent.shape[0]
    before = ones_where(iota((length, length), 0) < iota((length, length), 1))
    picked = routes_t[...]
    expert = iota((experts, length), 0)
    hot1 = ones_where(expert == picked[0:1], jnp.float32)
    hot2 = ones_where(expert == picked[1:2], jnp.float32)
    filled = jnp.sum(hot1, axis=1, keepdims=True)
    number1 = dot(hot1.astype(jnp.bfloat16), before)
    number2 = dot(hot2.astype(jnp.bfloat16), before) + filled
    place1 = jnp.sum(number1 * hot1, axis=0, keepdims=True).astype(jnp.int32)
    place2 = jnp.sum(number2 * hot2, axis=0, keepdims=True).astype(jnp.int32)
    slot1 = jnp.where(place1 < capacity, picked[0:1] * capacity + place1, -1)
    slot2 = jnp.where(place2 < capacity, picked[1:2] * capacity + place2, -1)
    slots_t[0:1] = slot1
    slots_t[1:2] = slot2
    lines = jnp.concatenate([slot1, slot2, picked, jnp.zeros((4, length), jnp.int32)], axis=0)
    columns[...] = lines.T
    slot = iota((experts * capacity, length), 0)
    dispatch = ones_where((slot == slot1) | (slot == slot2))
    cot_slots[...] = dot(dispatch, cotangent[...]).astype(jnp.bfloat16)


def route(routes, cotangent, experts, capacity):
    length, width = cotangent.shape
    return call(
        lambda *refs: route_body(capacity, experts, *refs),
        [
            shape((2, length), jnp.int32),
            shape((length, 8), jnp.int32),
            shape((experts * capacity, width)),
        ],
        in_specs=[VMEM] * 2,
        out_specs=[VMEM] * 3,
        name="route",
    )(routes.T, cotangent)


def start_all(copies):
    for copy in copies:
        copy.start()
    return copies


def wait_all(copies):
    for copy in copies:
        copy.wait()


def split2(x):
    high = x.astype(jnp.bfloat16)
    return high, (x - high.astype(jnp.float32)).astype(jnp.bfloat16)


def rms(x):
    return lax.rsqrt(jnp.mean(x * x, axis=1, keepdims=True) + EPSILON)


def split3(x):
    high = x.astype(jnp.bfloat16)
    rest = x - high.astype(jnp.float32)
    mid = rest.astype(jnp.bfloat16)
    return high, mid, (rest - mid.astype(jnp.float32)).astype(jnp.bfloat16)


def lane_parts(column):
    lane = iota((column.shape[0], LANES), 1)
    spread = jnp.zeros(lane.shape, jnp.float32)
    for place, part in enumerate(split3(column)):
        spread = jnp.where(lane == place, part.astype(jnp.float32), spread)
    return spread.astype(jnp.bfloat16)


def sum_parts(lanes):
    parts = lanes.astype(jnp.float32)
    return parts[:, 0:1] + parts[:, 1:2] + parts[:, 2:3]


def attend_body(
    heads, where, tokens, attention_gain, feedforward_gain, table_t, line_hot, router_t, columns, slots_t,
    wq, wk, wv, wo,
    normed_out, query_out, key_out, value_out, heads_done, left_send, middle, logits, gates, sent,
    weights, lines, acts, arrived, left,
):
    length, width = tokens.shape
    size = width // heads
    copies = start_all(
        [
            pltpu.make_async_copy(source, weights.at[place], arrived.at[place])
            for place, source in enumerate((wq, wk, wv, wo))
        ]
    )
    backs = [
        pltpu.make_async_copy(acts.at[place], target, left.at[place])
        for place, target in enumerate((normed_out, query_out, key_out, value_out, heads_done))
    ]
    lines[...] = dot(table_t[...], line_hot[0], precision=PRECISE)
    wait_all(copies[:3])
    x = tokens[...].astype(jnp.float32)
    low = (x * rms(x) * attention_gain[...]).astype(jnp.bfloat16)
    acts[0] = low
    backs[0].start()
    for place in range(3):
        acts[place + 1] = dot(acts[0], weights[place]).astype(jnp.bfloat16)
        backs[place + 1].start()
    first = iota((length, 2 * size), 1) < size
    zero = jnp.zeros((length, 2 * size), jnp.bfloat16)
    scale = 1.0 / math.sqrt(size)
    for pair in range(heads // 2):
        span = slice(pair * 2 * size, (pair + 1) * 2 * size)
        q, k, v = acts[1, :, span] * jnp.bfloat16(scale), acts[2, :, span], acts[3, :, span]
        outs = []
        for side in range(2):
            q_side = jnp.where(first, q, zero) if side == 0 else jnp.where(first, zero, q)
            head = 2 * pair + side
            line = jnp.broadcast_to(lines[head : head + 1, :], (length, 2 * length))
            bias = pltpu.roll(line, length + 1, 1, stride=1, stride_axis=0)[:, :length]
            scores = dot(q_side, k, COLS) + bias
            top = jnp.max(scores, axis=1, keepdims=True)
            grown = jnp.exp(scores - top)
            total = jnp.sum(grown, axis=1, keepdims=True)
            outs.append(dot((grown * (1.0 / total)).astype(jnp.bfloat16), v))
        acts[4, :, span] = jnp.where(first, outs[0], outs[1]).astype(jnp.bfloat16)
    backs[4].start()
    half = width // 2
    other = pl.ds(pl.multiple_of((1 - where[0]) * half, half), half)
    left_send[:, :half] = acts[0, :, other]
    left_send[:, half:] = acts[4, :, other]
    copies[3].wait()
    mid = x + dot(acts[4], weights[3])
    middle[...] = mid
    normed2 = mid * rms(mid) * feedforward_gain[...]
    high, rest = split2(normed2)
    experts = router_t.shape[0]
    router_high, router_rest = split2(router_t[...])
    logit = dot(high, router_high, COLS) + dot(high, router_rest, COLS) + dot(rest, router_high, COLS)
    logits[...] = logit
    picked = columns[:, 2:4]
    expert = iota(logit.shape, 1)
    logit1 = jnp.sum(jnp.where(expert == picked[:, 0:1], logit, 0.0), axis=1, keepdims=True)
    logit2 = jnp.sum(jnp.where(expert == picked[:, 1:2], logit, 0.0), axis=1, keepdims=True)
    gate1 = 1.0 / (1.0 + jnp.exp(logit2 - logit1))
    gate2 = 1.0 / (1.0 + jnp.exp(logit1 - logit2))
    gates[:, 0:1] = gate1
    gates[:, 1:2] = gate2
    slot = iota((sent.shape[0], length), 0)
    hot1 = ones_where(slot == slots_t[0:1])
    hot2 = ones_where(slot == slots_t[1:2])
    sent[:, :width] = dot(hot1 + hot2, high).astype(jnp.bfloat16)
    sent[:, width:] = (dot(hot1, lane_parts(gate1)) + dot(hot2, lane_parts(gate2))).astype(jnp.bfloat16)
    wait_all(backs)


def attend(heads, slot_count, where, line_hot, tokens, attention_gain, feedforward_gain, table_t, router_t, columns, slots_t, weights):
    length, width = tokens.shape
    experts = router_t.shape[0]
    act = shape((length, width))
    return call(
        lambda *refs: attend_body(heads, *refs),
        [
            act, act, act, act, act, act,
            shape((length, width), jnp.float32),
            shape((length, experts), jnp.float32),
            shape((length, 2), jnp.float32),
            shape((slot_count, width + LANES)),
        ],
        scratch=[
            pltpu.VMEM((4, width, width), jnp.bfloat16),
            pltpu.VMEM((heads, 2 * length), jnp.float32),
            pltpu.VMEM((5, length, width), jnp.bfloat16),
            pltpu.SemaphoreType.DMA((4,)),
            pltpu.SemaphoreType.DMA((5,)),
        ],
        in_specs=[SMEM] + [VMEM] * 8 + [HBM] * 4,
        out_specs=[HBM] * 5 + [VMEM] * 5,
        name="attend",
    )(where, tokens, attention_gain, feedforward_gain, table_t, line_hot, router_t, columns, slots_t, *weights)

def gelu_parts(x):
    slope = math.sqrt(2.0 / math.pi)
    cubic = 0.044715 * slope
    square = x * x
    half = 0.5 + 0.5 * jnp.tanh(x * (slope + cubic * square))
    act = x * half
    return act, half + (act - act * half) * (2.0 * slope + 6.0 * cubic * square)


def chunks_of(total, most):
    return [(start, min(most, total - start)) for start in range(0, total, most)]


FF_CHUNK = 768


def hidden_grad_body(rows, down, out, weight, arrived):
    spans = chunks_of(weight.shape[0], FF_CHUNK)
    copies = [
        pltpu.make_async_copy(
            down.at[0, pl.ds(start, size), :], weight.at[pl.ds(start, size), :], arrived.at[place]
        )
        for place, (start, size) in enumerate(spans)
    ]
    for copy in copies:
        copy.start()
    x = rows[...]
    for copy, (start, size) in zip(copies, spans):
        copy.wait()
        out[:, start : start + size] = dot(x, weight[start : start + size, :], COLS).astype(jnp.bfloat16)


def hidden_grad(rows, down_weight):
    count, width = rows.shape
    hidden = down_weight.shape[1]
    return call(
        hidden_grad_body,
        shape((count, hidden)),
        scratch=[
            pltpu.VMEM((hidden, width), jnp.bfloat16),
            pltpu.SemaphoreType.DMA((len(chunks_of(hidden, FF_CHUNK)),)),
        ],
        in_specs=[VMEM, HBM],
        out_specs=VMEM,
        name="hidden_grad",
    )(rows, down_weight)


EXPERT_CHUNK = 512


def expert_body(width, rows, back, gate_weight, up_weight, hidden, gate_low, up_low, out, gate, up, grads, kept, acts, total, arrived, left):
    spans = chunks_of(gate.shape[1], EXPERT_CHUNK)
    copies = []
    for place, (start, size) in enumerate(spans):
        span = pl.ds(start, size)
        for side, (source, target) in enumerate(
            ((gate_weight.at[0], gate), (up_weight.at[0], up), (back, grads))
        ):
            copies.append(
                pltpu.make_async_copy(source.at[:, span], target.at[:, span], arrived.at[3 * place + side])
            )
            copies[-1].start()
    count = len(spans)
    choice = jnp.zeros((rows.shape[0], 1), jnp.float32)
    backs = []
    for turn in range(count + 2):
        if turn < count:
            start, size = spans[turn]
            span = slice(start, start + size)
            for side in range(3):
                copies[3 * turn + side].wait()
            acts[turn % 2, 0, :, :size] = dot(rows[:, :width], gate[:, span])
            acts[turn % 2, 1, :, :size] = dot(rows[:, :width], up[:, span])
        if 0 < turn <= count:
            place = turn - 1
            start, size = spans[place]
            span = slice(start, start + size)
            act, slope = gelu_parts(acts[place % 2, 0, :, :size])
            up_act = acts[place % 2, 1, :, :size]
            grad = grads[:, span].astype(jnp.float32)
            value = act * up_act
            up_grad = grad * act
            kept[0, :, span] = value.astype(jnp.bfloat16)
            kept[1, :, span] = (grad * up_act * slope).astype(jnp.bfloat16)
            kept[2, :, span] = up_grad.astype(jnp.bfloat16)
            choice = choice + jnp.sum(up_grad * up_act, axis=1, keepdims=True)
        if turn > 1:
            place = turn - 2
            start, size = spans[place]
            span = slice(start, start + size)
            part = dot(kept[1, :, span], gate[:, span], COLS) + dot(kept[2, :, span], up[:, span], COLS)
            if place == 0:
                total[...] = part
            else:
                total[...] += part
            for which, target in enumerate((hidden, gate_low, up_low)):
                backs.append(
                    pltpu.make_async_copy(
                        kept.at[which, :, pl.ds(start, size)],
                        target.at[:, pl.ds(start, size)],
                        left.at[3 * place + which],
                    )
                )
                backs[-1].start()
    out[:, :width] = total[...].astype(jnp.bfloat16)
    out[:, width:] = lane_parts(choice)
    for copy in backs:
        copy.wait()


def expert(rows, back, gate_weight, up_weight):
    count = rows.shape[0]
    width, hidden = gate_weight.shape[1:]
    act = shape((count, hidden))
    chunks = len(chunks_of(hidden, EXPERT_CHUNK))
    return call(
        lambda *refs: expert_body(width, *refs),
        [act, act, act, shape(rows.shape)],
        scratch=[
            pltpu.VMEM((width, hidden), jnp.bfloat16),
            pltpu.VMEM((width, hidden), jnp.bfloat16),
            pltpu.VMEM((count, hidden), jnp.bfloat16),
            pltpu.VMEM((3, count, hidden), jnp.bfloat16),
            pltpu.VMEM((2, 2, count, EXPERT_CHUNK), jnp.float32),
            pltpu.VMEM((count, width), jnp.float32),
            pltpu.SemaphoreType.DMA((3 * chunks,)),
            pltpu.SemaphoreType.DMA((3 * chunks,)),
        ],
        in_specs=[VMEM] + [HBM] * 3,
        out_specs=[HBM, HBM, HBM, VMEM],
        name="expert",
    )(rows, back, gate_weight, up_weight)


def expert_out_body(hidden, down, out, acts, weight, total, arrived):
    spans = chunks_of(weight.shape[0], FF_CHUNK)
    copies = []
    for place, (start, size) in enumerate(spans):
        span = pl.ds(start, size)
        copies.append(pltpu.make_async_copy(hidden.at[:, span], acts.at[:, span], arrived.at[2 * place]))
        copies.append(pltpu.make_async_copy(down.at[0, span, :], weight.at[span, :], arrived.at[2 * place + 1]))
    start_all(copies)
    for place, (start, size) in enumerate(spans):
        wait_all(copies[2 * place : 2 * place + 2])
        part = dot(acts[:, start : start + size], weight[start : start + size, :])
        if place == 0:
            total[...] = part
        elif place < len(spans) - 1:
            total[...] += part
        else:
            out[...] = (total[...] + part).astype(jnp.bfloat16)


def expert_out(hidden, down_weight):
    count = hidden.shape[0]
    inner, width = down_weight.shape[1:]
    return call(
        expert_out_body,
        shape((count, width)),
        scratch=[
            pltpu.VMEM((count, inner), jnp.bfloat16),
            pltpu.VMEM((inner, width), jnp.bfloat16),
            pltpu.VMEM((count, width), jnp.float32),
            pltpu.SemaphoreType.DMA((2 * len(chunks_of(inner, FF_CHUNK)),)),
        ],
        in_specs=[HBM] * 2,
        out_specs=VMEM,
        name="expert_out",
    )(hidden, down_weight)


def expert_grads_body(count, width, *refs):
    sources, lefts, sent = refs[:count], refs[count : 2 * count], refs[2 * count]
    targets = refs[2 * count + 1 : 3 * count + 1]
    acts, turned, scaled, staged, arrived, left = refs[3 * count + 1 :]
    spans = chunks_of(sources[0].shape[1], FF_CHUNK)
    steps = [(which, start, size) for which in range(count) for start, size in spans]
    coming = start_all(
        [
            pltpu.make_async_copy(
                sources[which].at[:, pl.ds(start, size)], acts.at[which, :, pl.ds(start, size)], arrived.at[turn]
            )
            for turn, (which, start, size) in enumerate(steps)
        ]
    )
    gate = sum_parts(sent[:, width:])
    for which in range(count):
        scaled[which] = (lefts[which][:, :width].astype(jnp.float32) * gate).astype(jnp.bfloat16)
    backs = []
    for turn in range(len(steps) + 1):
        if turn < len(steps):
            which, start, size = steps[turn]
            coming[turn].wait()
            turned[turn % 2, :size, :] = acts[which, :, start : start + size].T
        if turn > 0:
            which, start, size = steps[turn - 1]
            slot = (turn - 1) % staged.shape[0]
            if turn - 1 >= staged.shape[0]:
                backs[turn - 1 - staged.shape[0]].wait()
            staged[slot, :size, :] = dot(turned[(turn - 1) % 2, :size, :], scaled[which]).astype(jnp.bfloat16)
            backs.append(
                pltpu.make_async_copy(
                    staged.at[slot, pl.ds(0, size), :], targets[which].at[pl.ds(start, size), :], left.at[turn - 1]
                )
            )
            backs[-1].start()
    wait_all(backs[-staged.shape[0] :])


def expert_grads(pairs, sent, width):
    count = len(pairs)
    slots, inner = pairs[0][0].shape
    chunks = len(chunks_of(inner, FF_CHUNK))
    return call(
        lambda *refs: expert_grads_body(count, width, *refs),
        [shape((inner, width))] * count,
        scratch=[
            pltpu.VMEM((count, slots, inner), jnp.bfloat16),
            pltpu.VMEM((2, FF_CHUNK, slots), jnp.bfloat16),
            pltpu.VMEM((count, slots, width), jnp.bfloat16),
            pltpu.VMEM((4, FF_CHUNK, width), jnp.bfloat16),
            pltpu.SemaphoreType.DMA((count * chunks,)),
            pltpu.SemaphoreType.DMA((count * chunks,)),
        ],
        in_specs=[HBM] * count + [VMEM] * (count + 1),
        out_specs=[HBM] * count,
        name="expert_grads",
    )(*[acts for acts, rows in pairs], *[rows for acts, rows in pairs], sent)


def combine_body(returned, columns, gates, middle, block_out):
    length = middle.shape[0]
    slot = iota((length, returned.shape[0]), 1)
    rows = returned[...]
    rows1 = dot(ones_where(slot == columns[:, 0:1]), rows)
    rows2 = dot(ones_where(slot == columns[:, 1:2]), rows)
    block_out[...] = (middle[...] + gates[:, 0:1] * rows1 + gates[:, 1:2] * rows2).astype(jnp.bfloat16)


def combine(returned, columns, gates, middle):
    length, width = middle.shape
    return call(
        combine_body,
        shape((length, width)),
        in_specs=[VMEM] * 4,
        out_specs=VMEM,
        name="combine",
    )(returned, columns, gates, middle)


def router_back(logit, choice, gate1, gate2, picked):
    experts = logit.shape[1]
    top = jnp.max(logit, axis=1, keepdims=True)
    grown = jnp.exp(logit - top)
    total = jnp.sum(grown, axis=1, keepdims=True)
    probs = grown / total
    lse = top + jnp.log(total)
    expert = iota(logit.shape, 1)
    hot1 = ones_where(expert == picked[:, 0:1], jnp.float32)
    hot = hot1 - ones_where(expert == picked[:, 1:2], jnp.float32)
    balance = (BALANCE_COEF * experts) * jnp.mean(hot1, axis=0, keepdims=True)
    even = jnp.sum(probs * balance, axis=1, keepdims=True)
    return hot * (choice * gate1 * gate2) + probs * (balance - even + 2.0 * Z_COEF * lse)


def diagonals(x):
    half = x.shape[0] // 2
    top, low = x[:half], x[half:]
    x = jnp.concatenate([low[:, :half], low[:, half:] + top[:, :half], top[:, half:], jnp.zeros_like(low[:, :half])], axis=1)
    while x.shape[0] > 1:
        half = x.shape[0] // 2
        x = pltpu.roll(x[:half], half, 1) + x[half:]
    return x


def attend_back_body(
    heads, sent_grad, columns, gates, middle, feedforward_gain, cotangent, table_t, line_hot,
    logits, router_t, query, key, value, wo,
    middle_grad, backs, gain_grad, bias_lines, router_grad,
    weight, acts, lines, heads_grad, grad_out, backs_out, arrived, left,
):
    length, width = middle.shape
    size = width // heads
    half = width // 2
    copies = start_all(
        [pltpu.make_async_copy(wo, weight, arrived.at[3])]
        + [
            pltpu.make_async_copy(source, acts.at[place], arrived.at[place])
            for place, source in enumerate((query, key, value))
        ]
    )
    lines[...] = dot(table_t[...], line_hot[1], precision=PRECISE)
    slot = iota((length, sent_grad.shape[0]), 1)
    rows = sent_grad[...]
    rows1 = dot(ones_where(slot == columns[:, 0:1]), rows)
    rows2 = dot(ones_where(slot == columns[:, 1:2]), rows)
    gate1, gate2 = gates[:, 0:1], gates[:, 1:2]
    choice = sum_parts(rows1[:, width:] - rows2[:, width:])
    logit_grad = router_back(logits[...], choice, gate1, gate2, columns[:, 2:4])
    mid = middle[...]
    r = rms(mid)
    scaled = mid * r
    high, rest = split2(scaled * feedforward_gain[...])
    grad_high, grad_rest = split2(logit_grad)
    router_high, router_rest = split2(router_t[...])
    router_grad[...] = dot(grad_high, high, ROWS) + dot(grad_rest, high, ROWS) + dot(grad_high, rest, ROWS)
    normed2_grad = (
        gate1 * rows1[:, :width]
        + gate2 * rows2[:, :width]
        + (dot(grad_high, router_high) + dot(grad_rest, router_high) + dot(grad_high, router_rest))
    )
    u = normed2_grad * feedforward_gain[...]
    gain_grad[...] = jnp.sum(normed2_grad * scaled, axis=0, keepdims=True)
    grad = (
        cotangent[...].astype(jnp.float32)
        + r * u
        - mid * (r * r * r * jnp.mean(u * mid, axis=1, keepdims=True))
    )
    grad_out[...] = grad
    grad_copy = pltpu.make_async_copy(grad_out, middle_grad, left.at[2])
    grad_copy.start()
    low = grad.astype(jnp.bfloat16)
    wait_all(copies)
    heads_grad[...] = dot(low, weight[...], COLS).astype(jnp.bfloat16)
    backs_out[:, 3 * width :] = low
    pair_width = 2 * size
    first = iota((length, pair_width), 1) < size
    first_t = iota((pair_width, length), 0) < size
    zero = jnp.zeros((length, pair_width), jnp.bfloat16)
    scale = jnp.bfloat16(1.0 / math.sqrt(size))
    for pair in range(heads // 2):
        start = pair * pair_width
        span = slice(start, start + pair_width)
        q, k, v, g = acts[0, :, span] * scale, acts[1, :, span], acts[2, :, span], heads_grad[:, span]
        k_turned = (k * scale).T
        kept = []
        for side in range(2):
            q_side = jnp.where(first, q, zero) if side == 0 else jnp.where(first, zero, q)
            g_side = jnp.where(first, g, zero) if side == 0 else jnp.where(first, zero, g)
            head = 2 * pair + side
            line = jnp.broadcast_to(lines[head : head + 1, :], (length, 2 * length))
            bias = pltpu.roll(line, length + 1, 1, stride=1, stride_axis=0)[:, :length]
            scores = dot(k, q_side, COLS) + bias
            top = jnp.max(scores, axis=0, keepdims=True)
            grown = jnp.exp(scores - top)
            probs = grown * (1.0 / jnp.sum(grown, axis=0, keepdims=True))
            probs_grad = dot(v, g_side, COLS)
            score_grad = probs * (probs_grad - jnp.sum(probs * probs_grad, axis=0, keepdims=True))
            score_low = score_grad.astype(jnp.bfloat16)
            bias_lines[head : head + 1, :] = diagonals(score_low.astype(jnp.float32))
            kept.append(
                (
                    dot(k_turned, score_low),
                    dot(score_low, q),
                    dot(probs.astype(jnp.bfloat16), g),
                )
            )
        results = (
            jnp.where(first_t, kept[0][0], kept[1][0]).astype(jnp.bfloat16).T,
            jnp.where(first, kept[0][1], kept[1][1]).astype(jnp.bfloat16),
            jnp.where(first, kept[0][2], kept[1][2]).astype(jnp.bfloat16),
        )
        for place, result in enumerate(results):
            backs_out[:, place * width + start : place * width + start + pair_width] = result
    leaving = pltpu.make_async_copy(backs_out, backs, left.at[0])
    leaving.start()
    leaving.wait()
    grad_copy.wait()


def attend_back(heads, line_hot, sent_grad, columns, gates, middle, feedforward_gain, cotangent, table_t, logits, router_t, query, key, value, wo):
    length, width = middle.shape
    return call(
        lambda *refs: attend_back_body(heads, *refs),
        [
            shape((length, width), jnp.float32),
            shape((length, 4 * width)),
            shape((1, width), jnp.float32),
            shape((heads, 2 * length), jnp.float32),
            shape(router_t.shape, jnp.float32),
        ],
        scratch=[
            pltpu.VMEM((width, width), jnp.bfloat16),
            pltpu.VMEM((3, length, width), jnp.bfloat16),
            pltpu.VMEM((heads, 2 * length), jnp.float32),
            pltpu.VMEM((length, width), jnp.bfloat16),
            pltpu.VMEM((length, width), jnp.float32),
            pltpu.VMEM((length, 4 * width), jnp.bfloat16),
            pltpu.SemaphoreType.DMA((4,)),
            pltpu.SemaphoreType.DMA((3,)),
        ],
        in_specs=[VMEM] * 10 + [HBM] * 4,
        out_specs=[HBM] * 2 + [VMEM] * 3,
        name="attend_back",
    )(sent_grad, columns, gates, middle, feedforward_gain, cotangent, table_t, line_hot, logits, router_t, query, key, value, wo)


def input_back_body(backs_in, grad_in, tokens, attention_gain, bias_lines, line_hot, wq, wk, wv, input_grad, vectors, weights, backs, middle_grad, arrived):
    length, width = tokens.shape
    copies = []
    for place, source in enumerate((wq, wk, wv)):
        span = pl.ds(place * width, width)
        copies.append(pltpu.make_async_copy(backs_in.at[:, span], backs.at[:, span], arrived.at[place]))
        copies.append(pltpu.make_async_copy(source, weights.at[place], arrived.at[3 + place]))
    copies.append(pltpu.make_async_copy(grad_in, middle_grad, arrived.at[6]))
    start_all(copies)
    bias = dot(bias_lines[...], line_hot[1], COLS, PRECISE)
    rows = bias.shape[0] // 4
    bias = jnp.concatenate([bias[rows * part : rows * (part + 1)] for part in range(4)], axis=1)
    x = tokens[...].astype(jnp.float32)
    s = rms(x)
    total = jnp.zeros((length, width), jnp.float32)
    for place in range(3):
        wait_all(copies[2 * place : 2 * place + 2])
        total = total + dot(backs[:, place * width : (place + 1) * width], weights[place], COLS)
    w = total * attention_gain[...]
    gain = jnp.sum(total * x * s, axis=0, keepdims=True)
    vectors[...] = jnp.zeros_like(vectors)
    for part in range(width // LANES):
        vectors[part : part + 1, :] = gain[:, part * LANES : (part + 1) * LANES]
    vectors[width // LANES : width // LANES + rows, :] = bias
    copies[6].wait()
    input_grad[...] = middle_grad[...] + s * w - x * (s * s * s * jnp.mean(w * x, axis=1, keepdims=True))


def input_back(line_hot, backs, middle_grad, tokens, attention_gain, bias_lines, wq, wk, wv):
    length, width = tokens.shape
    return call(
        input_back_body,
        [
            shape((length, width), jnp.float32),
            shape((BLOCK, LANES), jnp.float32),
        ],
        scratch=[
            pltpu.VMEM((3, width, width), jnp.bfloat16),
            pltpu.VMEM((length, 3 * width), jnp.bfloat16),
            pltpu.VMEM((length, width), jnp.float32),
            pltpu.SemaphoreType.DMA((7,)),
        ],
        in_specs=[HBM] * 2 + [VMEM] * 4 + [HBM] * 3,
        out_specs=[VMEM] * 2,
        name="input_back",
    )(backs, middle_grad, tokens, attention_gain, bias_lines, line_hot, wq, wk, wv)


EXTRA = 2 * LANES


def resplit(lanes):
    half = LANES // 2
    total = lanes + pltpu.roll(lanes, half, 1)
    high = total.astype(jnp.bfloat16).astype(jnp.float32)
    return jnp.where(iota(lanes.shape, 1) < half, high, total - high)


def rotated(place, side, block, step):
    return pl.ds(pl.multiple_of(((place + step) % side) * block, block), block)


def products_body(side, where, normed, heads_out, left_far, backs_in, far_in, feedforward_gain, router, *rest):
    pieces, (lefts, backs, payload, vectors, arrived, left) = rest[:side], rest[side:]
    length, width = normed.shape
    half = width // 2
    mine = pl.ds(pl.multiple_of(where[0] * half, half), half)
    copies = start_all(
        [
            pltpu.make_async_copy(normed.at[:, mine], lefts.at[0, :, pl.ds(0, half)], arrived.at[0]),
            pltpu.make_async_copy(heads_out.at[:, mine], lefts.at[0, :, pl.ds(half, half)], arrived.at[1]),
            pltpu.make_async_copy(left_far, lefts.at[1], arrived.at[2]),
        ]
        + [
            pltpu.make_async_copy(
                source.at[:, pl.ds(place * width, width)],
                backs.at[which, :, pl.ds(place * width, width)],
                arrived.at[3 + 2 * place + which],
            )
            for place in range(4)
            for which, source in enumerate((backs_in, far_in))
        ]
    )
    experts = router.shape[0]
    vectors[...] = jnp.zeros_like(vectors)
    vectors[0:1, :] = feedforward_gain[...]
    vectors[8 : 8 + experts, :] = router[...]
    for place in range(2):
        start = 4 * width + place * LANES
        payload[:, start : start + LANES] = resplit(vectors[:, place * half : (place + 1) * half].T).astype(jnp.bfloat16)
    position = where[2 + where[0]]
    leaving = []

    def leave(part, start, size):
        for step, piece in enumerate(pieces):
            leaving.append(
                pltpu.make_async_copy(
                    payload.at[rotated(position, side, half // side, step), pl.ds(start, size)],
                    piece.at[:, pl.ds(start, size)],
                    left.at[part * side + step],
                )
            )
            leaving[-1].start()

    leave(4, 4 * width, EXTRA)
    wait_all(copies[:3])
    for place in range(4):
        wait_all(copies[3 + 2 * place : 5 + 2 * place])
        span = slice(place * width, (place + 1) * width)
        start = 0 if place < 3 else half
        payload[:, span] = (
            dot(lefts[0, :, start : start + half], backs[0, :, span], ROWS)
            + dot(lefts[1, :, start : start + half], backs[1, :, span], ROWS)
        ).astype(jnp.bfloat16)
        leave(place, place * width, width)
    wait_all(leaving)


def products(where, side, normed, heads_out, left_far, backs, backs_far, feedforward_gain, router):
    length, width = normed.shape
    wide = 4 * width + EXTRA
    return call(
        lambda *refs: products_body(side, *refs),
        [shape((width // 2 // side, wide))] * side,
        scratch=[
            pltpu.VMEM((2, length, width), jnp.bfloat16),
            pltpu.VMEM((2, length, 4 * width), jnp.bfloat16),
            pltpu.VMEM((width // 2, wide), jnp.bfloat16),
            pltpu.VMEM((LANES, width), jnp.float32),
            pltpu.SemaphoreType.DMA((11,)),
            pltpu.SemaphoreType.DMA((5 * side,)),
        ],
        in_specs=[SMEM] + [HBM] * 5 + [VMEM] * 2,
        out_specs=[HBM] * side,
        name="products",
    )(where, normed, heads_out, left_far, backs, backs_far, feedforward_gain, router)


def total_into(out, refs, late):
    total = refs[0][...].astype(jnp.float32)
    for ref in refs[1:]:
        total = total + ref[...].astype(jnp.float32)
    wide = total.shape[1] - EXTRA - (LANES if late else 0)
    out[:, :wide] = total[:, :wide].astype(jnp.bfloat16)
    for start in range(wide, wide + EXTRA, LANES):
        out[:, start : start + LANES] = resplit(total[:, start : start + LANES]).astype(jnp.bfloat16)
    if late:
        out[:, wide + EXTRA :] = stack_parts(total[:BLOCK, wide + EXTRA :] + total[BLOCK:, wide + EXTRA :])


def stack_parts(block):
    return jnp.concatenate(split2(block), axis=0)


def fold_body(side, where, vectors, *refs):
    pieces, outs, total = refs[:side], refs[side : 2 * side], refs[-1]
    total_into(total, pieces, False)
    position = where[3 - where[0]]
    wide = total.shape[1]
    late = stack_parts(vectors[...])
    for step, out in enumerate(outs):
        out[:, :wide] = total[rotated(position, side, out.shape[0], step), :]
        out[:, wide:] = late


def fold(where, side, vectors, pieces):
    rows, wide = pieces[0].shape
    return call(
        lambda *refs: fold_body(side, *refs),
        [shape((rows // side, wide + LANES))] * side,
        scratch=[pltpu.VMEM((rows, wide), jnp.bfloat16)],
        in_specs=[SMEM] + [VMEM] * (side + 1),
        out_specs=[VMEM] * side,
        vmem=16,
        name="fold",
    )(where, vectors, *pieces)


def add_pieces(pieces):
    return call(
        lambda *refs: total_into(refs[-1], refs[:-1], True),
        shape(pieces[0].shape),
        in_specs=[VMEM] * len(pieces),
        out_specs=VMEM,
        vmem=12,
        name="add_pieces",
    )(*pieces)


def put_body(side, where, *refs):
    pieces, (whole, upper, lower) = refs[:side], refs[side:]
    position = where[3 - where[0]]
    rows = upper.shape[0]
    for step in range(side):
        whole[rotated(position, side, pieces[0].shape[0], step), :] = pieces[step][...]
    upper[...] = whole[:rows, :]
    lower[...] = whole[rows:, :]


def put(where, side, pieces):
    rows, wide = pieces[0].shape
    half = shape((side * rows // 2, wide))
    return call(
        lambda *refs: put_body(side, *refs),
        [shape((side * rows, wide)), half, half],
        in_specs=[SMEM] + [VMEM] * side,
        out_specs=[VMEM] * 3,
        vmem=24,
        name="put",
    )(where, *pieces)


def again_body(whole, upper, lower):
    rows = upper.shape[0]
    upper[...] = whole[:rows, :]
    lower[...] = whole[rows:, :]


def again(whole):
    half = shape((whole.shape[0] // 2, whole.shape[1]))
    return call(again_body, [half, half], in_specs=[VMEM], out_specs=[VMEM] * 2, vmem=24, name="again")(whole)


def finish_body(side, steps, where, *refs):
    parts = sum(len(order) for step, order in steps)
    pieces, refs = (refs[:parts], refs[parts : 2 * parts]), refs[2 * parts :]
    up_low, *outs, up_out, gain, feedforward_gain, router_t, bias_t, held, staged, up_held, up_staged, late, arrived, left = refs
    rows = staged.shape[2]
    width = staged.shape[3]
    half = width // 2
    copies = []
    for which in range(2):
        place = 0
        for block, (step, order) in enumerate(steps):
            size = rows // len(order)
            copies.append(
                start_all(
                    [
                        pltpu.make_async_copy(
                            pieces[which][place + part],
                            held.at[which, block, pl.ds(order[part] * size, size), :],
                            arrived.at[which * parts + place + part],
                        )
                        for part in range(len(order))
                    ]
                )
            )
            place += len(order)
    up_copy = pltpu.make_async_copy(up_low, up_held, arrived.at[2 * parts])
    up_copy.start()
    for vector in (feedforward_gain, router_t, late):
        vector[...] = jnp.zeros_like(vector)
    backs = []
    for block, (step, order) in enumerate(steps):
        for which in range(2):
            core = where[0] if which == 0 else 1 - where[0]
            slot = which * len(steps) + block
            wait_all(copies[slot])
            start = pl.multiple_of(((where[2 + core] + step) % side) * rows, rows)
            line = pl.ds(pl.multiple_of(core * half + start, rows), rows)
            for matrix in range(4):
                staged[slot, matrix] = held[which, block, :, matrix * width : (matrix + 1) * width].astype(jnp.float32)
                backs.append(
                    pltpu.make_async_copy(
                        staged.at[slot, matrix], outs[matrix].at[line, :], left.at[4 * slot + matrix]
                    )
                )
                backs[-1].start()
            for place in range(2):
                lanes = held[which, block, :, 4 * width + place * LANES : 4 * width + (place + 1) * LANES]
                lanes = lanes.astype(jnp.float32)
                turned = (lanes + pltpu.roll(lanes, LANES // 2, 1)).T
                line = pl.ds(pl.multiple_of(place * half + start, rows), rows)
                feedforward_gain[:, line] += turned[0:1]
                router_t[:, line] += turned[8 : 8 + router_t.shape[0]]
            block_rows = held[which, block, : 2 * BLOCK, 4 * width + EXTRA :].astype(jnp.float32)
            late[...] += block_rows[:BLOCK] + block_rows[BLOCK:]
    up_copy.wait()
    up_staged[...] = up_held[...].astype(jnp.float32)
    backs.append(pltpu.make_async_copy(up_staged, up_out, left.at[8 * len(steps)]))
    backs[-1].start()
    lines = width // LANES
    for part in range(lines):
        gain[:, part * LANES : (part + 1) * LANES] = late[part : part + 1, :]
    heads, buckets = bias_t.shape
    for part in range(4):
        bias_t[part * heads // 4 : (part + 1) * heads // 4, :] = late[
            lines : lines + heads // 4, part * buckets : (part + 1) * buckets
        ]
    wait_all(backs)


def finish(where, side, steps, near, far, up_low, experts, buckets, heads):
    wide = near[0].shape[1]
    width = (wide - EXTRA - LANES) // 4
    rows = width // 2 // side
    count, parts = len(steps), len(near)
    return call(
        lambda *refs: finish_body(side, steps, *refs),
        [shape((width, width), jnp.float32)] * 4
        + [
            shape(up_low.shape, jnp.float32),
            shape((1, width), jnp.float32),
            shape((1, width), jnp.float32),
            shape((experts, width), jnp.float32),
            shape((heads, buckets), jnp.float32),
        ],
        scratch=[
            pltpu.VMEM((2, count, rows, wide), jnp.bfloat16),
            pltpu.VMEM((2 * count, 4, rows, width), jnp.float32),
            pltpu.VMEM(up_low.shape, jnp.bfloat16),
            pltpu.VMEM(up_low.shape, jnp.float32),
            pltpu.VMEM((BLOCK, LANES), jnp.float32),
            pltpu.SemaphoreType.DMA((2 * parts + 1,)),
            pltpu.SemaphoreType.DMA((8 * count + 1,)),
        ],
        in_specs=[SMEM] + [HBM] * (2 * parts + 1),
        out_specs=[HBM] * 5 + [VMEM] * 4,
        name="finish",
    )(where, *near, *far, up_low)


def rotate_x(count, step):
    return [(x * 2 + c, ((x + step) % count) * 2 + c) for x in range(count) for c in range(2)]


def rotate_plane(chips, side, flip, step):
    pairs = []
    for x in range(chips):
        for core in range(2):
            for z in range(side):
                for y in range(side):
                    along_z = core ^ flip
                    to = ((z + step) % side, y) if along_z else (z, (y + step) % side)
                    base = (x * 2 + core) * side * side
                    pairs.append((base + z * side + y, base + to[0] * side + to[1]))
    return pairs


def swap_cores(count):
    return [(x * 2 + c, x * 2 + 1 - c) for x in range(count) for c in range(2)]


def shards(
    tokens,
    routes,
    cotangent,
    attention_gain,
    query_weight,
    key_weight,
    value_weight,
    output_weight,
    bias_table,
    feedforward_gain,
    router_weight,
    gate_weight,
    up_weight,
    down_weight,
):
    length, width = tokens.shape
    buckets, heads = bias_table.shape
    experts = lax.axis_size("expert")
    chips = lax.axis_size("dp") // 2
    side = math.isqrt(experts)
    replica, expert_place = lax.axis_index("dp"), lax.axis_index("expert")
    where = jnp.stack([replica % 2, replica // 2, expert_place % side, expert_place // side])
    capacity = max(2, (10 * length + 4 * experts - 1) // (4 * experts))
    swap = swap_cores(chips)
    line_hot = jnp.asarray(bucket_lines(length, buckets))
    gain1, gain2 = attention_gain[None], feedforward_gain[None]

    def exchange(rows):
        return lax.all_to_all(
            rows.reshape(experts, capacity, -1), "expert", split_axis=0, concat_axis=0, tiled=True
        ).reshape(experts * capacity, -1)

    table_t, router_t = bias_table.T, router_weight.T
    slots_t, columns, cot_slots = route(routes, cotangent, experts, capacity)
    cot_rows = exchange(cot_slots)
    normed, query, key, value, heads_out, left, middle, logits, gates, sent = attend(
        heads, experts * capacity, where, line_hot, tokens, gain1, gain2, table_t, router_t, columns, slots_t,
        (query_weight, key_weight, value_weight, output_weight),
    )

    def swapped(array):
        return lax.ppermute(array, "dp", swap)

    rows = exchange(sent)
    left_far = swapped(left)
    back = hidden_grad(cot_rows, down_weight)
    rows, left_far = lax.optimization_barrier((rows, left_far))
    hidden, gate_low, up_acts, rows_grad = expert(rows, back, gate_weight, up_weight)
    sent_grad = exchange(rows_grad)

    def scatter_dp(part):
        return lax.psum_scatter(part, "dp", scatter_dimension=0, tiled=True)

    grads = expert_grads(((hidden, cot_rows), (gate_low, rows)), rows, width)
    sent_grad, grads = lax.optimization_barrier((sent_grad, grads))
    down_grad, gate_grad = scatter_dp(grads[0]), scatter_dp(grads[1])

    middle_grad, backs, gain2_part, bias_lines, router_part = attend_back(
        heads, line_hot, sent_grad, columns, gates, middle, gain2, cotangent, table_t, logits,
        router_t, query, key, value, output_weight,
    )
    backs_far = swapped(backs)
    pieces = products(where, side, normed, heads_out, left_far, backs, backs_far, gain2_part, router_part)

    def turn(piece, flip, step):
        return lax.ppermute(piece, ("dp", "expert"), rotate_plane(chips, side, flip, step))

    def scatter_plane(pieces, flip):
        return [pieces[0]] + [turn(pieces[step], flip, step) for step in range(1, side)]

    pieces, hidden, backs = lax.optimization_barrier((pieces, hidden, backs))
    folded_in = scatter_plane(pieces, 0)
    input_grad, vectors = input_back(
        line_hot, backs, middle_grad, tokens, gain1, bias_lines, query_weight, key_weight, value_weight
    )
    returned = expert_out(hidden, down_weight)
    down_grad = down_grad.astype(jnp.float32)
    folded_in, vectors, returned, down_grad = lax.optimization_barrier((folded_in, vectors, returned, down_grad))
    shard = add_pieces(scatter_plane(fold(where, side, vectors, folded_in), 1))
    shard, returned, up_acts = lax.optimization_barrier((shard, returned, up_acts))
    returned = exchange(returned)
    (up_part,) = expert_grads(((up_acts, rows),), rows, width)
    total = add_pieces([shard] + [lax.ppermute(shard, "dp", rotate_x(chips, step)) for step in range(1, chips)])
    total, up_part, returned = lax.optimization_barrier((total, up_part, returned))
    up_low = scatter_dp(up_part)
    gathered = [total] + [turn(total, 1, -step) for step in range(1, side)]
    gate_grad = gate_grad.astype(jnp.float32)
    block_out = combine(returned, columns, gates, middle)
    gathered, gate_grad, block_out = lax.optimization_barrier((gathered, gate_grad, block_out))
    own, upper, lower = put(where, side, gathered)
    minus_upper, plus_lower = turn(upper, 0, 1), turn(lower, 0, -1)
    upper2, lower2 = again(own)
    minus_lower, plus_upper = turn(lower2, 0, 1), turn(upper2, 0, -1)
    across = [turn(minus_upper, 0, 1), turn(plus_lower, 0, -1)]
    near = [own, plus_lower, plus_upper, minus_lower, minus_upper, *across]
    far = [swapped(piece) for piece in near]
    query_grad, key_grad, value_grad, output_grad, up_grad, gain1_grad, gain2_grad, router_grad_t, bias_grad_t = finish(
        where, side, ((0, (0,)), (1, (1, 0)), (3, (1, 0)), (2, (0, 1))), near, far, up_low, experts, buckets, heads
    )
    return (
        block_out,
        input_grad,
        gain1_grad[0],
        query_grad,
        key_grad,
        value_grad,
        output_grad,
        bias_grad_t.T,
        gain2_grad[0],
        router_grad_t.T,
        gate_grad.T[None],
        up_grad.T[None],
        down_grad[None],
    )


def solution(mesh):
    return jax.shard_map(
        shards,
        mesh=mesh,
        in_specs=(
            P(("dp", "expert"), None),
            P(("dp", "expert"), None),
            P(("dp", "expert"), None),
            P(),
            P(),
            P(),
            P(),
            P(),
            P(),
            P(),
            P(),
            P("expert", None, None),
            P("expert", None, None),
            P("expert", None, None),
        ),
        out_specs=(
            P(("dp", "expert"), None),
            P(("dp", "expert"), None),
            P(),
            P(),
            P(),
            P(),
            P(),
            P(),
            P(),
            P(),
            P("expert", None, "dp"),
            P("expert", None, "dp"),
            P("expert", "dp", None),
        ),
        check_vma=False,
    )
```

```python
import math

import jax
import jax.numpy as jnp
import numpy as np
from jax import lax
from jax.experimental import pallas as pl
from jax.experimental.pallas import tpu as pltpu
from jax.sharding import PartitionSpec as P

EPSILON = 1e-06
Z_COEF = 0.001
BALANCE_COEF = 0.01
PRECISE = lax.Precision.HIGHEST
LANES = 128
BLOCK = 16
MIB = 1024 * 1024
VMEM = pl.BlockSpec(memory_space=pltpu.VMEM)
HBM = pl.BlockSpec(memory_space=pl.ANY)
SMEM = pl.BlockSpec(memory_space=pltpu.SMEM)


def bucket_table(length, bucket_count):
    half_count = bucket_count // 2
    exact_count = half_count // 2
    position = np.arange(length)
    relative = position[None, :] - position[:, None]
    distance = np.abs(relative)
    spread = (
        np.log(np.maximum(distance, 1) / exact_count)
        / np.log(128.0 / exact_count)
        * (half_count - exact_count)
    )
    far_bucket = np.minimum(
        exact_count + np.floor(np.maximum(spread, 0.0)).astype(np.int32), half_count - 1
    )
    bucket_index = np.where(distance < exact_count, distance, far_bucket)
    return (bucket_index + (relative > 0) * half_count).astype(np.int32)


def bucket_lines(length, bucket_count):
    table = bucket_table(length, bucket_count)
    line = np.concatenate([table[::-1, 0], table[0, 1:]])
    hot = np.zeros((2, bucket_count, 2 * length), np.float32)
    for place, bucket in enumerate(line):
        hot[0, bucket, place] = 1.0
        hot[1, bucket, 2 * length - 2 - place] = 1.0
    return hot


def dot(left, right, dims=((1,), (0,)), precision=None):
    return lax.dot_general(
        left, right, (dims, ((), ())), precision=precision, preferred_element_type=jnp.float32
    )


ROWS = ((0,), (0,))
COLS = ((1,), (1,))


def iota(shape, axis):
    return lax.broadcasted_iota(jnp.int32, shape, axis)


def ones_where(condition, dtype=jnp.bfloat16):
    return jnp.where(condition, 1.0, 0.0).astype(dtype)


def call(body, outs, scratch=(), vmem=63, flops=1024, **options):
    return pl.pallas_call(
        body,
        out_shape=outs,
        scratch_shapes=list(scratch),
        compiler_params=pltpu.CompilerParams(vmem_limit_bytes=vmem * MIB),
        cost_estimate=pl.CostEstimate(flops=flops, bytes_accessed=1024, transcendentals=0),
        **options,
    )


def shape(dims, dtype=jnp.bfloat16):
    return jax.ShapeDtypeStruct(dims, dtype)


def route_body(capacity, experts, routes_t, cotangent, slots_t, columns, cot_slots):
    length = cotangent.shape[0]
    before = ones_where(iota((length, length), 0) < iota((length, length), 1))
    picked = routes_t[...]
    expert = iota((experts, length), 0)
    hot1 = ones_where(expert == picked[0:1], jnp.float32)
    hot2 = ones_where(expert == picked[1:2], jnp.float32)
    filled = jnp.sum(hot1, axis=1, keepdims=True)
    number1 = dot(hot1.astype(jnp.bfloat16), before)
    number2 = dot(hot2.astype(jnp.bfloat16), before) + filled
    place1 = jnp.sum(number1 * hot1, axis=0, keepdims=True).astype(jnp.int32)
    place2 = jnp.sum(number2 * hot2, axis=0, keepdims=True).astype(jnp.int32)
    slot1 = jnp.where(place1 < capacity, picked[0:1] * capacity + place1, -1)
    slot2 = jnp.where(place2 < capacity, picked[1:2] * capacity + place2, -1)
    slots_t[0:1] = slot1
    slots_t[1:2] = slot2
    lines = jnp.concatenate([slot1, slot2, picked, jnp.zeros((4, length), jnp.int32)], axis=0)
    columns[...] = lines.T
    slot = iota((experts * capacity, length), 0)
    dispatch = ones_where((slot == slot1) | (slot == slot2))
    cot_slots[...] = dot(dispatch, cotangent[...]).astype(jnp.bfloat16)


def route(routes, cotangent, experts, capacity):
    length, width = cotangent.shape
    return call(
        lambda *refs: route_body(capacity, experts, *refs),
        [
            shape((2, length), jnp.int32),
            shape((length, 8), jnp.int32),
            shape((experts * capacity, width)),
        ],
        in_specs=[VMEM] * 2,
        out_specs=[VMEM] * 3,
        name="route",
    )(routes.T, cotangent)


def start_all(copies):
    for copy in copies:
        copy.start()
    return copies


def wait_all(copies):
    for copy in copies:
        copy.wait()


def split2(x):
    high = x.astype(jnp.bfloat16)
    return high, (x - high.astype(jnp.float32)).astype(jnp.bfloat16)


def rms(x):
    return lax.rsqrt(jnp.mean(x * x, axis=1, keepdims=True) + EPSILON)


def split3(x):
    high = x.astype(jnp.bfloat16)
    rest = x - high.astype(jnp.float32)
    mid = rest.astype(jnp.bfloat16)
    return high, mid, (rest - mid.astype(jnp.float32)).astype(jnp.bfloat16)


def lane_parts(column):
    lane = iota((column.shape[0], LANES), 1)
    spread = jnp.zeros(lane.shape, jnp.float32)
    for place, part in enumerate(split3(column)):
        spread = jnp.where(lane == place, part.astype(jnp.float32), spread)
    return spread.astype(jnp.bfloat16)


def sum_parts(lanes):
    parts = lanes.astype(jnp.float32)
    return parts[:, 0:1] + parts[:, 1:2] + parts[:, 2:3]


def attend_body(
    heads, where, tokens, attention_gain, feedforward_gain, table_t, line_hot, router_t, columns, slots_t,
    wq, wk, wv, wo,
    normed_out, query_out, key_out, value_out, heads_done, left_send, middle, logits, gates, sent,
    weights, lines, acts, arrived, left,
):
    length, width = tokens.shape
    size = width // heads
    copies = [
        pltpu.make_async_copy(source, weights.at[place], arrived.at[place])
        for place, source in enumerate((wq, wk, wv, wo))
    ]
    start_all(copies[:3])
    backs = [
        pltpu.make_async_copy(acts.at[place], target, left.at[place])
        for place, target in enumerate((normed_out, query_out, key_out, value_out, heads_done))
    ]
    lines[...] = dot(table_t[...], line_hot[0], precision=PRECISE)
    wait_all(copies[:3])
    copies[3].start()
    x = tokens[...].astype(jnp.float32)
    low = (x * rms(x) * attention_gain[...]).astype(jnp.bfloat16)
    acts[0] = low
    backs[0].start()
    for place in range(3):
        acts[place + 1] = dot(acts[0], weights[place]).astype(jnp.bfloat16)
        backs[place + 1].start()
    first = iota((length, 2 * size), 1) < size
    zero = jnp.zeros((length, 2 * size), jnp.bfloat16)
    scale = 1.0 / math.sqrt(size)
    for pair in range(heads // 2):
        span = slice(pair * 2 * size, (pair + 1) * 2 * size)
        q, k, v = acts[1, :, span] * jnp.bfloat16(scale), acts[2, :, span], acts[3, :, span]
        outs = []
        for side in range(2):
            q_side = jnp.where(first, q, zero) if side == 0 else jnp.where(first, zero, q)
            head = 2 * pair + side
            line = jnp.broadcast_to(lines[head : head + 1, :], (length, 2 * length))
            bias = pltpu.roll(line, length + 1, 1, stride=1, stride_axis=0)[:, :length]
            scores = dot(q_side, k, COLS) + bias
            top = jnp.max(scores, axis=1, keepdims=True)
            grown = jnp.exp(scores - top)
            total = jnp.sum(grown, axis=1, keepdims=True)
            outs.append(dot((grown * (1.0 / total)).astype(jnp.bfloat16), v))
        acts[4, :, span] = jnp.where(first, outs[0], outs[1]).astype(jnp.bfloat16)
    backs[4].start()
    half = width // 2
    other = pl.ds(pl.multiple_of((1 - where[0]) * half, half), half)
    left_send[:, :half] = acts[0, :, other]
    left_send[:, half:] = acts[4, :, other]
    copies[3].wait()
    mid = x + dot(acts[4], weights[3])
    middle[...] = mid
    normed2 = mid * rms(mid) * feedforward_gain[...]
    high, rest = split2(normed2)
    experts = router_t.shape[0]
    router_high, router_rest = split2(router_t[...])
    logit = dot(high, router_high, COLS) + dot(high, router_rest, COLS) + dot(rest, router_high, COLS)
    logits[...] = logit
    picked = columns[:, 2:4]
    expert = iota(logit.shape, 1)
    logit1 = jnp.sum(jnp.where(expert == picked[:, 0:1], logit, 0.0), axis=1, keepdims=True)
    logit2 = jnp.sum(jnp.where(expert == picked[:, 1:2], logit, 0.0), axis=1, keepdims=True)
    gate1 = 1.0 / (1.0 + jnp.exp(logit2 - logit1))
    gate2 = 1.0 / (1.0 + jnp.exp(logit1 - logit2))
    gates[:, 0:1] = gate1
    gates[:, 1:2] = gate2
    slot = iota((sent.shape[0], length), 0)
    hot1 = ones_where(slot == slots_t[0:1])
    hot2 = ones_where(slot == slots_t[1:2])
    sent[:, :width] = dot(hot1 + hot2, high).astype(jnp.bfloat16)
    sent[:, width:] = (dot(hot1, lane_parts(gate1)) + dot(hot2, lane_parts(gate2))).astype(jnp.bfloat16)
    wait_all(backs)


def attend(heads, slot_count, where, line_hot, tokens, attention_gain, feedforward_gain, table_t, router_t, columns, slots_t, weights):
    length, width = tokens.shape
    experts = router_t.shape[0]
    act = shape((length, width))
    return call(
        lambda *refs: attend_body(heads, *refs),
        [
            act, act, act, act, act, act,
            shape((length, width), jnp.float32),
            shape((length, experts), jnp.float32),
            shape((length, 2), jnp.float32),
            shape((slot_count, width + LANES)),
        ],
        scratch=[
            pltpu.VMEM((4, width, width), jnp.bfloat16),
            pltpu.VMEM((heads, 2 * length), jnp.float32),
            pltpu.VMEM((5, length, width), jnp.bfloat16),
            pltpu.SemaphoreType.DMA((4,)),
            pltpu.SemaphoreType.DMA((5,)),
        ],
        in_specs=[SMEM] + [VMEM] * 8 + [HBM] * 4,
        out_specs=[HBM] * 5 + [VMEM] * 5,
        name="attend",
    )(where, tokens, attention_gain, feedforward_gain, table_t, line_hot, router_t, columns, slots_t, *weights)

def gelu_parts(x):
    slope = math.sqrt(2.0 / math.pi)
    cubic = 0.044715 * slope
    square = x * x
    half = 0.5 + 0.5 * jnp.tanh(x * (slope + cubic * square))
    act = x * half
    return act, half + (act - act * half) * (2.0 * slope + 6.0 * cubic * square)


def chunks_of(total, most):
    return [(start, min(most, total - start)) for start in range(0, total, most)]


FF_CHUNK = 768


def hidden_grad_body(rows, down, out, weight, arrived):
    spans = chunks_of(weight.shape[0], FF_CHUNK)
    copies = [
        pltpu.make_async_copy(
            down.at[0, pl.ds(start, size), :], weight.at[pl.ds(start, size), :], arrived.at[place]
        )
        for place, (start, size) in enumerate(spans)
    ]
    for copy in copies:
        copy.start()
    x = rows[...]
    for copy, (start, size) in zip(copies, spans):
        copy.wait()
        out[:, start : start + size] = dot(x, weight[start : start + size, :], COLS).astype(jnp.bfloat16)


def hidden_grad(rows, down_weight):
    count, width = rows.shape
    hidden = down_weight.shape[1]
    return call(
        hidden_grad_body,
        shape((count, hidden)),
        scratch=[
            pltpu.VMEM((hidden, width), jnp.bfloat16),
            pltpu.SemaphoreType.DMA((len(chunks_of(hidden, FF_CHUNK)),)),
        ],
        in_specs=[VMEM, HBM],
        out_specs=VMEM,
        name="hidden_grad",
    )(rows, down_weight)


EXPERT_CHUNK = 256
EXPERT_FIRST = 3
EXPERT_SINGLE = 4
EXPERT_BLOCKS = 10
EXPERT_TILE = 256


def expert_body(width, rows, back, gate_weight, up_weight, hidden, gate_low, up_low, out, gate, up, grads, kept, acts, total, arrived, left):
    spans = chunks_of(gate.shape[1], EXPERT_CHUNK)
    copies = []
    for place, (start, size) in enumerate(spans):
        span = pl.ds(start, size)
        for side, (source, target) in enumerate(
            ((gate_weight.at[0], gate), (up_weight.at[0], up), (back, grads))
        ):
            copies.append(
                pltpu.make_async_copy(source.at[:, span], target.at[:, span], arrived.at[3 * place + side])
            )
    count = len(spans)
    start_all(copies[: 3 * EXPERT_FIRST])
    block = rows.shape[0] // EXPERT_BLOCKS
    choices = [jnp.zeros((block, 1), jnp.float32) for _ in range(EXPERT_BLOCKS)]
    backs = []

    def forward(turn, side, start, size):
        def step():
            weight = (gate, up)[side]
            at = spans[turn][0] + start
            acts[turn % 2, side, :, start : start + size] = dot(rows[:, :width], weight[:, at : at + size])

        return step

    def activate(place, part):
        def step():
            start, size = spans[place]
            span = slice(start, start + size)
            line = slice(part * block, (part + 1) * block)
            act, slope = gelu_parts(acts[place % 2, 0, line, :size])
            up_act = acts[place % 2, 1, line, :size]
            grad = grads[line, span].astype(jnp.float32)
            up_grad = grad * act
            kept[0, line, span] = (act * up_act).astype(jnp.bfloat16)
            kept[1, line, span] = (grad * up_act * slope).astype(jnp.bfloat16)
            kept[2, line, span] = up_grad.astype(jnp.bfloat16)
            choices[part] = choices[part] + jnp.sum(up_grad * up_act, axis=1, keepdims=True)

        return step

    def backward(place, start, size):
        def step():
            first, length = spans[place]
            span = slice(first, first + length)
            columns = slice(start, start + size)
            part = dot(kept[1, :, span], gate[columns, span], COLS) + dot(kept[2, :, span], up[columns, span], COLS)
            if place == 0:
                total[:, columns] = part
            else:
                total[:, columns] += part

        return step

    for turn in range(count + 2):
        products, elementwise = [], []
        if turn < count:
            if turn < EXPERT_SINGLE:
                wait_all(copies[3 * turn : 3 * turn + 3])
            elif turn == EXPERT_SINGLE:
                wait_all(copies[3 * turn :])
            if turn == 0:
                start_all(copies[3 * EXPERT_FIRST :])
            products += [
                forward(turn, side, *piece) for side in range(2) for piece in chunks_of(spans[turn][1], EXPERT_TILE)
            ]
        if 0 < turn <= count:
            elementwise = [activate(turn - 1, part) for part in range(EXPERT_BLOCKS)]
        if turn > 1:
            products += [backward(turn - 2, *piece) for piece in chunks_of(width, EXPERT_TILE)]
        done = 0
        for place, product in enumerate(products):
            product()
            target = len(elementwise) * (place + 1) // len(products)
            for step in elementwise[done:target]:
                step()
            done = target
        for step in elementwise[done:]:
            step()
        if turn > 1:
            place = turn - 2
            start, size = spans[place]
            for which, target in enumerate((hidden, gate_low, up_low)):
                backs.append(
                    pltpu.make_async_copy(
                        kept.at[which, :, pl.ds(start, size)],
                        target.at[:, pl.ds(start, size)],
                        left.at[3 * place + which],
                    )
                )
                backs[-1].start()
    choice = jnp.concatenate(choices, axis=0)
    out[:, :width] = total[...].astype(jnp.bfloat16)
    out[:, width:] = lane_parts(choice)
    for copy in backs:
        copy.wait()


def expert(rows, back, gate_weight, up_weight):
    count = rows.shape[0]
    width, hidden = gate_weight.shape[1:]
    act = shape((count, hidden))
    chunks = len(chunks_of(hidden, EXPERT_CHUNK))
    return call(
        lambda *refs: expert_body(width, *refs),
        [act, act, act, shape(rows.shape)],
        scratch=[
            pltpu.VMEM((width, hidden), jnp.bfloat16),
            pltpu.VMEM((width, hidden), jnp.bfloat16),
            pltpu.VMEM((count, hidden), jnp.bfloat16),
            pltpu.VMEM((3, count, hidden), jnp.bfloat16),
            pltpu.VMEM((2, 2, count, EXPERT_CHUNK), jnp.float32),
            pltpu.VMEM((count, width), jnp.float32),
            pltpu.SemaphoreType.DMA((3 * chunks,)),
            pltpu.SemaphoreType.DMA((3 * chunks,)),
        ],
        in_specs=[VMEM] + [HBM] * 3,
        out_specs=[HBM, HBM, HBM, VMEM],
        name="expert",
    )(rows, back, gate_weight, up_weight)


def expert_out_body(hidden, down, out, acts, weight, total, arrived):
    spans = chunks_of(weight.shape[0], FF_CHUNK)
    copies = []
    for place, (start, size) in enumerate(spans):
        span = pl.ds(start, size)
        copies.append(pltpu.make_async_copy(hidden.at[:, span], acts.at[:, span], arrived.at[2 * place]))
        copies.append(pltpu.make_async_copy(down.at[0, span, :], weight.at[span, :], arrived.at[2 * place + 1]))
    start_all(copies)
    for place, (start, size) in enumerate(spans):
        wait_all(copies[2 * place : 2 * place + 2])
        part = dot(acts[:, start : start + size], weight[start : start + size, :])
        if place == 0:
            total[...] = part
        elif place < len(spans) - 1:
            total[...] += part
        else:
            out[...] = (total[...] + part).astype(jnp.bfloat16)


def expert_out(hidden, down_weight):
    count = hidden.shape[0]
    inner, width = down_weight.shape[1:]
    return call(
        expert_out_body,
        shape((count, width)),
        scratch=[
            pltpu.VMEM((count, inner), jnp.bfloat16),
            pltpu.VMEM((inner, width), jnp.bfloat16),
            pltpu.VMEM((count, width), jnp.float32),
            pltpu.SemaphoreType.DMA((2 * len(chunks_of(inner, FF_CHUNK)),)),
        ],
        in_specs=[HBM] * 2,
        out_specs=VMEM,
        name="expert_out",
    )(hidden, down_weight)


def expert_grads_body(count, width, *refs):
    sources, lefts, sent = refs[:count], refs[count : 2 * count], refs[2 * count]
    targets = refs[2 * count + 1 : 3 * count + 1]
    acts, turned, scaled, staged, arrived, left = refs[3 * count + 1 :]
    spans = chunks_of(sources[0].shape[1], FF_CHUNK)
    steps = [(which, start, size) for which in range(count) for start, size in spans]
    coming = start_all(
        [
            pltpu.make_async_copy(
                sources[which].at[:, pl.ds(start, size)], acts.at[which, :, pl.ds(start, size)], arrived.at[turn]
            )
            for turn, (which, start, size) in enumerate(steps)
        ]
    )
    gate = sum_parts(sent[:, width:])
    for which in range(count):
        scaled[which] = (lefts[which][:, :width].astype(jnp.float32) * gate).astype(jnp.bfloat16)
    backs = []
    for turn in range(len(steps) + 1):
        if turn < len(steps):
            which, start, size = steps[turn]
            coming[turn].wait()
            turned[turn % 2, :size, :] = acts[which, :, start : start + size].T
        if turn > 0:
            which, start, size = steps[turn - 1]
            slot = (turn - 1) % staged.shape[0]
            if turn - 1 >= staged.shape[0]:
                backs[turn - 1 - staged.shape[0]].wait()
            staged[slot, :size, :] = dot(turned[(turn - 1) % 2, :size, :], scaled[which]).astype(jnp.bfloat16)
            backs.append(
                pltpu.make_async_copy(
                    staged.at[slot, pl.ds(0, size), :], targets[which].at[pl.ds(start, size), :], left.at[turn - 1]
                )
            )
            backs[-1].start()
    wait_all(backs[-staged.shape[0] :])


def expert_grads(pairs, sent, width):
    count = len(pairs)
    slots, inner = pairs[0][0].shape
    chunks = len(chunks_of(inner, FF_CHUNK))
    return call(
        lambda *refs: expert_grads_body(count, width, *refs),
        [shape((inner, width))] * count,
        scratch=[
            pltpu.VMEM((count, slots, inner), jnp.bfloat16),
            pltpu.VMEM((2, FF_CHUNK, slots), jnp.bfloat16),
            pltpu.VMEM((count, slots, width), jnp.bfloat16),
            pltpu.VMEM((4, FF_CHUNK, width), jnp.bfloat16),
            pltpu.SemaphoreType.DMA((count * chunks,)),
            pltpu.SemaphoreType.DMA((count * chunks,)),
        ],
        in_specs=[HBM] * count + [VMEM] * (count + 1),
        out_specs=[HBM] * count,
        name="expert_grads",
    )(*[acts for acts, rows in pairs], *[rows for acts, rows in pairs], sent)


def combine_body(returned, columns, gates, middle, block_out):
    length = middle.shape[0]
    slot = iota((length, returned.shape[0]), 1)
    rows = returned[...]
    rows1 = dot(ones_where(slot == columns[:, 0:1]), rows)
    rows2 = dot(ones_where(slot == columns[:, 1:2]), rows)
    block_out[...] = (middle[...] + gates[:, 0:1] * rows1 + gates[:, 1:2] * rows2).astype(jnp.bfloat16)


def combine(returned, columns, gates, middle):
    length, width = middle.shape
    return call(
        combine_body,
        shape((length, width)),
        in_specs=[VMEM] * 4,
        out_specs=VMEM,
        name="combine",
    )(returned, columns, gates, middle)


def router_back(logit, choice, gate1, gate2, picked):
    experts = logit.shape[1]
    top = jnp.max(logit, axis=1, keepdims=True)
    grown = jnp.exp(logit - top)
    total = jnp.sum(grown, axis=1, keepdims=True)
    probs = grown / total
    lse = top + jnp.log(total)
    expert = iota(logit.shape, 1)
    hot1 = ones_where(expert == picked[:, 0:1], jnp.float32)
    hot = hot1 - ones_where(expert == picked[:, 1:2], jnp.float32)
    balance = (BALANCE_COEF * experts) * jnp.mean(hot1, axis=0, keepdims=True)
    even = jnp.sum(probs * balance, axis=1, keepdims=True)
    return hot * (choice * gate1 * gate2) + probs * (balance - even + 2.0 * Z_COEF * lse)


def diagonals(x):
    half = x.shape[0] // 2
    top, low = x[:half], x[half:]
    x = jnp.concatenate([low[:, :half], low[:, half:] + top[:, :half], top[:, half:], jnp.zeros_like(low[:, :half])], axis=1)
    while x.shape[0] > 1:
        half = x.shape[0] // 2
        x = pltpu.roll(x[:half], half, 1) + x[half:]
    return x


def attend_back_body(
    heads, sent_grad, columns, gates, middle, feedforward_gain, cotangent, table_t, line_hot,
    logits, router_t, query, key, value, wo,
    middle_grad, backs, gain_grad, bias_lines, router_grad,
    weight, acts, lines, heads_grad, grad_out, backs_out, arrived, left,
):
    length, width = middle.shape
    size = width // heads
    half = width // 2
    copies = start_all(
        [pltpu.make_async_copy(wo, weight, arrived.at[3])]
        + [
            pltpu.make_async_copy(source, acts.at[place], arrived.at[place])
            for place, source in enumerate((query, key, value))
        ]
    )
    lines[...] = dot(table_t[...], line_hot[1], precision=PRECISE)
    slot = iota((length, sent_grad.shape[0]), 1)
    rows = sent_grad[...]
    rows1 = dot(ones_where(slot == columns[:, 0:1]), rows)
    rows2 = dot(ones_where(slot == columns[:, 1:2]), rows)
    gate1, gate2 = gates[:, 0:1], gates[:, 1:2]
    choice = sum_parts(rows1[:, width:] - rows2[:, width:])
    logit_grad = router_back(logits[...], choice, gate1, gate2, columns[:, 2:4])
    mid = middle[...]
    r = rms(mid)
    scaled = mid * r
    high, rest = split2(scaled * feedforward_gain[...])
    grad_high, grad_rest = split2(logit_grad)
    router_high, router_rest = split2(router_t[...])
    router_grad[...] = dot(grad_high, high, ROWS) + dot(grad_rest, high, ROWS) + dot(grad_high, rest, ROWS)
    normed2_grad = (
        gate1 * rows1[:, :width]
        + gate2 * rows2[:, :width]
        + (dot(grad_high, router_high) + dot(grad_rest, router_high) + dot(grad_high, router_rest))
    )
    u = normed2_grad * feedforward_gain[...]
    gain_grad[...] = jnp.sum(normed2_grad * scaled, axis=0, keepdims=True)
    grad = (
        cotangent[...].astype(jnp.float32)
        + r * u
        - mid * (r * r * r * jnp.mean(u * mid, axis=1, keepdims=True))
    )
    grad_out[...] = grad
    grad_copy = pltpu.make_async_copy(grad_out, middle_grad, left.at[2])
    grad_copy.start()
    low = grad.astype(jnp.bfloat16)
    wait_all(copies)
    heads_grad[...] = dot(low, weight[...], COLS).astype(jnp.bfloat16)
    backs_out[:, 3 * width :] = low
    pair_width = 2 * size
    first = iota((length, pair_width), 1) < size
    first_t = iota((pair_width, length), 0) < size
    zero = jnp.zeros((length, pair_width), jnp.bfloat16)
    scale = jnp.bfloat16(1.0 / math.sqrt(size))
    for pair in range(heads // 2):
        start = pair * pair_width
        span = slice(start, start + pair_width)
        q, k, v, g = acts[0, :, span] * scale, acts[1, :, span], acts[2, :, span], heads_grad[:, span]
        k_turned = (k * scale).T
        kept = []
        for side in range(2):
            q_side = jnp.where(first, q, zero) if side == 0 else jnp.where(first, zero, q)
            g_side = jnp.where(first, g, zero) if side == 0 else jnp.where(first, zero, g)
            head = 2 * pair + side
            line = jnp.broadcast_to(lines[head : head + 1, :], (length, 2 * length))
            bias = pltpu.roll(line, length + 1, 1, stride=1, stride_axis=0)[:, :length]
            scores = dot(k, q_side, COLS) + bias
            top = jnp.max(scores, axis=0, keepdims=True)
            grown = jnp.exp(scores - top)
            probs = grown * (1.0 / jnp.sum(grown, axis=0, keepdims=True))
            probs_grad = dot(v, g_side, COLS)
            score_grad = probs * (probs_grad - jnp.sum(probs * probs_grad, axis=0, keepdims=True))
            score_low = score_grad.astype(jnp.bfloat16)
            bias_lines[head : head + 1, :] = diagonals(score_low.astype(jnp.float32))
            kept.append(
                (
                    dot(k_turned, score_low),
                    dot(score_low, q),
                    dot(probs.astype(jnp.bfloat16), g),
                )
            )
        results = (
            jnp.where(first_t, kept[0][0], kept[1][0]).astype(jnp.bfloat16).T,
            jnp.where(first, kept[0][1], kept[1][1]).astype(jnp.bfloat16),
            jnp.where(first, kept[0][2], kept[1][2]).astype(jnp.bfloat16),
        )
        for place, result in enumerate(results):
            backs_out[:, place * width + start : place * width + start + pair_width] = result
    leaving = pltpu.make_async_copy(backs_out, backs, left.at[0])
    leaving.start()
    leaving.wait()
    grad_copy.wait()


def attend_back(heads, line_hot, sent_grad, columns, gates, middle, feedforward_gain, cotangent, table_t, logits, router_t, query, key, value, wo):
    length, width = middle.shape
    return call(
        lambda *refs: attend_back_body(heads, *refs),
        [
            shape((length, width), jnp.float32),
            shape((length, 4 * width)),
            shape((1, width), jnp.float32),
            shape((heads, 2 * length), jnp.float32),
            shape(router_t.shape, jnp.float32),
        ],
        scratch=[
            pltpu.VMEM((width, width), jnp.bfloat16),
            pltpu.VMEM((3, length, width), jnp.bfloat16),
            pltpu.VMEM((heads, 2 * length), jnp.float32),
            pltpu.VMEM((length, width), jnp.bfloat16),
            pltpu.VMEM((length, width), jnp.float32),
            pltpu.VMEM((length, 4 * width), jnp.bfloat16),
            pltpu.SemaphoreType.DMA((4,)),
            pltpu.SemaphoreType.DMA((3,)),
        ],
        in_specs=[VMEM] * 10 + [HBM] * 4,
        out_specs=[HBM] * 2 + [VMEM] * 3,
        name="attend_back",
    )(sent_grad, columns, gates, middle, feedforward_gain, cotangent, table_t, line_hot, logits, router_t, query, key, value, wo)


def input_back_body(backs_in, grad_in, tokens, attention_gain, bias_lines, line_hot, wq, wk, wv, input_grad, vectors, weights, backs, middle_grad, arrived):
    length, width = tokens.shape
    copies = []
    for place, source in enumerate((wq, wk, wv)):
        span = pl.ds(place * width, width)
        copies.append(pltpu.make_async_copy(backs_in.at[:, span], backs.at[:, span], arrived.at[place]))
        copies.append(pltpu.make_async_copy(source, weights.at[place], arrived.at[3 + place]))
    copies.append(pltpu.make_async_copy(grad_in, middle_grad, arrived.at[6]))
    start_all(copies)
    bias = dot(bias_lines[...], line_hot[1], COLS, PRECISE)
    rows = bias.shape[0] // 4
    bias = jnp.concatenate([bias[rows * part : rows * (part + 1)] for part in range(4)], axis=1)
    x = tokens[...].astype(jnp.float32)
    s = rms(x)
    total = jnp.zeros((length, width), jnp.float32)
    for place in range(3):
        wait_all(copies[2 * place : 2 * place + 2])
        total = total + dot(backs[:, place * width : (place + 1) * width], weights[place], COLS)
    w = total * attention_gain[...]
    gain = jnp.sum(total * x * s, axis=0, keepdims=True)
    vectors[...] = jnp.zeros_like(vectors)
    for part in range(width // LANES):
        vectors[part : part + 1, :] = gain[:, part * LANES : (part + 1) * LANES]
    vectors[width // LANES : width // LANES + rows, :] = bias
    copies[6].wait()
    input_grad[...] = middle_grad[...] + s * w - x * (s * s * s * jnp.mean(w * x, axis=1, keepdims=True))


def input_back(line_hot, backs, middle_grad, tokens, attention_gain, bias_lines, wq, wk, wv):
    length, width = tokens.shape
    return call(
        input_back_body,
        [
            shape((length, width), jnp.float32),
            shape((BLOCK, LANES), jnp.float32),
        ],
        scratch=[
            pltpu.VMEM((3, width, width), jnp.bfloat16),
            pltpu.VMEM((length, 3 * width), jnp.bfloat16),
            pltpu.VMEM((length, width), jnp.float32),
            pltpu.SemaphoreType.DMA((7,)),
        ],
        in_specs=[HBM] * 2 + [VMEM] * 4 + [HBM] * 3,
        out_specs=[VMEM] * 2,
        name="input_back",
    )(backs, middle_grad, tokens, attention_gain, bias_lines, line_hot, wq, wk, wv)


EXTRA = 2 * LANES


def resplit(lanes):
    half = LANES // 2
    total = lanes + pltpu.roll(lanes, half, 1)
    high = total.astype(jnp.bfloat16).astype(jnp.float32)
    return jnp.where(iota(lanes.shape, 1) < half, high, total - high)


def rotated(place, side, block, step):
    return pl.ds(pl.multiple_of(((place + step) % side) * block, block), block)


def products_body(side, where, normed, heads_out, left_far, backs_in, far_in, feedforward_gain, router, *rest):
    pieces, (lefts, backs, payload, vectors, arrived, left) = rest[:side], rest[side:]
    length, width = normed.shape
    half = width // 2
    mine = pl.ds(pl.multiple_of(where[0] * half, half), half)
    copies = start_all(
        [
            pltpu.make_async_copy(normed.at[:, mine], lefts.at[0, :, pl.ds(0, half)], arrived.at[0]),
            pltpu.make_async_copy(heads_out.at[:, mine], lefts.at[0, :, pl.ds(half, half)], arrived.at[1]),
            pltpu.make_async_copy(left_far, lefts.at[1], arrived.at[2]),
        ]
        + [
            pltpu.make_async_copy(
                source.at[:, pl.ds(place * width, width)],
                backs.at[which, :, pl.ds(place * width, width)],
                arrived.at[3 + 2 * place + which],
            )
            for place in range(4)
            for which, source in enumerate((backs_in, far_in))
        ]
    )
    experts = router.shape[0]
    vectors[...] = jnp.zeros_like(vectors)
    vectors[0:1, :] = feedforward_gain[...]
    vectors[8 : 8 + experts, :] = router[...]
    for place in range(2):
        start = 4 * width + place * LANES
        payload[:, start : start + LANES] = resplit(vectors[:, place * half : (place + 1) * half].T).astype(jnp.bfloat16)
    position = where[2 + where[0]]
    leaving = []

    def leave(part, start, size):
        for step, piece in enumerate(pieces):
            leaving.append(
                pltpu.make_async_copy(
                    payload.at[rotated(position, side, half // side, step), pl.ds(start, size)],
                    piece.at[:, pl.ds(start, size)],
                    left.at[part * side + step],
                )
            )
            leaving[-1].start()

    leave(4, 4 * width, EXTRA)
    wait_all(copies[:3])
    for place in range(4):
        wait_all(copies[3 + 2 * place : 5 + 2 * place])
        span = slice(place * width, (place + 1) * width)
        start = 0 if place < 3 else half
        payload[:, span] = (
            dot(lefts[0, :, start : start + half], backs[0, :, span], ROWS)
            + dot(lefts[1, :, start : start + half], backs[1, :, span], ROWS)
        ).astype(jnp.bfloat16)
        leave(place, place * width, width)
    wait_all(leaving)


def products(where, side, normed, heads_out, left_far, backs, backs_far, feedforward_gain, router):
    length, width = normed.shape
    wide = 4 * width + EXTRA
    return call(
        lambda *refs: products_body(side, *refs),
        [shape((width // 2 // side, wide))] * side,
        scratch=[
            pltpu.VMEM((2, length, width), jnp.bfloat16),
            pltpu.VMEM((2, length, 4 * width), jnp.bfloat16),
            pltpu.VMEM((width // 2, wide), jnp.bfloat16),
            pltpu.VMEM((LANES, width), jnp.float32),
            pltpu.SemaphoreType.DMA((11,)),
            pltpu.SemaphoreType.DMA((5 * side,)),
        ],
        in_specs=[SMEM] + [HBM] * 5 + [VMEM] * 2,
        out_specs=[HBM] * side,
        name="products",
    )(where, normed, heads_out, left_far, backs, backs_far, feedforward_gain, router)


def total_into(out, refs, late):
    total = refs[0][...].astype(jnp.float32)
    for ref in refs[1:]:
        total = total + ref[...].astype(jnp.float32)
    wide = total.shape[1] - EXTRA - (LANES if late else 0)
    out[:, :wide] = total[:, :wide].astype(jnp.bfloat16)
    for start in range(wide, wide + EXTRA, LANES):
        out[:, start : start + LANES] = resplit(total[:, start : start + LANES]).astype(jnp.bfloat16)
    if late:
        out[:, wide + EXTRA :] = stack_parts(total[:BLOCK, wide + EXTRA :] + total[BLOCK:, wide + EXTRA :])


def stack_parts(block):
    return jnp.concatenate(split2(block), axis=0)


def fold_body(side, where, vectors, *refs):
    pieces, outs, total = refs[:side], refs[side : 2 * side], refs[-1]
    total_into(total, pieces, False)
    position = where[3 - where[0]]
    wide = total.shape[1]
    late = stack_parts(vectors[...])
    for step, out in enumerate(outs):
        out[:, :wide] = total[rotated(position, side, out.shape[0], step), :]
        out[:, wide:] = late


def fold(where, side, vectors, pieces):
    rows, wide = pieces[0].shape
    return call(
        lambda *refs: fold_body(side, *refs),
        [shape((rows // side, wide + LANES))] * side,
        scratch=[pltpu.VMEM((rows, wide), jnp.bfloat16)],
        in_specs=[SMEM] + [VMEM] * (side + 1),
        out_specs=[VMEM] * side,
        vmem=16,
        name="fold",
    )(where, vectors, *pieces)


def add_pieces(pieces):
    return call(
        lambda *refs: total_into(refs[-1], refs[:-1], True),
        shape(pieces[0].shape),
        in_specs=[VMEM] * len(pieces),
        out_specs=VMEM,
        vmem=12,
        name="add_pieces",
    )(*pieces)


def put_body(side, where, *refs):
    pieces, (whole, upper, lower) = refs[:side], refs[side:]
    position = where[3 - where[0]]
    rows = upper.shape[0]
    for step in range(side):
        whole[rotated(position, side, pieces[0].shape[0], step), :] = pieces[step][...]
    upper[...] = whole[:rows, :]
    lower[...] = whole[rows:, :]


def put(where, side, pieces):
    rows, wide = pieces[0].shape
    half = shape((side * rows // 2, wide))
    return call(
        lambda *refs: put_body(side, *refs),
        [shape((side * rows, wide)), half, half],
        in_specs=[SMEM] + [VMEM] * side,
        out_specs=[VMEM] * 3,
        vmem=24,
        name="put",
    )(where, *pieces)


def again_body(whole, upper, lower):
    rows = upper.shape[0]
    upper[...] = whole[:rows, :]
    lower[...] = whole[rows:, :]


def again(whole):
    half = shape((whole.shape[0] // 2, whole.shape[1]))
    return call(again_body, [half, half], in_specs=[VMEM], out_specs=[VMEM] * 2, vmem=24, name="again")(whole)


def begin_body(side, where, near, far, *refs):
    outs, (held, staged, arrived, left) = refs[:4], refs[4:]
    rows, width = staged.shape[2:]
    copies = start_all(
        [
            pltpu.make_async_copy(source.at[:, pl.ds(0, 4 * width)], held.at[which], arrived.at[which])
            for which, source in enumerate((near, far))
        ]
    )
    backs = []
    for which in range(2):
        core = where[0] if which == 0 else 1 - where[0]
        copies[which].wait()
        line = pl.ds(pl.multiple_of(core * (width // 2) + where[2 + core] * rows, rows), rows)
        for matrix in range(4):
            staged[which, matrix] = held[which, :, matrix * width : (matrix + 1) * width].astype(jnp.float32)
            backs.append(
                pltpu.make_async_copy(staged.at[which, matrix], outs[matrix].at[line, :], left.at[4 * which + matrix])
            )
            backs[-1].start()
    wait_all(backs)


def begin(where, side, near, far):
    rows, wide = near.shape
    width = (wide - EXTRA - LANES) // 4
    return call(
        lambda *refs: begin_body(side, *refs),
        [shape((width, width), jnp.float32)] * 4,
        scratch=[
            pltpu.VMEM((2, rows, 4 * width), jnp.bfloat16),
            pltpu.VMEM((2, 4, rows, width), jnp.float32),
            pltpu.SemaphoreType.DMA((2,)),
            pltpu.SemaphoreType.DMA((8,)),
        ],
        in_specs=[SMEM] + [HBM] * 2,
        out_specs=[HBM] * 4,
        name="begin",
    )(where, near, far)


def finish_body(side, steps, where, *refs):
    parts = sum(len(order) for step, order in steps)
    pieces, refs = (refs[:parts], refs[parts : 2 * parts]), refs[2 * parts :]
    up_low, outs, refs = refs[0], refs[5:9], refs[9:]
    up_out, gain, feedforward_gain, router_t, bias_t, held, staged, up_held, up_staged, late, arrived, left = refs
    rows = staged.shape[2]
    width = staged.shape[3]
    half = width // 2
    wide = held.shape[3]
    copies = []
    for which in range(2):
        place = 0
        for block, (step, order) in enumerate(steps):
            size = rows // len(order)
            columns = pl.ds(0 if step else 4 * width, wide if step else wide - 4 * width)
            copies.append(
                start_all(
                    [
                        pltpu.make_async_copy(
                            pieces[which][place + part].at[:, columns],
                            held.at[which, block, pl.ds(order[part] * size, size), columns],
                            arrived.at[which * parts + place + part],
                        )
                        for part in range(len(order))
                    ]
                )
            )
            place += len(order)
    up_copy = pltpu.make_async_copy(up_low, up_held, arrived.at[2 * parts])
    up_copy.start()
    for vector in (feedforward_gain, router_t, late):
        vector[...] = jnp.zeros_like(vector)
    backs = []
    for block, (step, order) in enumerate(steps):
        for which in range(2):
            core = where[0] if which == 0 else 1 - where[0]
            slot = which * len(steps) + block
            wait_all(copies[slot])
            start = pl.multiple_of(((where[2 + core] + step) % side) * rows, rows)
            line = pl.ds(pl.multiple_of(core * half + start, rows), rows)
            for matrix in range(4 if step else 0):
                staged[slot, matrix] = held[which, block, :, matrix * width : (matrix + 1) * width].astype(jnp.float32)
                backs.append(
                    pltpu.make_async_copy(
                        staged.at[slot, matrix], outs[matrix].at[line, :], left.at[4 * slot + matrix]
                    )
                )
                backs[-1].start()
            for place in range(2):
                lanes = held[which, block, :, 4 * width + place * LANES : 4 * width + (place + 1) * LANES]
                lanes = lanes.astype(jnp.float32)
                turned = (lanes + pltpu.roll(lanes, LANES // 2, 1)).T
                line = pl.ds(pl.multiple_of(place * half + start, rows), rows)
                feedforward_gain[:, line] += turned[0:1]
                router_t[:, line] += turned[8 : 8 + router_t.shape[0]]
            block_rows = held[which, block, : 2 * BLOCK, 4 * width + EXTRA :].astype(jnp.float32)
            late[...] += block_rows[:BLOCK] + block_rows[BLOCK:]
    up_copy.wait()
    up_staged[...] = up_held[...].astype(jnp.float32)
    backs.append(pltpu.make_async_copy(up_staged, up_out, left.at[8 * len(steps)]))
    backs[-1].start()
    lines = width // LANES
    for part in range(lines):
        gain[:, part * LANES : (part + 1) * LANES] = late[part : part + 1, :]
    heads, buckets = bias_t.shape
    for part in range(4):
        bias_t[part * heads // 4 : (part + 1) * heads // 4, :] = late[
            lines : lines + heads // 4, part * buckets : (part + 1) * buckets
        ]
    wait_all(backs)


def finish(where, side, steps, near, far, up_low, begun, experts, buckets, heads):
    wide = near[0].shape[1]
    width = (wide - EXTRA - LANES) // 4
    rows = width // 2 // side
    count, parts = len(steps), len(near)
    return call(
        lambda *refs: finish_body(side, steps, *refs),
        [shape((width, width), jnp.float32)] * 4
        + [
            shape(up_low.shape, jnp.float32),
            shape((1, width), jnp.float32),
            shape((1, width), jnp.float32),
            shape((experts, width), jnp.float32),
            shape((heads, buckets), jnp.float32),
        ],
        scratch=[
            pltpu.VMEM((2, count, rows, wide), jnp.bfloat16),
            pltpu.VMEM((2 * count, 4, rows, width), jnp.float32),
            pltpu.VMEM(up_low.shape, jnp.bfloat16),
            pltpu.VMEM(up_low.shape, jnp.float32),
            pltpu.VMEM((BLOCK, LANES), jnp.float32),
            pltpu.SemaphoreType.DMA((2 * parts + 1,)),
            pltpu.SemaphoreType.DMA((8 * count + 1,)),
        ],
        in_specs=[SMEM] + [HBM] * (2 * parts + 5),
        out_specs=[HBM] * 5 + [VMEM] * 4,
        input_output_aliases={2 * parts + 2 + matrix: matrix for matrix in range(4)},
        name="finish",
    )(where, *near, *far, up_low, *begun)


def rotate_x(count, step):
    return [(x * 2 + c, ((x + step) % count) * 2 + c) for x in range(count) for c in range(2)]


def rotate_plane(chips, side, flip, step):
    pairs = []
    for x in range(chips):
        for core in range(2):
            for z in range(side):
                for y in range(side):
                    along_z = core ^ flip
                    to = ((z + step) % side, y) if along_z else (z, (y + step) % side)
                    base = (x * 2 + core) * side * side
                    pairs.append((base + z * side + y, base + to[0] * side + to[1]))
    return pairs


def swap_cores(count):
    return [(x * 2 + c, x * 2 + 1 - c) for x in range(count) for c in range(2)]


def shards(
    tokens,
    routes,
    cotangent,
    attention_gain,
    query_weight,
    key_weight,
    value_weight,
    output_weight,
    bias_table,
    feedforward_gain,
    router_weight,
    gate_weight,
    up_weight,
    down_weight,
):
    length, width = tokens.shape
    buckets, heads = bias_table.shape
    experts = lax.axis_size("expert")
    chips = lax.axis_size("dp") // 2
    side = math.isqrt(experts)
    replica, expert_place = lax.axis_index("dp"), lax.axis_index("expert")
    where = jnp.stack([replica % 2, replica // 2, expert_place % side, expert_place // side])
    capacity = max(2, (10 * length + 4 * experts - 1) // (4 * experts))
    swap = swap_cores(chips)
    line_hot = jnp.asarray(bucket_lines(length, buckets))
    gain1, gain2 = attention_gain[None], feedforward_gain[None]

    def exchange(rows):
        return lax.all_to_all(
            rows.reshape(experts, capacity, -1), "expert", split_axis=0, concat_axis=0, tiled=True
        ).reshape(experts * capacity, -1)

    table_t, router_t = bias_table.T, router_weight.T
    slots_t, columns, cot_slots = route(routes, cotangent, experts, capacity)
    cot_rows = exchange(cot_slots)
    normed, query, key, value, heads_out, left, middle, logits, gates, sent = attend(
        heads, experts * capacity, where, line_hot, tokens, gain1, gain2, table_t, router_t, columns, slots_t,
        (query_weight, key_weight, value_weight, output_weight),
    )

    def swapped(array):
        return lax.ppermute(array, "dp", swap)

    rows = exchange(sent)
    left_far = swapped(left)
    back = hidden_grad(cot_rows, down_weight)
    rows, left_far = lax.optimization_barrier((rows, left_far))
    hidden, gate_low, up_acts, rows_grad = expert(rows, back, gate_weight, up_weight)
    sent_grad = exchange(rows_grad)

    def scatter_dp(part):
        return lax.psum_scatter(part, "dp", scatter_dimension=0, tiled=True)

    grads = expert_grads(((hidden, cot_rows), (gate_low, rows)), rows, width)
    sent_grad, grads = lax.optimization_barrier((sent_grad, grads))
    down_grad, gate_grad = scatter_dp(grads[0]), scatter_dp(grads[1])

    middle_grad, backs, gain2_part, bias_lines, router_part = attend_back(
        heads, line_hot, sent_grad, columns, gates, middle, gain2, cotangent, table_t, logits,
        router_t, query, key, value, output_weight,
    )
    backs_far = swapped(backs)
    pieces = products(where, side, normed, heads_out, left_far, backs, backs_far, gain2_part, router_part)

    def turn(piece, flip, step):
        return lax.ppermute(piece, ("dp", "expert"), rotate_plane(chips, side, flip, step))

    def scatter_plane(pieces, flip):
        return [pieces[0]] + [turn(pieces[step], flip, step) for step in range(1, side)]

    pieces, hidden, backs = lax.optimization_barrier((pieces, hidden, backs))
    folded_in = scatter_plane(pieces, 0)
    input_grad, vectors = input_back(
        line_hot, backs, middle_grad, tokens, gain1, bias_lines, query_weight, key_weight, value_weight
    )
    returned = expert_out(hidden, down_weight)
    down_grad = down_grad.astype(jnp.float32)
    folded_in, vectors, returned, down_grad = lax.optimization_barrier((folded_in, vectors, returned, down_grad))
    shard = add_pieces(scatter_plane(fold(where, side, vectors, folded_in), 1))
    shard, returned, up_acts = lax.optimization_barrier((shard, returned, up_acts))
    returned = exchange(returned)
    (up_part,) = expert_grads(((up_acts, rows),), rows, width)
    total = add_pieces([shard] + [lax.ppermute(shard, "dp", rotate_x(chips, step)) for step in range(1, chips)])
    total, up_part, returned = lax.optimization_barrier((total, up_part, returned))
    up_low = scatter_dp(up_part)
    gathered = [total] + [turn(total, 1, -step) for step in range(1, side)]
    gate_grad = gate_grad.astype(jnp.float32)
    block_out = combine(returned, columns, gates, middle)
    gathered, gate_grad, block_out = lax.optimization_barrier((gathered, gate_grad, block_out))
    own, upper, lower = put(where, side, gathered)
    minus_upper, plus_lower = turn(upper, 0, 1), turn(lower, 0, -1)
    upper2, lower2 = again(own)
    minus_lower, plus_upper = turn(lower2, 0, 1), turn(upper2, 0, -1)
    own_far = swapped(own)
    plus_lower, begun = lax.optimization_barrier((plus_lower, begin(where, side, own, own_far)))
    across = [turn(minus_upper, 0, 1), turn(plus_lower, 0, -1)]
    near = [plus_lower, plus_upper, minus_lower, minus_upper, *across]
    far = [own_far, *[swapped(piece) for piece in near]]
    near = [own, *near]
    query_grad, key_grad, value_grad, output_grad, up_grad, gain1_grad, gain2_grad, router_grad_t, bias_grad_t = finish(
        where, side, ((0, (0,)), (1, (1, 0)), (3, (1, 0)), (2, (0, 1))), near, far, up_low, begun, experts, buckets, heads
    )
    return (
        block_out,
        input_grad,
        gain1_grad[0],
        query_grad,
        key_grad,
        value_grad,
        output_grad,
        bias_grad_t.T,
        gain2_grad[0],
        router_grad_t.T,
        gate_grad.T[None],
        up_grad.T[None],
        down_grad[None],
    )


def solution(mesh):
    return jax.shard_map(
        shards,
        mesh=mesh,
        in_specs=(
            P(("dp", "expert"), None),
            P(("dp", "expert"), None),
            P(("dp", "expert"), None),
            P(),
            P(),
            P(),
            P(),
            P(),
            P(),
            P(),
            P(),
            P("expert", None, None),
            P("expert", None, None),
            P("expert", None, None),
        ),
        out_specs=(
            P(("dp", "expert"), None),
            P(("dp", "expert"), None),
            P(),
            P(),
            P(),
            P(),
            P(),
            P(),
            P(),
            P(),
            P("expert", None, "dp"),
            P("expert", None, "dp"),
            P("expert", "dp", None),
        ),
        check_vma=False,
    )
```

```python
import math

import jax
import jax.numpy as jnp
import numpy as np
from jax import lax
from jax.experimental import pallas as pl
from jax.experimental.pallas import tpu as pltpu
from jax.sharding import PartitionSpec as P

EPSILON = 1e-06
Z_COEF = 0.001
BALANCE_COEF = 0.01
PRECISE = lax.Precision.HIGHEST
LANES = 128
BLOCK = 16
MIB = 1024 * 1024
VMEM = pl.BlockSpec(memory_space=pltpu.VMEM)
HBM = pl.BlockSpec(memory_space=pl.ANY)
SMEM = pl.BlockSpec(memory_space=pltpu.SMEM)


def bucket_table(length, bucket_count):
    half_count = bucket_count // 2
    exact_count = half_count // 2
    position = np.arange(length)
    relative = position[None, :] - position[:, None]
    distance = np.abs(relative)
    spread = (
        np.log(np.maximum(distance, 1) / exact_count)
        / np.log(128.0 / exact_count)
        * (half_count - exact_count)
    )
    far_bucket = np.minimum(
        exact_count + np.floor(np.maximum(spread, 0.0)).astype(np.int32), half_count - 1
    )
    bucket_index = np.where(distance < exact_count, distance, far_bucket)
    return (bucket_index + (relative > 0) * half_count).astype(np.int32)


def bucket_lines(length, bucket_count):
    table = bucket_table(length, bucket_count)
    line = np.concatenate([table[::-1, 0], table[0, 1:]])
    hot = np.zeros((2, bucket_count, 2 * length), np.float32)
    for place, bucket in enumerate(line):
        hot[0, bucket, place] = 1.0
        hot[1, bucket, 2 * length - 2 - place] = 1.0
    return hot


def dot(left, right, dims=((1,), (0,)), precision=None):
    return lax.dot_general(
        left, right, (dims, ((), ())), precision=precision, preferred_element_type=jnp.float32
    )


ROWS = ((0,), (0,))
COLS = ((1,), (1,))


def iota(shape, axis):
    return lax.broadcasted_iota(jnp.int32, shape, axis)


def ones_where(condition, dtype=jnp.bfloat16):
    return jnp.where(condition, 1.0, 0.0).astype(dtype)


def call(body, outs, scratch=(), vmem=63, flops=1024, **options):
    return pl.pallas_call(
        body,
        out_shape=outs,
        scratch_shapes=list(scratch),
        compiler_params=pltpu.CompilerParams(vmem_limit_bytes=vmem * MIB),
        cost_estimate=pl.CostEstimate(flops=flops, bytes_accessed=1024, transcendentals=0),
        **options,
    )


class Place:
    def __init__(self, side):
        replica, expert = lax.axis_index("dp"), lax.axis_index("expert")
        self.parts = (replica % 2, replica // 2, expert % side, expert // side)

    def __getitem__(self, which):
        if isinstance(which, int):
            return self.parts[which]
        return jnp.where(which == 2, self.parts[2], self.parts[3])


def shape(dims, dtype=jnp.bfloat16):
    return jax.ShapeDtypeStruct(dims, dtype)


def route_body(capacity, experts, routes_t, cotangent, slots_t, columns, cot_slots):
    length = cotangent.shape[0]
    before = ones_where(iota((length, length), 0) < iota((length, length), 1))
    picked = routes_t[...]
    expert = iota((experts, length), 0)
    hot1 = ones_where(expert == picked[0:1], jnp.float32)
    hot2 = ones_where(expert == picked[1:2], jnp.float32)
    filled = jnp.sum(hot1, axis=1, keepdims=True)
    number1 = dot(hot1.astype(jnp.bfloat16), before)
    number2 = dot(hot2.astype(jnp.bfloat16), before) + filled
    place1 = jnp.sum(number1 * hot1, axis=0, keepdims=True).astype(jnp.int32)
    place2 = jnp.sum(number2 * hot2, axis=0, keepdims=True).astype(jnp.int32)
    slot1 = jnp.where(place1 < capacity, picked[0:1] * capacity + place1, -1)
    slot2 = jnp.where(place2 < capacity, picked[1:2] * capacity + place2, -1)
    slots_t[0:1] = slot1
    slots_t[1:2] = slot2
    lines = jnp.concatenate([slot1, slot2, picked, jnp.zeros((4, length), jnp.int32)], axis=0)
    columns[...] = lines.T
    slot = iota((experts * capacity, length), 0)
    dispatch = ones_where((slot == slot1) | (slot == slot2))
    cot_slots[...] = dot(dispatch, cotangent[...]).astype(jnp.bfloat16)


def route(routes, cotangent, experts, capacity):
    length, width = cotangent.shape
    return call(
        lambda *refs: route_body(capacity, experts, *refs),
        [
            shape((2, length), jnp.int32),
            shape((length, 8), jnp.int32),
            shape((experts * capacity, width)),
        ],
        in_specs=[VMEM] * 2,
        out_specs=[VMEM] * 3,
        name="route",
    )(routes.T, cotangent)


def start_all(copies):
    for copy in copies:
        copy.start()
    return copies


def wait_all(copies):
    for copy in copies:
        copy.wait()


def split2(x):
    high = x.astype(jnp.bfloat16)
    return high, (x - high.astype(jnp.float32)).astype(jnp.bfloat16)


def rms(x):
    return lax.rsqrt(jnp.mean(x * x, axis=1, keepdims=True) + EPSILON)


def split3(x):
    high = x.astype(jnp.bfloat16)
    rest = x - high.astype(jnp.float32)
    mid = rest.astype(jnp.bfloat16)
    return high, mid, (rest - mid.astype(jnp.float32)).astype(jnp.bfloat16)


def lane_parts(column):
    lane = iota((column.shape[0], LANES), 1)
    spread = jnp.zeros(lane.shape, jnp.float32)
    for place, part in enumerate(split3(column)):
        spread = jnp.where(lane == place, part.astype(jnp.float32), spread)
    return spread.astype(jnp.bfloat16)


def sum_parts(lanes):
    parts = lanes.astype(jnp.float32)
    return parts[:, 0:1] + parts[:, 1:2] + parts[:, 2:3]


def attend_body(
    heads, where, tokens, attention_gain, feedforward_gain, table_t, line_hot, router_t, columns, slots_t,
    wq, wk, wv, wo,
    normed_out, query_out, key_out, value_out, heads_done, left_send, middle, logits, gates, sent,
    weights, lines, acts, arrived, left,
):
    length, width = tokens.shape
    size = width // heads
    copies = [
        pltpu.make_async_copy(source, weights.at[place], arrived.at[place])
        for place, source in enumerate((wq, wk, wv, wo))
    ]
    start_all(copies[:3])
    backs = [
        pltpu.make_async_copy(acts.at[place], target, left.at[place])
        for place, target in enumerate((normed_out, query_out, key_out, value_out, heads_done))
    ]
    lines[...] = dot(table_t[...], line_hot[0], precision=PRECISE)
    wait_all(copies[:3])
    copies[3].start()
    x = tokens[...].astype(jnp.float32)
    low = (x * rms(x) * attention_gain[...]).astype(jnp.bfloat16)
    acts[0] = low
    backs[0].start()
    for place in range(3):
        acts[place + 1] = dot(acts[0], weights[place]).astype(jnp.bfloat16)
        backs[place + 1].start()
    first = iota((length, 2 * size), 1) < size
    zero = jnp.zeros((length, 2 * size), jnp.bfloat16)
    scale = 1.0 / math.sqrt(size)
    for pair in range(heads // 2):
        span = slice(pair * 2 * size, (pair + 1) * 2 * size)
        q, k, v = acts[1, :, span] * jnp.bfloat16(scale), acts[2, :, span], acts[3, :, span]
        outs = []
        for side in range(2):
            q_side = jnp.where(first, q, zero) if side == 0 else jnp.where(first, zero, q)
            head = 2 * pair + side
            line = jnp.broadcast_to(lines[head : head + 1, :], (length, 2 * length))
            bias = pltpu.roll(line, length + 1, 1, stride=1, stride_axis=0)[:, :length]
            scores = dot(q_side, k, COLS) + bias
            top = jnp.max(scores, axis=1, keepdims=True)
            grown = jnp.exp(scores - top)
            total = jnp.sum(grown, axis=1, keepdims=True)
            outs.append(dot((grown * (1.0 / total)).astype(jnp.bfloat16), v))
        acts[4, :, span] = jnp.where(first, outs[0], outs[1]).astype(jnp.bfloat16)
    backs[4].start()
    half = width // 2
    other = pl.ds(pl.multiple_of((1 - where[0]) * half, half), half)
    left_send[:, :half] = acts[0, :, other]
    left_send[:, half:] = acts[4, :, other]
    copies[3].wait()
    mid = x + dot(acts[4], weights[3])
    middle[...] = mid
    normed2 = mid * rms(mid) * feedforward_gain[...]
    high, rest = split2(normed2)
    experts = router_t.shape[0]
    router_high, router_rest = split2(router_t[...])
    logit = dot(high, router_high, COLS) + dot(high, router_rest, COLS) + dot(rest, router_high, COLS)
    logits[...] = logit
    picked = columns[:, 2:4]
    expert = iota(logit.shape, 1)
    logit1 = jnp.sum(jnp.where(expert == picked[:, 0:1], logit, 0.0), axis=1, keepdims=True)
    logit2 = jnp.sum(jnp.where(expert == picked[:, 1:2], logit, 0.0), axis=1, keepdims=True)
    gate1 = 1.0 / (1.0 + jnp.exp(logit2 - logit1))
    gate2 = 1.0 / (1.0 + jnp.exp(logit1 - logit2))
    gates[:, 0:1] = gate1
    gates[:, 1:2] = gate2
    slot = iota((sent.shape[0], length), 0)
    hot1 = ones_where(slot == slots_t[0:1])
    hot2 = ones_where(slot == slots_t[1:2])
    sent[:, :width] = dot(hot1 + hot2, high).astype(jnp.bfloat16)
    sent[:, width:] = (dot(hot1, lane_parts(gate1)) + dot(hot2, lane_parts(gate2))).astype(jnp.bfloat16)
    wait_all(backs)


def attend(heads, slot_count, side, line_hot, tokens, attention_gain, feedforward_gain, table_t, router_t, columns, slots_t, weights):
    length, width = tokens.shape
    experts = router_t.shape[0]
    act = shape((length, width))
    return call(
        lambda *refs: attend_body(heads, Place(side), *refs),
        [
            act, act, act, act, act, act,
            shape((length, width), jnp.float32),
            shape((length, experts), jnp.float32),
            shape((length, 2), jnp.float32),
            shape((slot_count, width + LANES)),
        ],
        scratch=[
            pltpu.VMEM((4, width, width), jnp.bfloat16),
            pltpu.VMEM((heads, 2 * length), jnp.float32),
            pltpu.VMEM((5, length, width), jnp.bfloat16),
            pltpu.SemaphoreType.DMA((4,)),
            pltpu.SemaphoreType.DMA((5,)),
        ],
        in_specs=[VMEM] * 8 + [HBM] * 4,
        out_specs=[HBM] * 5 + [VMEM] * 5,
        name="attend",
    )(tokens, attention_gain, feedforward_gain, table_t, line_hot, router_t, columns, slots_t, *weights)

def gelu_parts(x):
    slope = math.sqrt(2.0 / math.pi)
    cubic = 0.044715 * slope
    square = x * x
    half = 0.5 + 0.5 * jnp.tanh(x * (slope + cubic * square))
    act = x * half
    return act, half + (act - act * half) * (2.0 * slope + 6.0 * cubic * square)


def chunks_of(total, most):
    return [(start, min(most, total - start)) for start in range(0, total, most)]


FF_CHUNK = 768


def hidden_grad_body(rows, down, out, weight, arrived):
    spans = chunks_of(weight.shape[0], FF_CHUNK)
    copies = [
        pltpu.make_async_copy(
            down.at[0, pl.ds(start, size), :], weight.at[pl.ds(start, size), :], arrived.at[place]
        )
        for place, (start, size) in enumerate(spans)
    ]
    for copy in copies:
        copy.start()
    x = rows[...]
    for copy, (start, size) in zip(copies, spans):
        copy.wait()
        out[:, start : start + size] = dot(x, weight[start : start + size, :], COLS).astype(jnp.bfloat16)


def hidden_grad(rows, down_weight):
    count, width = rows.shape
    hidden = down_weight.shape[1]
    return call(
        hidden_grad_body,
        shape((count, hidden)),
        scratch=[
            pltpu.VMEM((hidden, width), jnp.bfloat16),
            pltpu.SemaphoreType.DMA((len(chunks_of(hidden, FF_CHUNK)),)),
        ],
        in_specs=[VMEM, HBM],
        out_specs=VMEM,
        name="hidden_grad",
    )(rows, down_weight)


EXPERT_CHUNK = 256
EXPERT_FIRST = 3
EXPERT_SINGLE = 4
EXPERT_BLOCKS = 10
EXPERT_TILE = 256


def expert_body(width, rows, back, gate_weight, up_weight, hidden, gate_low, up_low, out, gate, up, grads, kept, acts, total, arrived, left):
    spans = chunks_of(gate.shape[1], EXPERT_CHUNK)
    copies = []
    for place, (start, size) in enumerate(spans):
        span = pl.ds(start, size)
        for side, (source, target) in enumerate(
            ((gate_weight.at[0], gate), (up_weight.at[0], up), (back, grads))
        ):
            copies.append(
                pltpu.make_async_copy(source.at[:, span], target.at[:, span], arrived.at[3 * place + side])
            )
    count = len(spans)
    start_all(copies[: 3 * EXPERT_FIRST])
    block = rows.shape[0] // EXPERT_BLOCKS
    choices = [jnp.zeros((block, 1), jnp.float32) for _ in range(EXPERT_BLOCKS)]
    backs = []

    def forward(turn, side, start, size):
        def step():
            weight = (gate, up)[side]
            at = spans[turn][0] + start
            acts[turn % 2, side, :, start : start + size] = dot(rows[:, :width], weight[:, at : at + size])

        return step

    def activate(place, part):
        def step():
            start, size = spans[place]
            span = slice(start, start + size)
            line = slice(part * block, (part + 1) * block)
            act, slope = gelu_parts(acts[place % 2, 0, line, :size])
            up_act = acts[place % 2, 1, line, :size]
            grad = grads[line, span].astype(jnp.float32)
            up_grad = grad * act
            kept[0, line, span] = (act * up_act).astype(jnp.bfloat16)
            kept[1, line, span] = (grad * up_act * slope).astype(jnp.bfloat16)
            kept[2, line, span] = up_grad.astype(jnp.bfloat16)
            choices[part] = choices[part] + jnp.sum(up_grad * up_act, axis=1, keepdims=True)

        return step

    def backward(place, start, size):
        def step():
            first, length = spans[place]
            span = slice(first, first + length)
            columns = slice(start, start + size)
            part = dot(kept[1, :, span], gate[columns, span], COLS) + dot(kept[2, :, span], up[columns, span], COLS)
            if place == 0:
                total[:, columns] = part
            else:
                total[:, columns] += part

        return step

    for turn in range(count + 2):
        products, elementwise = [], []
        if turn < count:
            if turn < EXPERT_SINGLE:
                wait_all(copies[3 * turn : 3 * turn + 3])
            elif turn == EXPERT_SINGLE:
                wait_all(copies[3 * turn :])
            if turn == 0:
                start_all(copies[3 * EXPERT_FIRST :])
            products += [
                forward(turn, side, *piece) for side in range(2) for piece in chunks_of(spans[turn][1], EXPERT_TILE)
            ]
        if 0 < turn <= count:
            elementwise = [activate(turn - 1, part) for part in range(EXPERT_BLOCKS)]
        if turn > 1:
            products += [backward(turn - 2, *piece) for piece in chunks_of(width, EXPERT_TILE)]
        done = 0
        for place, product in enumerate(products):
            product()
            target = len(elementwise) * (place + 1) // len(products)
            for step in elementwise[done:target]:
                step()
            done = target
        for step in elementwise[done:]:
            step()
        if turn > 1:
            place = turn - 2
            start, size = spans[place]
            for which, target in enumerate((hidden, gate_low, up_low)):
                backs.append(
                    pltpu.make_async_copy(
                        kept.at[which, :, pl.ds(start, size)],
                        target.at[:, pl.ds(start, size)],
                        left.at[3 * place + which],
                    )
                )
                backs[-1].start()
    choice = jnp.concatenate(choices, axis=0)
    out[:, :width] = total[...].astype(jnp.bfloat16)
    out[:, width:] = lane_parts(choice)
    for copy in backs:
        copy.wait()


def expert(rows, back, gate_weight, up_weight):
    count = rows.shape[0]
    width, hidden = gate_weight.shape[1:]
    act = shape((count, hidden))
    chunks = len(chunks_of(hidden, EXPERT_CHUNK))
    return call(
        lambda *refs: expert_body(width, *refs),
        [act, act, act, shape(rows.shape)],
        scratch=[
            pltpu.VMEM((width, hidden), jnp.bfloat16),
            pltpu.VMEM((width, hidden), jnp.bfloat16),
            pltpu.VMEM((count, hidden), jnp.bfloat16),
            pltpu.VMEM((3, count, hidden), jnp.bfloat16),
            pltpu.VMEM((2, 2, count, EXPERT_CHUNK), jnp.float32),
            pltpu.VMEM((count, width), jnp.float32),
            pltpu.SemaphoreType.DMA((3 * chunks,)),
            pltpu.SemaphoreType.DMA((3 * chunks,)),
        ],
        in_specs=[VMEM] + [HBM] * 3,
        out_specs=[HBM, HBM, HBM, VMEM],
        name="expert",
    )(rows, back, gate_weight, up_weight)


def expert_out_body(hidden, down, out, acts, weight, total, arrived):
    spans = chunks_of(weight.shape[0], FF_CHUNK)
    copies = []
    for place, (start, size) in enumerate(spans):
        span = pl.ds(start, size)
        copies.append(pltpu.make_async_copy(hidden.at[:, span], acts.at[:, span], arrived.at[2 * place]))
        copies.append(pltpu.make_async_copy(down.at[0, span, :], weight.at[span, :], arrived.at[2 * place + 1]))
    start_all(copies)
    for place, (start, size) in enumerate(spans):
        wait_all(copies[2 * place : 2 * place + 2])
        part = dot(acts[:, start : start + size], weight[start : start + size, :])
        if place == 0:
            total[...] = part
        elif place < len(spans) - 1:
            total[...] += part
        else:
            out[...] = (total[...] + part).astype(jnp.bfloat16)


def expert_out(hidden, down_weight):
    count = hidden.shape[0]
    inner, width = down_weight.shape[1:]
    return call(
        expert_out_body,
        shape((count, width)),
        scratch=[
            pltpu.VMEM((count, inner), jnp.bfloat16),
            pltpu.VMEM((inner, width), jnp.bfloat16),
            pltpu.VMEM((count, width), jnp.float32),
            pltpu.SemaphoreType.DMA((2 * len(chunks_of(inner, FF_CHUNK)),)),
        ],
        in_specs=[HBM] * 2,
        out_specs=VMEM,
        name="expert_out",
    )(hidden, down_weight)


def expert_grads_body(count, width, *refs):
    sources, lefts, sent = refs[:count], refs[count : 2 * count], refs[2 * count]
    targets = refs[2 * count + 1 : 3 * count + 1]
    acts, turned, scaled, staged, arrived, left = refs[3 * count + 1 :]
    spans = chunks_of(sources[0].shape[1], FF_CHUNK)
    steps = [(which, start, size) for which in range(count) for start, size in spans]
    coming = start_all(
        [
            pltpu.make_async_copy(
                sources[which].at[:, pl.ds(start, size)], acts.at[which, :, pl.ds(start, size)], arrived.at[turn]
            )
            for turn, (which, start, size) in enumerate(steps)
        ]
    )
    gate = sum_parts(sent[:, width:])
    for which in range(count):
        scaled[which] = (lefts[which][:, :width].astype(jnp.float32) * gate).astype(jnp.bfloat16)
    backs = []
    for turn in range(len(steps) + 1):
        if turn < len(steps):
            which, start, size = steps[turn]
            coming[turn].wait()
            turned[turn % 2, :size, :] = acts[which, :, start : start + size].T
        if turn > 0:
            which, start, size = steps[turn - 1]
            slot = (turn - 1) % staged.shape[0]
            if turn - 1 >= staged.shape[0]:
                backs[turn - 1 - staged.shape[0]].wait()
            staged[slot, :size, :] = dot(turned[(turn - 1) % 2, :size, :], scaled[which]).astype(jnp.bfloat16)
            backs.append(
                pltpu.make_async_copy(
                    staged.at[slot, pl.ds(0, size), :], targets[which].at[pl.ds(start, size), :], left.at[turn - 1]
                )
            )
            backs[-1].start()
    wait_all(backs[-staged.shape[0] :])


def expert_grads(pairs, sent, width):
    count = len(pairs)
    slots, inner = pairs[0][0].shape
    chunks = len(chunks_of(inner, FF_CHUNK))
    return call(
        lambda *refs: expert_grads_body(count, width, *refs),
        [shape((inner, width))] * count,
        scratch=[
            pltpu.VMEM((count, slots, inner), jnp.bfloat16),
            pltpu.VMEM((2, FF_CHUNK, slots), jnp.bfloat16),
            pltpu.VMEM((count, slots, width), jnp.bfloat16),
            pltpu.VMEM((4, FF_CHUNK, width), jnp.bfloat16),
            pltpu.SemaphoreType.DMA((count * chunks,)),
            pltpu.SemaphoreType.DMA((count * chunks,)),
        ],
        in_specs=[HBM] * count + [VMEM] * (count + 1),
        out_specs=[HBM] * count,
        name="expert_grads",
    )(*[acts for acts, rows in pairs], *[rows for acts, rows in pairs], sent)


def combine_body(returned, columns, gates, middle, block_out):
    length = middle.shape[0]
    slot = iota((length, returned.shape[0]), 1)
    rows = returned[...]
    rows1 = dot(ones_where(slot == columns[:, 0:1]), rows)
    rows2 = dot(ones_where(slot == columns[:, 1:2]), rows)
    block_out[...] = (middle[...] + gates[:, 0:1] * rows1 + gates[:, 1:2] * rows2).astype(jnp.bfloat16)


def combine(returned, columns, gates, middle):
    length, width = middle.shape
    return call(
        combine_body,
        shape((length, width)),
        in_specs=[VMEM] * 4,
        out_specs=VMEM,
        name="combine",
    )(returned, columns, gates, middle)


def router_back(logit, choice, gate1, gate2, picked):
    experts = logit.shape[1]
    top = jnp.max(logit, axis=1, keepdims=True)
    grown = jnp.exp(logit - top)
    total = jnp.sum(grown, axis=1, keepdims=True)
    probs = grown / total
    lse = top + jnp.log(total)
    expert = iota(logit.shape, 1)
    hot1 = ones_where(expert == picked[:, 0:1], jnp.float32)
    hot = hot1 - ones_where(expert == picked[:, 1:2], jnp.float32)
    balance = (BALANCE_COEF * experts) * jnp.mean(hot1, axis=0, keepdims=True)
    even = jnp.sum(probs * balance, axis=1, keepdims=True)
    return hot * (choice * gate1 * gate2) + probs * (balance - even + 2.0 * Z_COEF * lse)


def diagonals(x):
    half = x.shape[0] // 2
    top, low = x[:half], x[half:]
    x = jnp.concatenate([low[:, :half], low[:, half:] + top[:, :half], top[:, half:], jnp.zeros_like(low[:, :half])], axis=1)
    while x.shape[0] > 1:
        half = x.shape[0] // 2
        x = pltpu.roll(x[:half], half, 1) + x[half:]
    return x


def attend_back_body(
    heads, sent_grad, columns, gates, middle, feedforward_gain, cotangent, table_t, line_hot,
    logits, router_t, query, key, value, wo,
    middle_grad, backs, gain_grad, bias_lines, router_grad,
    weight, acts, lines, heads_grad, grad_out, backs_out, arrived, left,
):
    length, width = middle.shape
    size = width // heads
    half = width // 2
    copies = start_all(
        [pltpu.make_async_copy(wo, weight, arrived.at[3])]
        + [
            pltpu.make_async_copy(source, acts.at[place], arrived.at[place])
            for place, source in enumerate((query, key, value))
        ]
    )
    lines[...] = dot(table_t[...], line_hot[1], precision=PRECISE)
    slot = iota((length, sent_grad.shape[0]), 1)
    rows = sent_grad[...]
    rows1 = dot(ones_where(slot == columns[:, 0:1]), rows)
    rows2 = dot(ones_where(slot == columns[:, 1:2]), rows)
    gate1, gate2 = gates[:, 0:1], gates[:, 1:2]
    choice = sum_parts(rows1[:, width:] - rows2[:, width:])
    logit_grad = router_back(logits[...], choice, gate1, gate2, columns[:, 2:4])
    mid = middle[...]
    r = rms(mid)
    scaled = mid * r
    high, rest = split2(scaled * feedforward_gain[...])
    grad_high, grad_rest = split2(logit_grad)
    router_high, router_rest = split2(router_t[...])
    router_grad[...] = dot(grad_high, high, ROWS) + dot(grad_rest, high, ROWS) + dot(grad_high, rest, ROWS)
    normed2_grad = (
        gate1 * rows1[:, :width]
        + gate2 * rows2[:, :width]
        + (dot(grad_high, router_high) + dot(grad_rest, router_high) + dot(grad_high, router_rest))
    )
    u = normed2_grad * feedforward_gain[...]
    gain_grad[...] = jnp.sum(normed2_grad * scaled, axis=0, keepdims=True)
    grad = (
        cotangent[...].astype(jnp.float32)
        + r * u
        - mid * (r * r * r * jnp.mean(u * mid, axis=1, keepdims=True))
    )
    grad_out[...] = grad
    grad_copy = pltpu.make_async_copy(grad_out, middle_grad, left.at[2])
    grad_copy.start()
    low = grad.astype(jnp.bfloat16)
    wait_all(copies)
    heads_grad[...] = dot(low, weight[...], COLS).astype(jnp.bfloat16)
    backs_out[:, 3 * width :] = low
    pair_width = 2 * size
    first = iota((length, pair_width), 1) < size
    first_t = iota((pair_width, length), 0) < size
    zero = jnp.zeros((length, pair_width), jnp.bfloat16)
    scale = jnp.bfloat16(1.0 / math.sqrt(size))
    for pair in range(heads // 2):
        start = pair * pair_width
        span = slice(start, start + pair_width)
        q, k, v, g = acts[0, :, span] * scale, acts[1, :, span], acts[2, :, span], heads_grad[:, span]
        k_turned = (k * scale).T
        kept = []
        for side in range(2):
            q_side = jnp.where(first, q, zero) if side == 0 else jnp.where(first, zero, q)
            g_side = jnp.where(first, g, zero) if side == 0 else jnp.where(first, zero, g)
            head = 2 * pair + side
            line = jnp.broadcast_to(lines[head : head + 1, :], (length, 2 * length))
            bias = pltpu.roll(line, length + 1, 1, stride=1, stride_axis=0)[:, :length]
            scores = dot(k, q_side, COLS) + bias
            top = jnp.max(scores, axis=0, keepdims=True)
            grown = jnp.exp(scores - top)
            probs = grown * (1.0 / jnp.sum(grown, axis=0, keepdims=True))
            probs_grad = dot(v, g_side, COLS)
            score_grad = probs * (probs_grad - jnp.sum(probs * probs_grad, axis=0, keepdims=True))
            score_low = score_grad.astype(jnp.bfloat16)
            bias_lines[head : head + 1, :] = diagonals(score_low.astype(jnp.float32))
            kept.append(
                (
                    dot(k_turned, score_low),
                    dot(score_low, q),
                    dot(probs.astype(jnp.bfloat16), g),
                )
            )
        results = (
            jnp.where(first_t, kept[0][0], kept[1][0]).astype(jnp.bfloat16).T,
            jnp.where(first, kept[0][1], kept[1][1]).astype(jnp.bfloat16),
            jnp.where(first, kept[0][2], kept[1][2]).astype(jnp.bfloat16),
        )
        for place, result in enumerate(results):
            backs_out[:, place * width + start : place * width + start + pair_width] = result
    leaving = pltpu.make_async_copy(backs_out, backs, left.at[0])
    leaving.start()
    leaving.wait()
    grad_copy.wait()


def attend_back(heads, line_hot, sent_grad, columns, gates, middle, feedforward_gain, cotangent, table_t, logits, router_t, query, key, value, wo):
    length, width = middle.shape
    return call(
        lambda *refs: attend_back_body(heads, *refs),
        [
            shape((length, width), jnp.float32),
            shape((length, 4 * width)),
            shape((1, width), jnp.float32),
            shape((heads, 2 * length), jnp.float32),
            shape(router_t.shape, jnp.float32),
        ],
        scratch=[
            pltpu.VMEM((width, width), jnp.bfloat16),
            pltpu.VMEM((3, length, width), jnp.bfloat16),
            pltpu.VMEM((heads, 2 * length), jnp.float32),
            pltpu.VMEM((length, width), jnp.bfloat16),
            pltpu.VMEM((length, width), jnp.float32),
            pltpu.VMEM((length, 4 * width), jnp.bfloat16),
            pltpu.SemaphoreType.DMA((4,)),
            pltpu.SemaphoreType.DMA((3,)),
        ],
        in_specs=[VMEM] * 10 + [HBM] * 4,
        out_specs=[HBM] * 2 + [VMEM] * 3,
        name="attend_back",
    )(sent_grad, columns, gates, middle, feedforward_gain, cotangent, table_t, line_hot, logits, router_t, query, key, value, wo)


def input_back_body(backs_in, grad_in, tokens, attention_gain, bias_lines, line_hot, wq, wk, wv, input_grad, vectors, weights, backs, middle_grad, arrived):
    length, width = tokens.shape
    copies = []
    for place, source in enumerate((wq, wk, wv)):
        span = pl.ds(place * width, width)
        copies.append(pltpu.make_async_copy(backs_in.at[:, span], backs.at[:, span], arrived.at[place]))
        copies.append(pltpu.make_async_copy(source, weights.at[place], arrived.at[3 + place]))
    copies.append(pltpu.make_async_copy(grad_in, middle_grad, arrived.at[6]))
    start_all(copies)
    bias = dot(bias_lines[...], line_hot[1], COLS, PRECISE)
    rows = bias.shape[0] // 4
    bias = jnp.concatenate([bias[rows * part : rows * (part + 1)] for part in range(4)], axis=1)
    x = tokens[...].astype(jnp.float32)
    s = rms(x)
    total = jnp.zeros((length, width), jnp.float32)
    for place in range(3):
        wait_all(copies[2 * place : 2 * place + 2])
        total = total + dot(backs[:, place * width : (place + 1) * width], weights[place], COLS)
    w = total * attention_gain[...]
    gain = jnp.sum(total * x * s, axis=0, keepdims=True)
    vectors[...] = jnp.zeros_like(vectors)
    for part in range(width // LANES):
        vectors[part : part + 1, :] = gain[:, part * LANES : (part + 1) * LANES]
    vectors[width // LANES : width // LANES + rows, :] = bias
    copies[6].wait()
    input_grad[...] = middle_grad[...] + s * w - x * (s * s * s * jnp.mean(w * x, axis=1, keepdims=True))


def input_back(line_hot, backs, middle_grad, tokens, attention_gain, bias_lines, wq, wk, wv):
    length, width = tokens.shape
    return call(
        input_back_body,
        [
            shape((length, width), jnp.float32),
            shape((BLOCK, LANES), jnp.float32),
        ],
        scratch=[
            pltpu.VMEM((3, width, width), jnp.bfloat16),
            pltpu.VMEM((length, 3 * width), jnp.bfloat16),
            pltpu.VMEM((length, width), jnp.float32),
            pltpu.SemaphoreType.DMA((7,)),
        ],
        in_specs=[HBM] * 2 + [VMEM] * 4 + [HBM] * 3,
        out_specs=[VMEM] * 2,
        name="input_back",
    )(backs, middle_grad, tokens, attention_gain, bias_lines, line_hot, wq, wk, wv)


EXTRA = 2 * LANES


def resplit(lanes):
    half = LANES // 2
    total = lanes + pltpu.roll(lanes, half, 1)
    high = total.astype(jnp.bfloat16).astype(jnp.float32)
    return jnp.where(iota(lanes.shape, 1) < half, high, total - high)


def rotated(place, side, block, step):
    return pl.ds(pl.multiple_of(((place + step) % side) * block, block), block)


def products_body(side, where, normed, heads_out, left_far, backs_in, far_in, feedforward_gain, router, *rest):
    pieces, (lefts, backs, payload, vectors, arrived, left) = rest[:side], rest[side:]
    length, width = normed.shape
    half = width // 2
    mine = pl.ds(pl.multiple_of(where[0] * half, half), half)
    copies = start_all(
        [
            pltpu.make_async_copy(normed.at[:, mine], lefts.at[0, :, pl.ds(0, half)], arrived.at[0]),
            pltpu.make_async_copy(heads_out.at[:, mine], lefts.at[0, :, pl.ds(half, half)], arrived.at[1]),
            pltpu.make_async_copy(left_far, lefts.at[1], arrived.at[2]),
        ]
        + [
            pltpu.make_async_copy(
                source.at[:, pl.ds(place * width, width)],
                backs.at[which, :, pl.ds(place * width, width)],
                arrived.at[3 + 2 * place + which],
            )
            for place in range(4)
            for which, source in enumerate((backs_in, far_in))
        ]
    )
    experts = router.shape[0]
    vectors[...] = jnp.zeros_like(vectors)
    vectors[0:1, :] = feedforward_gain[...]
    vectors[8 : 8 + experts, :] = router[...]
    for place in range(2):
        start = 4 * width + place * LANES
        payload[:, start : start + LANES] = resplit(vectors[:, place * half : (place + 1) * half].T).astype(jnp.bfloat16)
    position = where[2 + where[0]]
    leaving = []

    def leave(part, start, size):
        for step, piece in enumerate(pieces):
            leaving.append(
                pltpu.make_async_copy(
                    payload.at[rotated(position, side, half // side, step), pl.ds(start, size)],
                    piece.at[:, pl.ds(start, size)],
                    left.at[part * side + step],
                )
            )
            leaving[-1].start()

    leave(4, 4 * width, EXTRA)
    wait_all(copies[:3])
    for place in range(4):
        wait_all(copies[3 + 2 * place : 5 + 2 * place])
        span = slice(place * width, (place + 1) * width)
        start = 0 if place < 3 else half
        payload[:, span] = (
            dot(lefts[0, :, start : start + half], backs[0, :, span], ROWS)
            + dot(lefts[1, :, start : start + half], backs[1, :, span], ROWS)
        ).astype(jnp.bfloat16)
        leave(place, place * width, width)
    wait_all(leaving)


def products(side, normed, heads_out, left_far, backs, backs_far, feedforward_gain, router):
    length, width = normed.shape
    wide = 4 * width + EXTRA
    return call(
        lambda *refs: products_body(side, Place(side), *refs),
        [shape((width // 2 // side, wide))] * side,
        scratch=[
            pltpu.VMEM((2, length, width), jnp.bfloat16),
            pltpu.VMEM((2, length, 4 * width), jnp.bfloat16),
            pltpu.VMEM((width // 2, wide), jnp.bfloat16),
            pltpu.VMEM((LANES, width), jnp.float32),
            pltpu.SemaphoreType.DMA((11,)),
            pltpu.SemaphoreType.DMA((5 * side,)),
        ],
        in_specs=[HBM] * 5 + [VMEM] * 2,
        out_specs=[HBM] * side,
        name="products",
    )(normed, heads_out, left_far, backs, backs_far, feedforward_gain, router)


def total_into(out, refs, late):
    total = refs[0][...].astype(jnp.float32)
    for ref in refs[1:]:
        total = total + ref[...].astype(jnp.float32)
    wide = total.shape[1] - EXTRA - (LANES if late else 0)
    out[:, :wide] = total[:, :wide].astype(jnp.bfloat16)
    for start in range(wide, wide + EXTRA, LANES):
        out[:, start : start + LANES] = resplit(total[:, start : start + LANES]).astype(jnp.bfloat16)
    if late:
        out[:, wide + EXTRA :] = stack_parts(total[:BLOCK, wide + EXTRA :] + total[BLOCK:, wide + EXTRA :])


def stack_parts(block):
    return jnp.concatenate(split2(block), axis=0)


def fold_body(side, where, vectors, *refs):
    pieces, outs, total = refs[:side], refs[side : 2 * side], refs[-1]
    total_into(total, pieces, False)
    position = where[3 - where[0]]
    wide = total.shape[1]
    late = stack_parts(vectors[...])
    for step, out in enumerate(outs):
        out[:, :wide] = total[rotated(position, side, out.shape[0], step), :]
        out[:, wide:] = late


def fold(side, vectors, pieces):
    rows, wide = pieces[0].shape
    return call(
        lambda *refs: fold_body(side, Place(side), *refs),
        [shape((rows // side, wide + LANES))] * side,
        scratch=[pltpu.VMEM((rows, wide), jnp.bfloat16)],
        in_specs=[VMEM] * (side + 1),
        out_specs=[VMEM] * side,
        vmem=16,
        name="fold",
    )(vectors, *pieces)


def add_pieces(pieces):
    return call(
        lambda *refs: total_into(refs[-1], refs[:-1], True),
        shape(pieces[0].shape),
        in_specs=[VMEM] * len(pieces),
        out_specs=VMEM,
        vmem=12,
        name="add_pieces",
    )(*pieces)


def put_body(side, where, *refs):
    pieces, (whole, upper, lower) = refs[:side], refs[side:]
    position = where[3 - where[0]]
    rows = upper.shape[0]
    for step in range(side):
        whole[rotated(position, side, pieces[0].shape[0], step), :] = pieces[step][...]
    upper[...] = whole[:rows, :]
    lower[...] = whole[rows:, :]


def put(side, pieces):
    rows, wide = pieces[0].shape
    half = shape((side * rows // 2, wide))
    return call(
        lambda *refs: put_body(side, Place(side), *refs),
        [shape((side * rows, wide)), half, half],
        in_specs=[VMEM] * side,
        out_specs=[VMEM] * 3,
        vmem=24,
        name="put",
    )(*pieces)


def again_body(whole, upper, lower):
    rows = upper.shape[0]
    upper[...] = whole[:rows, :]
    lower[...] = whole[rows:, :]


def again(whole):
    half = shape((whole.shape[0] // 2, whole.shape[1]))
    return call(again_body, [half, half], in_specs=[VMEM], out_specs=[VMEM] * 2, vmem=24, name="again")(whole)


def begin_body(side, where, near, far, *refs):
    outs, (held, staged, arrived, left) = refs[:4], refs[4:]
    rows, width = staged.shape[2:]
    copies = start_all(
        [
            pltpu.make_async_copy(source.at[:, pl.ds(0, 4 * width)], held.at[which], arrived.at[which])
            for which, source in enumerate((near, far))
        ]
    )
    backs = []
    for which in range(2):
        core = where[0] if which == 0 else 1 - where[0]
        copies[which].wait()
        line = pl.ds(pl.multiple_of(core * (width // 2) + where[2 + core] * rows, rows), rows)
        for matrix in range(4):
            staged[which, matrix] = held[which, :, matrix * width : (matrix + 1) * width].astype(jnp.float32)
            backs.append(
                pltpu.make_async_copy(staged.at[which, matrix], outs[matrix].at[line, :], left.at[4 * which + matrix])
            )
            backs[-1].start()
    wait_all(backs)


def begin(side, near, far):
    rows, wide = near.shape
    width = (wide - EXTRA - LANES) // 4
    return call(
        lambda *refs: begin_body(side, Place(side), *refs),
        [shape((width, width), jnp.float32)] * 4,
        scratch=[
            pltpu.VMEM((2, rows, 4 * width), jnp.bfloat16),
            pltpu.VMEM((2, 4, rows, width), jnp.float32),
            pltpu.SemaphoreType.DMA((2,)),
            pltpu.SemaphoreType.DMA((8,)),
        ],
        in_specs=[HBM] * 2,
        out_specs=[HBM] * 4,
        name="begin",
    )(near, far)


def finish_body(side, steps, where, *refs):
    parts = sum(len(order) for step, order in steps)
    pieces, refs = (refs[:parts], refs[parts : 2 * parts]), refs[2 * parts :]
    up_low, outs, refs = refs[0], refs[5:9], refs[9:]
    up_out, gain, feedforward_gain, router_t, bias_t, held, staged, up_held, up_staged, late, arrived, left = refs
    rows = staged.shape[2]
    width = staged.shape[3]
    half = width // 2
    wide = held.shape[3]
    copies = []
    for which in range(2):
        place = 0
        for block, (step, order) in enumerate(steps):
            size = rows // len(order)
            columns = pl.ds(0 if step else 4 * width, wide if step else wide - 4 * width)
            copies.append(
                start_all(
                    [
                        pltpu.make_async_copy(
                            pieces[which][place + part].at[:, columns],
                            held.at[which, block, pl.ds(order[part] * size, size), columns],
                            arrived.at[which * parts + place + part],
                        )
                        for part in range(len(order))
                    ]
                )
            )
            place += len(order)
    up_copy = pltpu.make_async_copy(up_low, up_held, arrived.at[2 * parts])
    up_copy.start()
    for vector in (feedforward_gain, router_t, late):
        vector[...] = jnp.zeros_like(vector)
    backs = []
    for block, (step, order) in enumerate(steps):
        for which in range(2):
            core = where[0] if which == 0 else 1 - where[0]
            slot = which * len(steps) + block
            wait_all(copies[slot])
            start = pl.multiple_of(((where[2 + core] + step) % side) * rows, rows)
            line = pl.ds(pl.multiple_of(core * half + start, rows), rows)
            for matrix in range(4 if step else 0):
                staged[slot, matrix] = held[which, block, :, matrix * width : (matrix + 1) * width].astype(jnp.float32)
                backs.append(
                    pltpu.make_async_copy(
                        staged.at[slot, matrix], outs[matrix].at[line, :], left.at[4 * slot + matrix]
                    )
                )
                backs[-1].start()
            for place in range(2):
                lanes = held[which, block, :, 4 * width + place * LANES : 4 * width + (place + 1) * LANES]
                lanes = lanes.astype(jnp.float32)
                turned = (lanes + pltpu.roll(lanes, LANES // 2, 1)).T
                line = pl.ds(pl.multiple_of(place * half + start, rows), rows)
                feedforward_gain[:, line] += turned[0:1]
                router_t[:, line] += turned[8 : 8 + router_t.shape[0]]
            block_rows = held[which, block, : 2 * BLOCK, 4 * width + EXTRA :].astype(jnp.float32)
            late[...] += block_rows[:BLOCK] + block_rows[BLOCK:]
    up_copy.wait()
    up_staged[...] = up_held[...].astype(jnp.float32)
    backs.append(pltpu.make_async_copy(up_staged, up_out, left.at[8 * len(steps)]))
    backs[-1].start()
    lines = width // LANES
    for part in range(lines):
        gain[:, part * LANES : (part + 1) * LANES] = late[part : part + 1, :]
    heads, buckets = bias_t.shape
    for part in range(4):
        bias_t[part * heads // 4 : (part + 1) * heads // 4, :] = late[
            lines : lines + heads // 4, part * buckets : (part + 1) * buckets
        ]
    wait_all(backs)


def finish(side, steps, near, far, up_low, begun, experts, buckets, heads):
    wide = near[0].shape[1]
    width = (wide - EXTRA - LANES) // 4
    rows = width // 2 // side
    count, parts = len(steps), len(near)
    return call(
        lambda *refs: finish_body(side, steps, Place(side), *refs),
        [shape((width, width), jnp.float32)] * 4
        + [
            shape(up_low.shape, jnp.float32),
            shape((1, width), jnp.float32),
            shape((1, width), jnp.float32),
            shape((experts, width), jnp.float32),
            shape((heads, buckets), jnp.float32),
        ],
        scratch=[
            pltpu.VMEM((2, count, rows, wide), jnp.bfloat16),
            pltpu.VMEM((2 * count, 4, rows, width), jnp.float32),
            pltpu.VMEM(up_low.shape, jnp.bfloat16),
            pltpu.VMEM(up_low.shape, jnp.float32),
            pltpu.VMEM((BLOCK, LANES), jnp.float32),
            pltpu.SemaphoreType.DMA((2 * parts + 1,)),
            pltpu.SemaphoreType.DMA((8 * count + 1,)),
        ],
        in_specs=[HBM] * (2 * parts + 5),
        out_specs=[HBM] * 5 + [VMEM] * 4,
        input_output_aliases={2 * parts + 1 + matrix: matrix for matrix in range(4)},
        name="finish",
    )(*near, *far, up_low, *begun)


def rotate_x(count, step):
    return [(x * 2 + c, ((x + step) % count) * 2 + c) for x in range(count) for c in range(2)]


def rotate_plane(chips, side, flip, step):
    pairs = []
    for x in range(chips):
        for core in range(2):
            for z in range(side):
                for y in range(side):
                    along_z = core ^ flip
                    to = ((z + step) % side, y) if along_z else (z, (y + step) % side)
                    base = (x * 2 + core) * side * side
                    pairs.append((base + z * side + y, base + to[0] * side + to[1]))
    return pairs


def swap_cores(count):
    return [(x * 2 + c, x * 2 + 1 - c) for x in range(count) for c in range(2)]


def shards(
    tokens,
    routes,
    cotangent,
    attention_gain,
    query_weight,
    key_weight,
    value_weight,
    output_weight,
    bias_table,
    feedforward_gain,
    router_weight,
    gate_weight,
    up_weight,
    down_weight,
):
    length, width = tokens.shape
    buckets, heads = bias_table.shape
    experts = lax.axis_size("expert")
    chips = lax.axis_size("dp") // 2
    side = math.isqrt(experts)
    capacity = max(2, (10 * length + 4 * experts - 1) // (4 * experts))
    swap = swap_cores(chips)
    line_hot = jnp.asarray(bucket_lines(length, buckets))
    gain1, gain2 = attention_gain[None], feedforward_gain[None]

    def exchange(rows):
        return lax.all_to_all(
            rows.reshape(experts, capacity, -1), "expert", split_axis=0, concat_axis=0, tiled=True
        ).reshape(experts * capacity, -1)

    table_t, router_t = bias_table.T, router_weight.T
    slots_t, columns, cot_slots = route(routes, cotangent, experts, capacity)
    cot_rows = exchange(cot_slots)
    normed, query, key, value, heads_out, left, middle, logits, gates, sent = attend(
        heads, experts * capacity, side, line_hot, tokens, gain1, gain2, table_t, router_t, columns, slots_t,
        (query_weight, key_weight, value_weight, output_weight),
    )

    def swapped(array):
        return lax.ppermute(array, "dp", swap)

    rows = exchange(sent)
    left_far = swapped(left)
    back = hidden_grad(cot_rows, down_weight)
    rows, left_far = lax.optimization_barrier((rows, left_far))
    hidden, gate_low, up_acts, rows_grad = expert(rows, back, gate_weight, up_weight)
    sent_grad = exchange(rows_grad)

    def scatter_dp(part):
        return lax.psum_scatter(part, "dp", scatter_dimension=0, tiled=True)

    grads = expert_grads(((hidden, cot_rows), (gate_low, rows)), rows, width)
    sent_grad, grads = lax.optimization_barrier((sent_grad, grads))
    down_grad, gate_grad = scatter_dp(grads[0]), scatter_dp(grads[1])

    middle_grad, backs, gain2_part, bias_lines, router_part = attend_back(
        heads, line_hot, sent_grad, columns, gates, middle, gain2, cotangent, table_t, logits,
        router_t, query, key, value, output_weight,
    )
    backs_far = swapped(backs)
    pieces = products(side, normed, heads_out, left_far, backs, backs_far, gain2_part, router_part)

    def turn(piece, flip, step):
        return lax.ppermute(piece, ("dp", "expert"), rotate_plane(chips, side, flip, step))

    def scatter_plane(pieces, flip):
        return [pieces[0]] + [turn(pieces[step], flip, step) for step in range(1, side)]

    pieces, hidden, backs = lax.optimization_barrier((pieces, hidden, backs))
    folded_in = scatter_plane(pieces, 0)
    input_grad, vectors = input_back(
        line_hot, backs, middle_grad, tokens, gain1, bias_lines, query_weight, key_weight, value_weight
    )
    returned = expert_out(hidden, down_weight)
    down_grad = down_grad.astype(jnp.float32)
    folded_in, vectors, returned, down_grad = lax.optimization_barrier((folded_in, vectors, returned, down_grad))
    shard = add_pieces(scatter_plane(fold(side, vectors, folded_in), 1))
    shard, returned, up_acts = lax.optimization_barrier((shard, returned, up_acts))
    returned = exchange(returned)
    (up_part,) = expert_grads(((up_acts, rows),), rows, width)
    total = add_pieces([shard] + [lax.ppermute(shard, "dp", rotate_x(chips, step)) for step in range(1, chips)])
    total, up_part, returned = lax.optimization_barrier((total, up_part, returned))
    up_low = scatter_dp(up_part)
    gathered = [total] + [turn(total, 1, -step) for step in range(1, side)]
    gate_grad = gate_grad.astype(jnp.float32)
    block_out = combine(returned, columns, gates, middle)
    gathered, gate_grad, block_out = lax.optimization_barrier((gathered, gate_grad, block_out))
    own, upper, lower = put(side, gathered)
    minus_upper, plus_lower = turn(upper, 0, 1), turn(lower, 0, -1)
    upper2, lower2 = again(own)
    minus_lower, plus_upper = turn(lower2, 0, 1), turn(upper2, 0, -1)
    own_far = swapped(own)
    plus_lower, begun = lax.optimization_barrier((plus_lower, begin(side, own, own_far)))
    across = [turn(minus_upper, 0, 1), turn(plus_lower, 0, -1)]
    near = [plus_lower, plus_upper, minus_lower, minus_upper, *across]
    far = [own_far, *[swapped(piece) for piece in near]]
    near = [own, *near]
    query_grad, key_grad, value_grad, output_grad, up_grad, gain1_grad, gain2_grad, router_grad_t, bias_grad_t = finish(
        side, ((0, (0,)), (1, (1, 0)), (3, (1, 0)), (2, (0, 1))), near, far, up_low, begun, experts, buckets, heads
    )
    return (
        block_out,
        input_grad,
        gain1_grad[0],
        query_grad,
        key_grad,
        value_grad,
        output_grad,
        bias_grad_t.T,
        gain2_grad[0],
        router_grad_t.T,
        gate_grad.T[None],
        up_grad.T[None],
        down_grad[None],
    )


def solution(mesh):
    return jax.shard_map(
        shards,
        mesh=mesh,
        in_specs=(
            P(("dp", "expert"), None),
            P(("dp", "expert"), None),
            P(("dp", "expert"), None),
            P(),
            P(),
            P(),
            P(),
            P(),
            P(),
            P(),
            P(),
            P("expert", None, None),
            P("expert", None, None),
            P("expert", None, None),
        ),
        out_specs=(
            P(("dp", "expert"), None),
            P(("dp", "expert"), None),
            P(),
            P(),
            P(),
            P(),
            P(),
            P(),
            P(),
            P(),
            P("expert", None, "dp"),
            P("expert", None, "dp"),
            P("expert", "dp", None),
        ),
        check_vma=False,
    )
```

```python
import math

import jax
import jax.numpy as jnp
import numpy as np
from jax import lax
from jax.experimental import pallas as pl
from jax.experimental.pallas import tpu as pltpu
from jax.sharding import PartitionSpec as P

EPSILON = 1e-06
Z_COEF = 0.001
BALANCE_COEF = 0.01
PRECISE = lax.Precision.HIGHEST
LANES = 128
BLOCK = 16
MIB = 1024 * 1024
VMEM = pl.BlockSpec(memory_space=pltpu.VMEM)
HBM = pl.BlockSpec(memory_space=pl.ANY)
SMEM = pl.BlockSpec(memory_space=pltpu.SMEM)


def bucket_table(length, bucket_count):
    half_count = bucket_count // 2
    exact_count = half_count // 2
    position = np.arange(length)
    relative = position[None, :] - position[:, None]
    distance = np.abs(relative)
    spread = (
        np.log(np.maximum(distance, 1) / exact_count)
        / np.log(128.0 / exact_count)
        * (half_count - exact_count)
    )
    far_bucket = np.minimum(
        exact_count + np.floor(np.maximum(spread, 0.0)).astype(np.int32), half_count - 1
    )
    bucket_index = np.where(distance < exact_count, distance, far_bucket)
    return (bucket_index + (relative > 0) * half_count).astype(np.int32)


def bucket_lines(length, bucket_count):
    table = bucket_table(length, bucket_count)
    line = np.concatenate([table[::-1, 0], table[0, 1:]])
    hot = np.zeros((2, bucket_count, 2 * length), np.float32)
    for place, bucket in enumerate(line):
        hot[0, bucket, place] = 1.0
        hot[1, bucket, 2 * length - 2 - place] = 1.0
    return hot


def dot(left, right, dims=((1,), (0,)), precision=None):
    return lax.dot_general(
        left, right, (dims, ((), ())), precision=precision, preferred_element_type=jnp.float32
    )


ROWS = ((0,), (0,))
COLS = ((1,), (1,))


def iota(shape, axis):
    return lax.broadcasted_iota(jnp.int32, shape, axis)


def ones_where(condition, dtype=jnp.bfloat16):
    return jnp.where(condition, 1.0, 0.0).astype(dtype)


def call(body, outs, scratch=(), vmem=63, flops=1024, **options):
    return pl.pallas_call(
        body,
        out_shape=outs,
        scratch_shapes=list(scratch),
        compiler_params=pltpu.CompilerParams(vmem_limit_bytes=vmem * MIB),
        cost_estimate=pl.CostEstimate(flops=flops, bytes_accessed=1024, transcendentals=0),
        **options,
    )


class Place:
    def __init__(self, side):
        replica, expert = lax.axis_index("dp"), lax.axis_index("expert")
        self.parts = (replica % 2, replica // 2, expert % side, expert // side)

    def __getitem__(self, which):
        if isinstance(which, int):
            return self.parts[which]
        return jnp.where(which == 2, self.parts[2], self.parts[3])


def shape(dims, dtype=jnp.bfloat16):
    return jax.ShapeDtypeStruct(dims, dtype)


def route_body(capacity, experts, routes_t, cotangent, slots_t, columns, cot_slots):
    length = cotangent.shape[0]
    before = ones_where(iota((length, length), 0) < iota((length, length), 1))
    picked = routes_t[...]
    expert = iota((experts, length), 0)
    hot1 = ones_where(expert == picked[0:1], jnp.float32)
    hot2 = ones_where(expert == picked[1:2], jnp.float32)
    filled = jnp.sum(hot1, axis=1, keepdims=True)
    number1 = dot(hot1.astype(jnp.bfloat16), before)
    number2 = dot(hot2.astype(jnp.bfloat16), before) + filled
    place1 = jnp.sum(number1 * hot1, axis=0, keepdims=True).astype(jnp.int32)
    place2 = jnp.sum(number2 * hot2, axis=0, keepdims=True).astype(jnp.int32)
    slot1 = jnp.where(place1 < capacity, picked[0:1] * capacity + place1, -1)
    slot2 = jnp.where(place2 < capacity, picked[1:2] * capacity + place2, -1)
    slots_t[0:1] = slot1
    slots_t[1:2] = slot2
    lines = jnp.concatenate([slot1, slot2, picked, jnp.zeros((4, length), jnp.int32)], axis=0)
    columns[...] = lines.T
    slot = iota((experts * capacity, length), 0)
    dispatch = ones_where((slot == slot1) | (slot == slot2))
    cot_slots[...] = dot(dispatch, cotangent[...]).astype(jnp.bfloat16)


def route(routes, cotangent, experts, capacity):
    length, width = cotangent.shape
    return call(
        lambda *refs: route_body(capacity, experts, *refs),
        [
            shape((2, length), jnp.int32),
            shape((length, 8), jnp.int32),
            shape((experts * capacity, width)),
        ],
        in_specs=[VMEM] * 2,
        out_specs=[VMEM] * 3,
        name="route",
    )(routes.T, cotangent)


def start_all(copies):
    for copy in copies:
        copy.start()
    return copies


def wait_all(copies):
    for copy in copies:
        copy.wait()


def split2(x):
    high = x.astype(jnp.bfloat16)
    return high, (x - high.astype(jnp.float32)).astype(jnp.bfloat16)


def rms(x):
    return lax.rsqrt(jnp.mean(x * x, axis=1, keepdims=True) + EPSILON)


def split3(x):
    high = x.astype(jnp.bfloat16)
    rest = x - high.astype(jnp.float32)
    mid = rest.astype(jnp.bfloat16)
    return high, mid, (rest - mid.astype(jnp.float32)).astype(jnp.bfloat16)


def lane_parts(column):
    lane = iota((column.shape[0], LANES), 1)
    spread = jnp.zeros(lane.shape, jnp.float32)
    for place, part in enumerate(split3(column)):
        spread = jnp.where(lane == place, part.astype(jnp.float32), spread)
    return spread.astype(jnp.bfloat16)


def sum_parts(lanes):
    parts = lanes.astype(jnp.float32)
    return parts[:, 0:1] + parts[:, 1:2] + parts[:, 2:3]


def attend_body(
    heads, where, tokens, attention_gain, feedforward_gain, table_t, line_hot, router_t, columns, slots_t,
    wq, wk, wv, wo,
    normed_out, query_out, key_out, value_out, heads_done, left_send, middle, logits, gates, sent,
    weights, lines, acts, arrived, left,
):
    length, width = tokens.shape
    size = width // heads
    copies = [
        pltpu.make_async_copy(source, weights.at[place], arrived.at[place])
        for place, source in enumerate((wq, wk, wv, wo))
    ]
    start_all(copies[:3])
    backs = [
        pltpu.make_async_copy(acts.at[place], target, left.at[place])
        for place, target in enumerate((normed_out, query_out, key_out, value_out, heads_done))
    ]
    lines[...] = dot(table_t[...], line_hot[0], precision=PRECISE)
    wait_all(copies[:3])
    copies[3].start()
    x = tokens[...].astype(jnp.float32)
    low = (x * rms(x) * attention_gain[...]).astype(jnp.bfloat16)
    acts[0] = low
    backs[0].start()
    for place in range(3):
        acts[place + 1] = dot(acts[0], weights[place]).astype(jnp.bfloat16)
        backs[place + 1].start()
    first = iota((length, 2 * size), 1) < size
    zero = jnp.zeros((length, 2 * size), jnp.bfloat16)
    scale = 1.0 / math.sqrt(size)
    for pair in range(heads // 2):
        span = slice(pair * 2 * size, (pair + 1) * 2 * size)
        q, k, v = acts[1, :, span] * jnp.bfloat16(scale), acts[2, :, span], acts[3, :, span]
        outs = []
        for side in range(2):
            q_side = jnp.where(first, q, zero) if side == 0 else jnp.where(first, zero, q)
            head = 2 * pair + side
            line = jnp.broadcast_to(lines[head : head + 1, :], (length, 2 * length))
            bias = pltpu.roll(line, length + 1, 1, stride=1, stride_axis=0)[:, :length]
            scores = dot(q_side, k, COLS) + bias
            top = jnp.max(scores, axis=1, keepdims=True)
            grown = jnp.exp(scores - top)
            total = jnp.sum(grown, axis=1, keepdims=True)
            outs.append(dot((grown * (1.0 / total)).astype(jnp.bfloat16), v))
        acts[4, :, span] = jnp.where(first, outs[0], outs[1]).astype(jnp.bfloat16)
    backs[4].start()
    half = width // 2
    other = pl.ds(pl.multiple_of((1 - where[0]) * half, half), half)
    left_send[:, :half] = acts[0, :, other]
    left_send[:, half:] = acts[4, :, other]
    copies[3].wait()
    mid = x + dot(acts[4], weights[3])
    middle[...] = mid
    normed2 = mid * rms(mid) * feedforward_gain[...]
    high, rest = split2(normed2)
    experts = router_t.shape[0]
    router_high, router_rest = split2(router_t[...])
    logit = dot(high, router_high, COLS) + dot(high, router_rest, COLS) + dot(rest, router_high, COLS)
    logits[...] = logit
    picked = columns[:, 2:4]
    expert = iota(logit.shape, 1)
    logit1 = jnp.sum(jnp.where(expert == picked[:, 0:1], logit, 0.0), axis=1, keepdims=True)
    logit2 = jnp.sum(jnp.where(expert == picked[:, 1:2], logit, 0.0), axis=1, keepdims=True)
    gate1 = 1.0 / (1.0 + jnp.exp(logit2 - logit1))
    gate2 = 1.0 / (1.0 + jnp.exp(logit1 - logit2))
    gates[:, 0:1] = gate1
    gates[:, 1:2] = gate2
    slot = iota((sent.shape[0], length), 0)
    hot1 = ones_where(slot == slots_t[0:1])
    hot2 = ones_where(slot == slots_t[1:2])
    sent[:, :width] = dot(hot1 + hot2, high).astype(jnp.bfloat16)
    sent[:, width:] = (dot(hot1, lane_parts(gate1)) + dot(hot2, lane_parts(gate2))).astype(jnp.bfloat16)
    wait_all(backs)


def attend(heads, slot_count, side, line_hot, tokens, attention_gain, feedforward_gain, table_t, router_t, columns, slots_t, weights):
    length, width = tokens.shape
    experts = router_t.shape[0]
    act = shape((length, width))
    return call(
        lambda *refs: attend_body(heads, Place(side), *refs),
        [
            act, act, act, act, act, act,
            shape((length, width), jnp.float32),
            shape((length, experts), jnp.float32),
            shape((length, 2), jnp.float32),
            shape((slot_count, width + LANES)),
        ],
        scratch=[
            pltpu.VMEM((4, width, width), jnp.bfloat16),
            pltpu.VMEM((heads, 2 * length), jnp.float32),
            pltpu.VMEM((5, length, width), jnp.bfloat16),
            pltpu.SemaphoreType.DMA((4,)),
            pltpu.SemaphoreType.DMA((5,)),
        ],
        in_specs=[VMEM] * 8 + [HBM] * 4,
        out_specs=[HBM] * 5 + [VMEM] * 5,
        name="attend",
    )(tokens, attention_gain, feedforward_gain, table_t, line_hot, router_t, columns, slots_t, *weights)

def gelu_parts(x):
    slope = math.sqrt(2.0 / math.pi)
    cubic = 0.044715 * slope
    square = x * x
    half = 0.5 + 0.5 * jnp.tanh(x * (slope + cubic * square))
    act = x * half
    return act, half + (act - act * half) * (2.0 * slope + 6.0 * cubic * square)


def chunks_of(total, most):
    return [(start, min(most, total - start)) for start in range(0, total, most)]


FF_CHUNK = 768


def hidden_grad_body(rows, down, out, weight, arrived):
    spans = chunks_of(weight.shape[0], FF_CHUNK)
    copies = [
        pltpu.make_async_copy(
            down.at[0, pl.ds(start, size), :], weight.at[pl.ds(start, size), :], arrived.at[place]
        )
        for place, (start, size) in enumerate(spans)
    ]
    for copy in copies:
        copy.start()
    x = rows[...]
    for copy, (start, size) in zip(copies, spans):
        copy.wait()
        out[:, start : start + size] = dot(x, weight[start : start + size, :], COLS).astype(jnp.bfloat16)


def hidden_grad(rows, down_weight):
    count, width = rows.shape
    hidden = down_weight.shape[1]
    return call(
        hidden_grad_body,
        shape((count, hidden)),
        scratch=[
            pltpu.VMEM((hidden, width), jnp.bfloat16),
            pltpu.SemaphoreType.DMA((len(chunks_of(hidden, FF_CHUNK)),)),
        ],
        in_specs=[VMEM, HBM],
        out_specs=VMEM,
        name="hidden_grad",
    )(rows, down_weight)


EXPERT_CHUNK = 256
EXPERT_FIRST = 3
EXPERT_SINGLE = 4
EXPERT_BLOCKS = 10
EXPERT_TILE = 256


def expert_body(width, rows, back, gate_weight, up_weight, hidden, gate_low, up_low, out, gate, up, grads, kept, acts, total, arrived, left):
    spans = chunks_of(gate.shape[1], EXPERT_CHUNK)
    copies = []
    for place, (start, size) in enumerate(spans):
        span = pl.ds(start, size)
        for side, (source, target) in enumerate(
            ((gate_weight.at[0], gate), (up_weight.at[0], up), (back, grads))
        ):
            copies.append(
                pltpu.make_async_copy(source.at[:, span], target.at[:, span], arrived.at[3 * place + side])
            )
    count = len(spans)
    start_all(copies[: 3 * EXPERT_FIRST])
    block = rows.shape[0] // EXPERT_BLOCKS
    choices = [jnp.zeros((block, 1), jnp.float32) for _ in range(EXPERT_BLOCKS)]
    backs = []

    def forward(turn, side, start, size):
        def step():
            weight = (gate, up)[side]
            at = spans[turn][0] + start
            acts[turn % 2, side, :, start : start + size] = dot(rows[:, :width], weight[:, at : at + size])

        return step

    def activate(place, part):
        def step():
            start, size = spans[place]
            span = slice(start, start + size)
            line = slice(part * block, (part + 1) * block)
            act, slope = gelu_parts(acts[place % 2, 0, line, :size])
            up_act = acts[place % 2, 1, line, :size]
            grad = grads[line, span].astype(jnp.float32)
            up_grad = grad * act
            kept[0, line, span] = (act * up_act).astype(jnp.bfloat16)
            kept[1, line, span] = (grad * up_act * slope).astype(jnp.bfloat16)
            kept[2, line, span] = up_grad.astype(jnp.bfloat16)
            choices[part] = choices[part] + jnp.sum(up_grad * up_act, axis=1, keepdims=True)

        return step

    def backward(place, start, size):
        def step():
            first, length = spans[place]
            span = slice(first, first + length)
            columns = slice(start, start + size)
            part = dot(kept[1, :, span], gate[columns, span], COLS) + dot(kept[2, :, span], up[columns, span], COLS)
            if place == 0:
                total[:, columns] = part
            else:
                total[:, columns] += part

        return step

    for turn in range(count + 2):
        products, elementwise = [], []
        if turn < count:
            if turn < EXPERT_SINGLE:
                wait_all(copies[3 * turn : 3 * turn + 3])
            elif turn == EXPERT_SINGLE:
                wait_all(copies[3 * turn :])
            if turn == 0:
                start_all(copies[3 * EXPERT_FIRST :])
            products += [
                forward(turn, side, *piece) for side in range(2) for piece in chunks_of(spans[turn][1], EXPERT_TILE)
            ]
        if 0 < turn <= count:
            elementwise = [activate(turn - 1, part) for part in range(EXPERT_BLOCKS)]
        if turn > 1:
            products += [backward(turn - 2, *piece) for piece in chunks_of(width, EXPERT_TILE)]
        done = 0
        for place, product in enumerate(products):
            product()
            target = len(elementwise) * (place + 1) // len(products)
            for step in elementwise[done:target]:
                step()
            done = target
        for step in elementwise[done:]:
            step()
        if turn > 1:
            place = turn - 2
            start, size = spans[place]
            for which, target in enumerate((hidden, gate_low, up_low)):
                backs.append(
                    pltpu.make_async_copy(
                        kept.at[which, :, pl.ds(start, size)],
                        target.at[:, pl.ds(start, size)],
                        left.at[3 * place + which],
                    )
                )
                backs[-1].start()
    choice = jnp.concatenate(choices, axis=0)
    out[:, :width] = total[...].astype(jnp.bfloat16)
    out[:, width:] = lane_parts(choice)
    for copy in backs:
        copy.wait()


def expert(rows, back, gate_weight, up_weight):
    count = rows.shape[0]
    width, hidden = gate_weight.shape[1:]
    act = shape((count, hidden))
    chunks = len(chunks_of(hidden, EXPERT_CHUNK))
    return call(
        lambda *refs: expert_body(width, *refs),
        [act, act, act, shape(rows.shape)],
        scratch=[
            pltpu.VMEM((width, hidden), jnp.bfloat16),
            pltpu.VMEM((width, hidden), jnp.bfloat16),
            pltpu.VMEM((count, hidden), jnp.bfloat16),
            pltpu.VMEM((3, count, hidden), jnp.bfloat16),
            pltpu.VMEM((2, 2, count, EXPERT_CHUNK), jnp.float32),
            pltpu.VMEM((count, width), jnp.float32),
            pltpu.SemaphoreType.DMA((3 * chunks,)),
            pltpu.SemaphoreType.DMA((3 * chunks,)),
        ],
        in_specs=[VMEM] + [HBM] * 3,
        out_specs=[HBM, HBM, HBM, VMEM],
        name="expert",
    )(rows, back, gate_weight, up_weight)


def expert_out_body(hidden, down, out, acts, weight, total, arrived):
    spans = chunks_of(weight.shape[0], FF_CHUNK)
    copies = []
    for place, (start, size) in enumerate(spans):
        span = pl.ds(start, size)
        copies.append(pltpu.make_async_copy(hidden.at[:, span], acts.at[:, span], arrived.at[2 * place]))
        copies.append(pltpu.make_async_copy(down.at[0, span, :], weight.at[span, :], arrived.at[2 * place + 1]))
    start_all(copies)
    for place, (start, size) in enumerate(spans):
        wait_all(copies[2 * place : 2 * place + 2])
        part = dot(acts[:, start : start + size], weight[start : start + size, :])
        if place == 0:
            total[...] = part
        elif place < len(spans) - 1:
            total[...] += part
        else:
            out[...] = (total[...] + part).astype(jnp.bfloat16)


def expert_out(hidden, down_weight):
    count = hidden.shape[0]
    inner, width = down_weight.shape[1:]
    return call(
        expert_out_body,
        shape((count, width)),
        scratch=[
            pltpu.VMEM((count, inner), jnp.bfloat16),
            pltpu.VMEM((inner, width), jnp.bfloat16),
            pltpu.VMEM((count, width), jnp.float32),
            pltpu.SemaphoreType.DMA((2 * len(chunks_of(inner, FF_CHUNK)),)),
        ],
        in_specs=[HBM] * 2,
        out_specs=VMEM,
        name="expert_out",
    )(hidden, down_weight)


def expert_grads_body(count, width, *refs):
    sources, lefts, sent = refs[:count], refs[count : 2 * count], refs[2 * count]
    targets = refs[2 * count + 1 : 3 * count + 1]
    acts, turned, scaled, staged, arrived, left = refs[3 * count + 1 :]
    spans = chunks_of(sources[0].shape[1], FF_CHUNK)
    steps = [(which, start, size) for which in range(count) for start, size in spans]
    coming = start_all(
        [
            pltpu.make_async_copy(
                sources[which].at[:, pl.ds(start, size)], acts.at[which, :, pl.ds(start, size)], arrived.at[turn]
            )
            for turn, (which, start, size) in enumerate(steps)
        ]
    )
    gate = sum_parts(sent[:, width:])
    for which in range(count):
        scaled[which] = (lefts[which][:, :width].astype(jnp.float32) * gate).astype(jnp.bfloat16)
    backs = []
    for turn in range(len(steps) + 1):
        if turn < len(steps):
            which, start, size = steps[turn]
            coming[turn].wait()
            turned[turn % 2, :size, :] = acts[which, :, start : start + size].T
        if turn > 0:
            which, start, size = steps[turn - 1]
            slot = (turn - 1) % staged.shape[0]
            if turn - 1 >= staged.shape[0]:
                backs[turn - 1 - staged.shape[0]].wait()
            staged[slot, :size, :] = dot(turned[(turn - 1) % 2, :size, :], scaled[which]).astype(jnp.bfloat16)
            backs.append(
                pltpu.make_async_copy(
                    staged.at[slot, pl.ds(0, size), :], targets[which].at[pl.ds(start, size), :], left.at[turn - 1]
                )
            )
            backs[-1].start()
    wait_all(backs[-staged.shape[0] :])


def expert_grads(pairs, sent, width):
    count = len(pairs)
    slots, inner = pairs[0][0].shape
    chunks = len(chunks_of(inner, FF_CHUNK))
    return call(
        lambda *refs: expert_grads_body(count, width, *refs),
        [shape((inner, width))] * count,
        scratch=[
            pltpu.VMEM((count, slots, inner), jnp.bfloat16),
            pltpu.VMEM((2, FF_CHUNK, slots), jnp.bfloat16),
            pltpu.VMEM((count, slots, width), jnp.bfloat16),
            pltpu.VMEM((4, FF_CHUNK, width), jnp.bfloat16),
            pltpu.SemaphoreType.DMA((count * chunks,)),
            pltpu.SemaphoreType.DMA((count * chunks,)),
        ],
        in_specs=[HBM] * count + [VMEM] * (count + 1),
        out_specs=[HBM] * count,
        name="expert_grads",
    )(*[acts for acts, rows in pairs], *[rows for acts, rows in pairs], sent)


def combine_body(returned, columns, gates, middle, block_out):
    length = middle.shape[0]
    slot = iota((length, returned.shape[0]), 1)
    rows = returned[...]
    rows1 = dot(ones_where(slot == columns[:, 0:1]), rows)
    rows2 = dot(ones_where(slot == columns[:, 1:2]), rows)
    block_out[...] = (middle[...] + gates[:, 0:1] * rows1 + gates[:, 1:2] * rows2).astype(jnp.bfloat16)


def combine(returned, columns, gates, middle):
    length, width = middle.shape
    return call(
        combine_body,
        shape((length, width)),
        in_specs=[VMEM] * 4,
        out_specs=VMEM,
        name="combine",
    )(returned, columns, gates, middle)


def router_back(logit, choice, gate1, gate2, picked):
    experts = logit.shape[1]
    top = jnp.max(logit, axis=1, keepdims=True)
    grown = jnp.exp(logit - top)
    total = jnp.sum(grown, axis=1, keepdims=True)
    probs = grown / total
    lse = top + jnp.log(total)
    expert = iota(logit.shape, 1)
    hot1 = ones_where(expert == picked[:, 0:1], jnp.float32)
    hot = hot1 - ones_where(expert == picked[:, 1:2], jnp.float32)
    balance = (BALANCE_COEF * experts) * jnp.mean(hot1, axis=0, keepdims=True)
    even = jnp.sum(probs * balance, axis=1, keepdims=True)
    return hot * (choice * gate1 * gate2) + probs * (balance - even + 2.0 * Z_COEF * lse)


def diagonals(x):
    half = x.shape[0] // 2
    top, low = x[:half], x[half:]
    x = jnp.concatenate([low[:, :half], low[:, half:] + top[:, :half], top[:, half:], jnp.zeros_like(low[:, :half])], axis=1)
    while x.shape[0] > 1:
        half = x.shape[0] // 2
        x = pltpu.roll(x[:half], half, 1) + x[half:]
    return x


def attend_back_body(
    heads, sent_grad, columns, gates, middle, feedforward_gain, cotangent, table_t, line_hot,
    logits, router_t, query, key, value, wo,
    middle_grad, backs, gain_grad, bias_lines, router_grad,
    weight, acts, lines, heads_grad, grad_out, backs_out, arrived, left,
):
    length, width = middle.shape
    size = width // heads
    half = width // 2
    copies = start_all(
        [pltpu.make_async_copy(wo, weight, arrived.at[3])]
        + [
            pltpu.make_async_copy(source, acts.at[place], arrived.at[place])
            for place, source in enumerate((query, key, value))
        ]
    )
    lines[...] = dot(table_t[...], line_hot[1], precision=PRECISE)
    slot = iota((length, sent_grad.shape[0]), 1)
    rows = sent_grad[...]
    rows1 = dot(ones_where(slot == columns[:, 0:1]), rows)
    rows2 = dot(ones_where(slot == columns[:, 1:2]), rows)
    gate1, gate2 = gates[:, 0:1], gates[:, 1:2]
    choice = sum_parts(rows1[:, width:] - rows2[:, width:])
    logit_grad = router_back(logits[...], choice, gate1, gate2, columns[:, 2:4])
    mid = middle[...]
    r = rms(mid)
    scaled = mid * r
    high, rest = split2(scaled * feedforward_gain[...])
    grad_high, grad_rest = split2(logit_grad)
    router_high, router_rest = split2(router_t[...])
    router_grad[...] = dot(grad_high, high, ROWS) + dot(grad_rest, high, ROWS) + dot(grad_high, rest, ROWS)
    normed2_grad = (
        gate1 * rows1[:, :width]
        + gate2 * rows2[:, :width]
        + (dot(grad_high, router_high) + dot(grad_rest, router_high) + dot(grad_high, router_rest))
    )
    u = normed2_grad * feedforward_gain[...]
    gain_grad[...] = jnp.sum(normed2_grad * scaled, axis=0, keepdims=True)
    grad = (
        cotangent[...].astype(jnp.float32)
        + r * u
        - mid * (r * r * r * jnp.mean(u * mid, axis=1, keepdims=True))
    )
    grad_out[...] = grad
    grad_copy = pltpu.make_async_copy(grad_out, middle_grad, left.at[2])
    grad_copy.start()
    low = grad.astype(jnp.bfloat16)
    wait_all(copies)
    heads_grad[...] = dot(low, weight[...], COLS).astype(jnp.bfloat16)
    backs_out[:, 3 * width :] = low
    pair_width = 2 * size
    first = iota((length, pair_width), 1) < size
    first_t = iota((pair_width, length), 0) < size
    zero = jnp.zeros((length, pair_width), jnp.bfloat16)
    scale = jnp.bfloat16(1.0 / math.sqrt(size))
    for pair in range(heads // 2):
        start = pair * pair_width
        span = slice(start, start + pair_width)
        q, k, v, g = acts[0, :, span] * scale, acts[1, :, span], acts[2, :, span], heads_grad[:, span]
        k_turned = (k * scale).T
        kept = []
        for side in range(2):
            q_side = jnp.where(first, q, zero) if side == 0 else jnp.where(first, zero, q)
            g_side = jnp.where(first, g, zero) if side == 0 else jnp.where(first, zero, g)
            head = 2 * pair + side
            line = jnp.broadcast_to(lines[head : head + 1, :], (length, 2 * length))
            bias = pltpu.roll(line, length + 1, 1, stride=1, stride_axis=0)[:, :length]
            scores = dot(k, q_side, COLS) + bias
            top = jnp.max(scores, axis=0, keepdims=True)
            grown = jnp.exp(scores - top)
            probs = grown * (1.0 / jnp.sum(grown, axis=0, keepdims=True))
            probs_grad = dot(v, g_side, COLS)
            score_grad = probs * (probs_grad - jnp.sum(probs * probs_grad, axis=0, keepdims=True))
            score_low = score_grad.astype(jnp.bfloat16)
            bias_lines[head : head + 1, :] = diagonals(score_low.astype(jnp.float32))
            kept.append(
                (
                    dot(k_turned, score_low),
                    dot(score_low, q),
                    dot(probs.astype(jnp.bfloat16), g),
                )
            )
        results = (
            jnp.where(first_t, kept[0][0], kept[1][0]).astype(jnp.bfloat16).T,
            jnp.where(first, kept[0][1], kept[1][1]).astype(jnp.bfloat16),
            jnp.where(first, kept[0][2], kept[1][2]).astype(jnp.bfloat16),
        )
        for place, result in enumerate(results):
            backs_out[:, place * width + start : place * width + start + pair_width] = result
    leaving = pltpu.make_async_copy(backs_out, backs, left.at[0])
    leaving.start()
    leaving.wait()
    grad_copy.wait()


def attend_back(heads, line_hot, sent_grad, columns, gates, middle, feedforward_gain, cotangent, table_t, logits, router_t, query, key, value, wo):
    length, width = middle.shape
    return call(
        lambda *refs: attend_back_body(heads, *refs),
        [
            shape((length, width), jnp.float32),
            shape((length, 4 * width)),
            shape((1, width), jnp.float32),
            shape((heads, 2 * length), jnp.float32),
            shape(router_t.shape, jnp.float32),
        ],
        scratch=[
            pltpu.VMEM((width, width), jnp.bfloat16),
            pltpu.VMEM((3, length, width), jnp.bfloat16),
            pltpu.VMEM((heads, 2 * length), jnp.float32),
            pltpu.VMEM((length, width), jnp.bfloat16),
            pltpu.VMEM((length, width), jnp.float32),
            pltpu.VMEM((length, 4 * width), jnp.bfloat16),
            pltpu.SemaphoreType.DMA((4,)),
            pltpu.SemaphoreType.DMA((3,)),
        ],
        in_specs=[VMEM] * 10 + [HBM] * 4,
        out_specs=[HBM] * 2 + [VMEM] * 3,
        name="attend_back",
    )(sent_grad, columns, gates, middle, feedforward_gain, cotangent, table_t, line_hot, logits, router_t, query, key, value, wo)


def input_back_body(backs_in, grad_in, tokens, attention_gain, bias_lines, line_hot, wq, wk, wv, input_grad, vectors, weights, backs, middle_grad, arrived):
    length, width = tokens.shape
    copies = []
    for place, source in enumerate((wq, wk, wv)):
        span = pl.ds(place * width, width)
        copies.append(pltpu.make_async_copy(backs_in.at[:, span], backs.at[:, span], arrived.at[place]))
        copies.append(pltpu.make_async_copy(source, weights.at[place], arrived.at[3 + place]))
    copies.append(pltpu.make_async_copy(grad_in, middle_grad, arrived.at[6]))
    start_all(copies)
    bias = dot(bias_lines[...], line_hot[1], COLS, PRECISE)
    rows = bias.shape[0] // 4
    bias = jnp.concatenate([bias[rows * part : rows * (part + 1)] for part in range(4)], axis=1)
    x = tokens[...].astype(jnp.float32)
    s = rms(x)
    total = jnp.zeros((length, width), jnp.float32)
    for place in range(3):
        wait_all(copies[2 * place : 2 * place + 2])
        total = total + dot(backs[:, place * width : (place + 1) * width], weights[place], COLS)
    w = total * attention_gain[...]
    gain = jnp.sum(total * x * s, axis=0, keepdims=True)
    vectors[...] = jnp.zeros_like(vectors)
    for part in range(width // LANES):
        vectors[part : part + 1, :] = gain[:, part * LANES : (part + 1) * LANES]
    vectors[width // LANES : width // LANES + rows, :] = bias
    copies[6].wait()
    input_grad[...] = middle_grad[...] + s * w - x * (s * s * s * jnp.mean(w * x, axis=1, keepdims=True))


def input_back(line_hot, backs, middle_grad, tokens, attention_gain, bias_lines, wq, wk, wv):
    length, width = tokens.shape
    return call(
        input_back_body,
        [
            shape((length, width), jnp.float32),
            shape((BLOCK, LANES), jnp.float32),
        ],
        scratch=[
            pltpu.VMEM((3, width, width), jnp.bfloat16),
            pltpu.VMEM((length, 3 * width), jnp.bfloat16),
            pltpu.VMEM((length, width), jnp.float32),
            pltpu.SemaphoreType.DMA((7,)),
        ],
        in_specs=[HBM] * 2 + [VMEM] * 4 + [HBM] * 3,
        out_specs=[VMEM] * 2,
        name="input_back",
    )(backs, middle_grad, tokens, attention_gain, bias_lines, line_hot, wq, wk, wv)


EXTRA = 2 * LANES


def resplit(lanes):
    half = LANES // 2
    total = lanes + pltpu.roll(lanes, half, 1)
    high = total.astype(jnp.bfloat16).astype(jnp.float32)
    return jnp.where(iota(lanes.shape, 1) < half, high, total - high)


def rotated(place, side, block, step):
    return pl.ds(pl.multiple_of(((place + step) % side) * block, block), block)


def products_body(side, where, normed, heads_out, left_far, backs_in, far_in, feedforward_gain, router, *rest):
    pieces, (lefts, backs, payload, vectors, arrived, left) = rest[:side], rest[side:]
    length, width = normed.shape
    half = width // 2
    mine = pl.ds(pl.multiple_of(where[0] * half, half), half)
    copies = start_all(
        [
            pltpu.make_async_copy(normed.at[:, mine], lefts.at[0, :, pl.ds(0, half)], arrived.at[0]),
            pltpu.make_async_copy(heads_out.at[:, mine], lefts.at[0, :, pl.ds(half, half)], arrived.at[1]),
            pltpu.make_async_copy(left_far, lefts.at[1], arrived.at[2]),
        ]
        + [
            pltpu.make_async_copy(
                source.at[:, pl.ds(place * width, width)],
                backs.at[which, :, pl.ds(place * width, width)],
                arrived.at[3 + 2 * place + which],
            )
            for place in range(4)
            for which, source in enumerate((backs_in, far_in))
        ]
    )
    experts = router.shape[0]
    vectors[...] = jnp.zeros_like(vectors)
    vectors[0:1, :] = feedforward_gain[...]
    vectors[8 : 8 + experts, :] = router[...]
    for place in range(2):
        start = 4 * width + place * LANES
        payload[:, start : start + LANES] = resplit(vectors[:, place * half : (place + 1) * half].T).astype(jnp.bfloat16)
    position = where[2 + where[0]]
    leaving = []

    def leave(part, start, size):
        for step, piece in enumerate(pieces):
            leaving.append(
                pltpu.make_async_copy(
                    payload.at[rotated(position, side, half // side, step), pl.ds(start, size)],
                    piece.at[:, pl.ds(start, size)],
                    left.at[part * side + step],
                )
            )
            leaving[-1].start()

    leave(4, 4 * width, EXTRA)
    wait_all(copies[:3])
    for place in range(4):
        wait_all(copies[3 + 2 * place : 5 + 2 * place])
        span = slice(place * width, (place + 1) * width)
        start = 0 if place < 3 else half
        payload[:, span] = (
            dot(lefts[0, :, start : start + half], backs[0, :, span], ROWS)
            + dot(lefts[1, :, start : start + half], backs[1, :, span], ROWS)
        ).astype(jnp.bfloat16)
        leave(place, place * width, width)
    wait_all(leaving)


def products(side, normed, heads_out, left_far, backs, backs_far, feedforward_gain, router):
    length, width = normed.shape
    wide = 4 * width + EXTRA
    return call(
        lambda *refs: products_body(side, Place(side), *refs),
        [shape((width // 2 // side, wide))] * side,
        scratch=[
            pltpu.VMEM((2, length, width), jnp.bfloat16),
            pltpu.VMEM((2, length, 4 * width), jnp.bfloat16),
            pltpu.VMEM((width // 2, wide), jnp.bfloat16),
            pltpu.VMEM((LANES, width), jnp.float32),
            pltpu.SemaphoreType.DMA((11,)),
            pltpu.SemaphoreType.DMA((5 * side,)),
        ],
        in_specs=[HBM] * 5 + [VMEM] * 2,
        out_specs=[HBM] * side,
        name="products",
    )(normed, heads_out, left_far, backs, backs_far, feedforward_gain, router)


def total_into(out, refs, late):
    total = refs[0][...].astype(jnp.float32)
    for ref in refs[1:]:
        total = total + ref[...].astype(jnp.float32)
    wide = total.shape[1] - EXTRA - (LANES if late else 0)
    out[:, :wide] = total[:, :wide].astype(jnp.bfloat16)
    for start in range(wide, wide + EXTRA, LANES):
        out[:, start : start + LANES] = resplit(total[:, start : start + LANES]).astype(jnp.bfloat16)
    if late:
        out[:, wide + EXTRA :] = stack_parts(total[:BLOCK, wide + EXTRA :] + total[BLOCK:, wide + EXTRA :])


def stack_parts(block):
    return jnp.concatenate(split2(block), axis=0)


def fold_body(side, where, vectors, *refs):
    pieces, outs, total = refs[:side], refs[side : 2 * side], refs[-1]
    total_into(total, pieces, False)
    position = where[3 - where[0]]
    wide = total.shape[1]
    late = stack_parts(vectors[...])
    for step, out in enumerate(outs):
        out[:, :wide] = total[rotated(position, side, out.shape[0], step), :]
        out[:, wide:] = late


def fold(side, vectors, pieces):
    rows, wide = pieces[0].shape
    return call(
        lambda *refs: fold_body(side, Place(side), *refs),
        [shape((rows // side, wide + LANES))] * side,
        scratch=[pltpu.VMEM((rows, wide), jnp.bfloat16)],
        in_specs=[VMEM] * (side + 1),
        out_specs=[VMEM] * side,
        vmem=16,
        name="fold",
    )(vectors, *pieces)


def add_pieces(pieces):
    return call(
        lambda *refs: total_into(refs[-1], refs[:-1], True),
        shape(pieces[0].shape),
        in_specs=[VMEM] * len(pieces),
        out_specs=VMEM,
        vmem=12,
        name="add_pieces",
    )(*pieces)


def put_body(side, where, *refs):
    pieces, (whole, upper, lower) = refs[:side], refs[side:]
    position = where[3 - where[0]]
    rows = upper.shape[0]
    for step in range(side):
        whole[rotated(position, side, pieces[0].shape[0], step), :] = pieces[step][...]
    upper[...] = whole[:rows, :]
    lower[...] = whole[rows:, :]


def put(side, pieces):
    rows, wide = pieces[0].shape
    half = shape((side * rows // 2, wide))
    return call(
        lambda *refs: put_body(side, Place(side), *refs),
        [shape((side * rows, wide)), half, half],
        in_specs=[VMEM] * side,
        out_specs=[VMEM] * 3,
        vmem=24,
        name="put",
    )(*pieces)


def again_body(whole, upper, lower):
    rows = upper.shape[0]
    upper[...] = whole[:rows, :]
    lower[...] = whole[rows:, :]


def again(whole):
    half = shape((whole.shape[0] // 2, whole.shape[1]))
    return call(again_body, [half, half], in_specs=[VMEM], out_specs=[VMEM] * 2, vmem=24, name="again")(whole)


def begin_body(side, where, near, far, *refs):
    outs, (held, staged, arrived, left) = refs[:4], refs[4:]
    rows, width = staged.shape[2:]
    copies = start_all(
        [
            pltpu.make_async_copy(source.at[:, pl.ds(0, 4 * width)], held.at[which], arrived.at[which])
            for which, source in enumerate((near, far))
        ]
    )
    backs = []
    for which in range(2):
        core = where[0] if which == 0 else 1 - where[0]
        copies[which].wait()
        line = pl.ds(pl.multiple_of(core * (width // 2) + where[2 + core] * rows, rows), rows)
        for matrix in range(4):
            staged[which, matrix] = held[which, :, matrix * width : (matrix + 1) * width].astype(jnp.float32)
            backs.append(
                pltpu.make_async_copy(staged.at[which, matrix], outs[matrix].at[line, :], left.at[4 * which + matrix])
            )
            backs[-1].start()
    wait_all(backs)


def begin(side, near, far):
    rows, wide = near.shape
    width = (wide - EXTRA - LANES) // 4
    return call(
        lambda *refs: begin_body(side, Place(side), *refs),
        [shape((width, width), jnp.float32)] * 4,
        scratch=[
            pltpu.VMEM((2, rows, 4 * width), jnp.bfloat16),
            pltpu.VMEM((2, 4, rows, width), jnp.float32),
            pltpu.SemaphoreType.DMA((2,)),
            pltpu.SemaphoreType.DMA((8,)),
        ],
        in_specs=[HBM] * 2,
        out_specs=[HBM] * 4,
        name="begin",
    )(near, far)


def finish_body(side, steps, where, *refs):
    parts = sum(len(order) for step, order in steps)
    pieces, refs = (refs[:parts], refs[parts : 2 * parts]), refs[2 * parts :]
    up_low, outs, refs = refs[0], refs[5:9], refs[9:]
    up_out, gain, feedforward_gain, router_t, bias_t, held, staged, up_held, up_staged, late, arrived, left = refs
    rows = staged.shape[2]
    width = staged.shape[3]
    half = width // 2
    wide = held.shape[3]
    copies = []
    for which in range(2):
        place = 0
        for block, (step, order) in enumerate(steps):
            size = rows // len(order)
            columns = pl.ds(0 if step else 4 * width, wide if step else wide - 4 * width)
            copies.append(
                start_all(
                    [
                        pltpu.make_async_copy(
                            pieces[which][place + part].at[:, columns],
                            held.at[which, block, pl.ds(order[part] * size, size), columns],
                            arrived.at[which * parts + place + part],
                        )
                        for part in range(len(order))
                    ]
                )
            )
            place += len(order)
    up_copy = pltpu.make_async_copy(up_low, up_held, arrived.at[2 * parts])
    up_copy.start()
    for vector in (feedforward_gain, router_t, late):
        vector[...] = jnp.zeros_like(vector)
    backs = []
    for block, (step, order) in enumerate(steps):
        for which in range(2):
            core = where[0] if which == 0 else 1 - where[0]
            slot = which * len(steps) + block
            wait_all(copies[slot])
            start = pl.multiple_of(((where[2 + core] + step) % side) * rows, rows)
            line = pl.ds(pl.multiple_of(core * half + start, rows), rows)
            for matrix in range(4 if step else 0):
                staged[slot, matrix] = held[which, block, :, matrix * width : (matrix + 1) * width].astype(jnp.float32)
                backs.append(
                    pltpu.make_async_copy(
                        staged.at[slot, matrix], outs[matrix].at[line, :], left.at[4 * slot + matrix]
                    )
                )
                backs[-1].start()
            for place in range(2):
                lanes = held[which, block, :, 4 * width + place * LANES : 4 * width + (place + 1) * LANES]
                lanes = lanes.astype(jnp.float32)
                turned = (lanes + pltpu.roll(lanes, LANES // 2, 1)).T
                line = pl.ds(pl.multiple_of(place * half + start, rows), rows)
                feedforward_gain[:, line] += turned[0:1]
                router_t[:, line] += turned[8 : 8 + router_t.shape[0]]
            block_rows = held[which, block, : 2 * BLOCK, 4 * width + EXTRA :].astype(jnp.float32)
            late[...] += block_rows[:BLOCK] + block_rows[BLOCK:]
    up_copy.wait()
    up_staged[...] = up_held[...].astype(jnp.float32)
    backs.append(pltpu.make_async_copy(up_staged, up_out, left.at[8 * len(steps)]))
    backs[-1].start()
    lines = width // LANES
    for part in range(lines):
        gain[:, part * LANES : (part + 1) * LANES] = late[part : part + 1, :]
    heads, buckets = bias_t.shape
    for part in range(4):
        bias_t[part * heads // 4 : (part + 1) * heads // 4, :] = late[
            lines : lines + heads // 4, part * buckets : (part + 1) * buckets
        ]
    wait_all(backs)


def finish(side, steps, near, far, up_low, begun, experts, buckets, heads):
    wide = near[0].shape[1]
    width = (wide - EXTRA - LANES) // 4
    rows = width // 2 // side
    count, parts = len(steps), len(near)
    return call(
        lambda *refs: finish_body(side, steps, Place(side), *refs),
        [shape((width, width), jnp.float32)] * 4
        + [
            shape(up_low.shape, jnp.float32),
            shape((1, width), jnp.float32),
            shape((1, width), jnp.float32),
            shape((experts, width), jnp.float32),
            shape((heads, buckets), jnp.float32),
        ],
        scratch=[
            pltpu.VMEM((2, count, rows, wide), jnp.bfloat16),
            pltpu.VMEM((2 * count, 4, rows, width), jnp.float32),
            pltpu.VMEM(up_low.shape, jnp.bfloat16),
            pltpu.VMEM(up_low.shape, jnp.float32),
            pltpu.VMEM((BLOCK, LANES), jnp.float32),
            pltpu.SemaphoreType.DMA((2 * parts + 1,)),
            pltpu.SemaphoreType.DMA((8 * count + 1,)),
        ],
        in_specs=[HBM] * (2 * parts + 5),
        out_specs=[HBM] * 5 + [VMEM] * 4,
        input_output_aliases={2 * parts + 1 + matrix: matrix for matrix in range(4)},
        name="finish",
    )(*near, *far, up_low, *begun)


def rotate_x(count, step):
    return [(x * 2 + c, ((x + step) % count) * 2 + c) for x in range(count) for c in range(2)]


def rotate_plane(chips, side, flip, step):
    pairs = []
    for x in range(chips):
        for core in range(2):
            for z in range(side):
                for y in range(side):
                    along_z = core ^ flip
                    to = ((z + step) % side, y) if along_z else (z, (y + step) % side)
                    base = (x * 2 + core) * side * side
                    pairs.append((base + z * side + y, base + to[0] * side + to[1]))
    return pairs


def swap_cores(count):
    return [(x * 2 + c, x * 2 + 1 - c) for x in range(count) for c in range(2)]


def shards(
    tokens,
    routes,
    cotangent,
    attention_gain,
    query_weight,
    key_weight,
    value_weight,
    output_weight,
    bias_table,
    feedforward_gain,
    router_weight,
    gate_weight,
    up_weight,
    down_weight,
):
    length, width = tokens.shape
    buckets, heads = bias_table.shape
    experts = lax.axis_size("expert")
    chips = lax.axis_size("dp") // 2
    side = math.isqrt(experts)
    capacity = max(2, (10 * length + 4 * experts - 1) // (4 * experts))
    swap = swap_cores(chips)
    line_hot = jnp.asarray(bucket_lines(length, buckets))
    gain1, gain2 = attention_gain[None], feedforward_gain[None]

    def exchange(rows):
        return lax.all_to_all(
            rows.reshape(experts, capacity, -1), "expert", split_axis=0, concat_axis=0, tiled=True
        ).reshape(experts * capacity, -1)

    table_t, router_t = bias_table.T, router_weight.T
    slots_t, columns, cot_slots = route(routes, cotangent, experts, capacity)
    cot_rows = exchange(cot_slots)
    normed, query, key, value, heads_out, left, middle, logits, gates, sent = attend(
        heads, experts * capacity, side, line_hot, tokens, gain1, gain2, table_t, router_t, columns, slots_t,
        (query_weight, key_weight, value_weight, output_weight),
    )

    def swapped(array):
        return lax.ppermute(array, "dp", swap)

    rows = exchange(sent)
    left_far = swapped(left)
    back = hidden_grad(cot_rows, down_weight)
    rows, left_far = lax.optimization_barrier((rows, left_far))
    hidden, gate_low, up_acts, rows_grad = expert(rows, back, gate_weight, up_weight)
    sent_grad = exchange(rows_grad)

    def scatter_dp(part):
        return lax.psum_scatter(part, "dp", scatter_dimension=0, tiled=True)

    grads = expert_grads(((hidden, cot_rows), (gate_low, rows)), rows, width)
    sent_grad, grads = lax.optimization_barrier((sent_grad, grads))
    down_grad, gate_grad = scatter_dp(grads[0]), scatter_dp(grads[1])

    middle_grad, backs, gain2_part, bias_lines, router_part = attend_back(
        heads, line_hot, sent_grad, columns, gates, middle, gain2, cotangent, table_t, logits,
        router_t, query, key, value, output_weight,
    )
    backs_far = swapped(backs)
    pieces = products(side, normed, heads_out, left_far, backs, backs_far, gain2_part, router_part)

    def turn(piece, flip, step):
        return lax.ppermute(piece, ("dp", "expert"), rotate_plane(chips, side, flip, step))

    def scatter_plane(pieces, flip):
        return [pieces[0]] + [turn(pieces[step], flip, step) for step in range(1, side)]

    pieces, hidden, backs = lax.optimization_barrier((pieces, hidden, backs))
    folded_in = scatter_plane(pieces, 0)
    input_grad, vectors = input_back(
        line_hot, backs, middle_grad, tokens, gain1, bias_lines, query_weight, key_weight, value_weight
    )
    returned = expert_out(hidden, down_weight)
    down_grad = down_grad.astype(jnp.float32)
    folded_in, vectors, returned, down_grad = lax.optimization_barrier((folded_in, vectors, returned, down_grad))
    shard = add_pieces(scatter_plane(fold(side, vectors, folded_in), 1))
    shard, returned, up_acts = lax.optimization_barrier((shard, returned, up_acts))
    returned = exchange(returned)
    (up_part,) = expert_grads(((up_acts, rows),), rows, width)
    total = add_pieces([shard] + [lax.ppermute(shard, "dp", rotate_x(chips, step)) for step in range(1, chips)])
    total, up_part, returned = lax.optimization_barrier((total, up_part, returned))
    up_low = scatter_dp(up_part)
    gathered = [total] + [turn(total, 1, -step) for step in range(1, side)]
    gate_grad = gate_grad.astype(jnp.float32)
    block_out = combine(returned, columns, gates, middle)
    gathered, gate_grad, block_out = lax.optimization_barrier((gathered, gate_grad, block_out))
    own, upper, lower = put(side, gathered)
    minus_upper, plus_lower = turn(upper, 0, 1), turn(lower, 0, -1)
    upper2, lower2 = again(own)
    minus_lower, plus_upper = turn(lower2, 0, 1), turn(upper2, 0, -1)
    own_far = swapped(own)
    plus_upper, begun = lax.optimization_barrier((plus_upper, begin(side, own, own_far)))
    across = [turn(minus_upper, 0, 1), turn(plus_lower, 0, -1)]
    near = [plus_lower, plus_upper, minus_lower, minus_upper, *across]
    far = [own_far, *[swapped(piece) for piece in near]]
    near = [own, *near]
    query_grad, key_grad, value_grad, output_grad, up_grad, gain1_grad, gain2_grad, router_grad_t, bias_grad_t = finish(
        side, ((0, (0,)), (1, (1, 0)), (3, (1, 0)), (2, (0, 1))), near, far, up_low, begun, experts, buckets, heads
    )
    return (
        block_out,
        input_grad,
        gain1_grad[0],
        query_grad,
        key_grad,
        value_grad,
        output_grad,
        bias_grad_t.T,
        gain2_grad[0],
        router_grad_t.T,
        gate_grad.T[None],
        up_grad.T[None],
        down_grad[None],
    )


def solution(mesh):
    return jax.shard_map(
        shards,
        mesh=mesh,
        in_specs=(
            P(("dp", "expert"), None),
            P(("dp", "expert"), None),
            P(("dp", "expert"), None),
            P(),
            P(),
            P(),
            P(),
            P(),
            P(),
            P(),
            P(),
            P("expert", None, None),
            P("expert", None, None),
            P("expert", None, None),
        ),
        out_specs=(
            P(("dp", "expert"), None),
            P(("dp", "expert"), None),
            P(),
            P(),
            P(),
            P(),
            P(),
            P(),
            P(),
            P(),
            P("expert", None, "dp"),
            P("expert", None, "dp"),
            P("expert", "dp", None),
        ),
        check_vma=False,
    )
```
